32 devices in a mesh: dp: 8 (over z, y), expert: 4 (over x, core).
Axes of the slice: x: 2, y: 2, z: 4, core: 2. Of those that a mesh axis runs over, the one named last changes fastest.
Arguments:
- tokens: bfloat16 [4096, 2048], P(('dp', 'expert')), may hold values from -6 to 6
- cotangent: bfloat16 [4096, 2048], P(('dp', 'expert')), may hold values from -6 to 6
- expert_ids: int32 [4096, 2], P(('dp', 'expert')), may hold values from 0 to 3, all different within a row; in each aligned block of 128 rows (0 to 127, 128 to 255, ...) at most 80 rows name the same one
- gate_probs: float32 [4096, 2], P(('dp', 'expert')), may hold values from 0.2 to 1
- gate_up_weight: bfloat16 [4, 2048, 1024], P('expert'), may hold values from -0.125 to 0.125
- down_weight: bfloat16 [4, 512, 2048], P('expert'), may hold values from -0.25 to 0.25
- down_residual: bfloat16 [8, 4, 512, 2048], P('dp', 'expert'), may hold values from -12 to 12
Outputs:
- token_grad: bfloat16 [4096, 2048], P(('dp', 'expert'))
- grad_gate_up: float32 [4, 2048, 1024], P('expert', 'dp')
- grad_down: float32 [4, 512, 2048], P('expert', 'dp')
The draws below stay inside these ranges and needn't reach their ends.
Inputs may be any that keep to these rules, and one draw needn't show every extreme that they name: `expert_ids`: each token names 2 different experts. Among the tokens of one device no expert is named by more than 80 tokens, and in some device's tokens one expert is named by exactly 80.
All inputs are finite; a program needn't handle non-finite values.
Results may differ from the reference program's by a relative error of at most 0.0065.
Values may be sent and summed in bfloat16 or wider, within the bound.
No kernel may reach another device: no remote copies, remote signals or barrier semaphores. Data moves between devices by JAX's collectives and lax.ppermute only.
A program may use at most 128 MiB of HBM per device.

```python
import math
import jax
import jax.numpy as jnp
import numpy as np
from jax import lax

D = 2048
TOP = 2
H_DEV = 512
TOK_DEV = 128
EXPERTS = 4
DP_GROUPS = 8
CAP = 80
TOKENS = 4096


def strengthened(values, key, source, target, blocks, factor):
    owner, partner = [(jnp.arange(values.shape[position]) // (values.shape[position] // blocks)).reshape([-1 if axis == position else 1 for axis in range(values.ndim)]) for position in (source, target)]
    chosen = jax.random.permutation(key, blocks)[partner]
    strong = (owner == chosen) | (owner == (partner + blocks // 2) % blocks)
    return jnp.where(strong, factor * values, values)


def level_of(key, dims, split, low, top_value):
    factor_of, own = 1.0, jax.random.fold_in(key, 6)
    for axis_at, shards_of in split:
        draws = jnp.exp(jax.random.uniform(jax.random.fold_in(own, axis_at), (shards_of,), jnp.float32, low / len(split), top_value / len(split)))
        factor_of = factor_of * jnp.repeat(draws, dims[axis_at] // shards_of).reshape([-1 if axis == axis_at else 1 for axis in range(len(dims))])
    return factor_of


def deal_out(key, own, number, rows, count, top, reach, slope):
    ranking = jax.random.permutation(key, count)
    packed, usual = shares(count, rows * top, reach, slope, True), shares(count, rows * top, reach, slope, False)
    places = jnp.arange(count)

    def named(lengths, rotation):
        used = int((lengths > 0).sum())
        fixed = max(1, used // 4)
        moved = fixed + (places - fixed + rotation * (used - fixed)) % max(1, count - fixed)
        return jnp.zeros((count,), jnp.int32).at[ranking[jnp.where(places < fixed, places, moved)]].set(jnp.asarray(lengths, jnp.int32))

    lengths = jnp.where(number % 4 == 0, named(packed, number // 4), named(usual, number - number // 4 - 1))
    mixed = jax.random.permutation(jax.random.fold_in(own, 3), count)
    giver, receiver = mixed[0:count // 2 * 2:2], mixed[1:count // 2 * 2:2]
    margin = jnp.minimum(lengths[giver] - 1, reach - lengths[receiver]) // 2
    margin = jnp.where((giver == ranking[0]) | (receiver == ranking[0]) | (lengths[receiver] == 0), 0, jnp.maximum(margin, 0))
    moved = jax.random.randint(jax.random.fold_in(own, 4), (count // 2,), 0, 1 << 20) % (margin + 1)
    lengths = lengths.at[giver].add(-moved).at[receiver].add(moved)
    members = jnp.searchsorted(jnp.cumsum(lengths), jnp.arange(rows * top), side="right").astype(jnp.int32)
    table = members.reshape(top, rows).T
    table = table[jax.random.permutation(jax.random.fold_in(own, 1), rows)]
    rotation = jax.random.randint(jax.random.fold_in(own, 2), (rows, 1), 0, top)
    return jnp.take_along_axis(table, (jnp.arange(top)[None, :] + rotation) % top, axis=1)


def shares(number_of, total, limit, skew, full):
    weights = [(1 << 20) // math.isqrt(rank ** skew) + 1 for rank in range(1, number_of + 1)]
    largest = limit if full else min(limit, max(-(-total // number_of), total * weights[0] // sum(weights)))
    least = 1 if total - largest >= number_of - 1 else 0
    counts, rest = [largest] + [least] * (number_of - 1), total - largest - least * (number_of - 1)
    while rest > 0:
        free = [i for i in range(1, number_of) if counts[i] < largest] or [i for i in range(1, number_of) if counts[i] < limit]
        whole, remaining = sum([weights[i] for i in free]), rest
        for i in free:
            extra = min(limit - counts[i], max(1, remaining * weights[i] // whole), rest)
            counts[i] = counts[i] + extra
            rest = rest - extra
    return np.array(counts)


def noise(rng, extent, deviation, bound, cuts=(), held_as=jnp.bfloat16):
    loudness = level_of(rng, extent, cuts, -0.22, 0.18) if cuts else 1.0
    drawn = jax.random.normal(rng, extent, jnp.float32) * deviation * loudness
    return jnp.minimum(jnp.maximum(drawn, -bound), bound).astype(held_as)


def noise_with(own_key, extent, scale, limit, cuts, heavy, dtype=jnp.bfloat16):
    array = scale * jax.random.normal(own_key, extent, jnp.float32)
    if cuts:
        array = array * level_of(own_key, extent, cuts, -0.22, 0.18)
    return jnp.clip(strengthened(array, jax.random.fold_in(own_key, 3), *heavy), -limit, limit).astype(dtype)


def setup_inputs(seed: int = 0) -> dict:
    streams_of = jax.random.split(jax.random.key(seed), 8)
    tokens = noise(streams_of[0], (TOKENS, D), 1.0, 6.0, ((0, 32),))
    cotangent = noise(streams_of[1], (TOKENS, D), 1.0, 6.0, ((0, 32),))
    expert_ids_keys = jax.random.split(jax.random.fold_in(streams_of[2], 1), TOKENS // TOK_DEV)
    expert_ids_turns = jax.random.permutation(jax.random.fold_in(streams_of[2], 3), TOKENS // TOK_DEV)
    expert_ids = jax.vmap(lambda own, number: deal_out(jax.random.fold_in(streams_of[2], 2), own, number, TOK_DEV, EXPERTS, TOP, CAP, 1))(expert_ids_keys, expert_ids_turns).reshape((TOKENS, TOP))
    gate_probs = jnp.clip(0.2 + 0.8 * jax.random.uniform(streams_of[3], (TOKENS, TOP), jnp.float32) ** level_of(streams_of[3], (TOKENS, TOP), ((0, 32),), -0.2, 0.2), 0.2, 1.0)
    gate_up_weight = noise(streams_of[4], (EXPERTS, D, 2 * H_DEV), D ** -0.5, 0.125, ((0, 4),))
    down_weight = noise(streams_of[5], (EXPERTS, H_DEV, D), H_DEV ** -0.5, 0.25, ((0, 4),))
    down_residual = noise_with(streams_of[6], (DP_GROUPS, EXPERTS, H_DEV, D), 2.0, 12.0, ((0, 8), (1, 4)), (0, 2, 8, 2.0))
    return {"tokens": tokens, "cotangent": cotangent, "expert_ids": expert_ids, "gate_probs": gate_probs, "gate_up_weight": gate_up_weight, "down_weight": down_weight, "down_residual": down_residual}


def expert_forward(token_rows, gate_up):
    hidden_units = gate_up.shape[1] // 2
    projected = jnp.dot(token_rows, gate_up, preferred_element_type=jnp.float32)
    gate_part = projected[:, :hidden_units]
    up_part = projected[:, hidden_units:]
    gate_sig = jax.nn.sigmoid(gate_part)
    activated = gate_part * gate_sig
    hidden = (activated * up_part).astype(jnp.bfloat16)
    return gate_part, up_part, gate_sig, activated, hidden


def expert_backward(token_rows, scaled, forward, gate_up, down_matrix):
    gate_part, up_part, gate_sig, activated, hidden = forward
    back_hidden = jnp.dot(scaled, down_matrix.T, preferred_element_type=jnp.float32)
    back_gate = back_hidden * up_part * gate_sig * (1.0 + gate_part * (1.0 - gate_sig))
    back_up = back_hidden * activated
    back_both = jnp.concatenate([back_gate, back_up], axis=1).astype(jnp.bfloat16)
    token_part = jnp.dot(back_both, gate_up.T, preferred_element_type=jnp.float32).astype(jnp.bfloat16)
    contract = (((0,), (0,)), ((), ()))
    gate_up_term = lax.dot_general(token_rows, back_both, contract, preferred_element_type=jnp.float32)
    down_term = lax.dot_general(hidden, scaled, contract, preferred_element_type=jnp.float32)
    return token_part, gate_up_term, down_term


def round_trip(values):
    return lax.optimization_barrier(values.astype(jnp.bfloat16)).astype(jnp.float32)


def reference(tokens, cotangent, expert_ids, gate_probs, gate_up_weight, down_weight, down_residual):
    group_rows = TOKENS // DP_GROUPS

    def per_group(running, inputs):
        gate_up_sum, down_sum = running
        token_rows, grad_rows, routes, route_probs, residual = inputs
        token_sum = jnp.zeros((group_rows, D), jnp.float32)
        gate_up_list = []
        down_list = []
        for expert in range(EXPERTS):
            weight = jnp.sum(jnp.where(routes == expert, route_probs, jnp.zeros_like(route_probs)), axis=1)
            scaled = (grad_rows.astype(jnp.float32) * weight[:, None]).astype(jnp.bfloat16)
            forward = expert_forward(token_rows, gate_up_weight[expert])
            token_part, gate_up_term, down_term = expert_backward(token_rows, scaled, forward, gate_up_weight[expert], down_weight[expert])
            token_sum = token_sum + token_part.astype(jnp.float32)
            gate_up_list.append(round_trip(gate_up_term))
            down_list.append(round_trip(down_term + residual[expert].astype(jnp.float32)))
        gate_up_sum = gate_up_sum + jnp.stack(gate_up_list)
        down_sum = down_sum + jnp.stack(down_list)
        return (gate_up_sum, down_sum), token_sum.astype(jnp.bfloat16)

    start = (jnp.zeros((EXPERTS, D, 2 * H_DEV), jnp.float32), jnp.zeros((EXPERTS, H_DEV, D), jnp.float32))
    inputs = (tokens.reshape(DP_GROUPS, group_rows, D), cotangent.reshape(DP_GROUPS, group_rows, D), expert_ids.reshape(DP_GROUPS, group_rows, TOP), gate_probs.reshape(DP_GROUPS, group_rows, TOP), down_residual)
    (gate_up_sum, down_sum), token_parts = lax.scan(per_group, start, inputs)
    factor = 1.0 / DP_GROUPS
    return token_parts.reshape(TOKENS, D), gate_up_sum * factor, down_sum * factor
```

```python
import jax
import jax.numpy as jnp
import numpy as np
from jax import lax
from jax.sharding import PartitionSpec as P

INNER = 2


def line_plan(length):
    orders = []
    for place in range(length):
        order = []
        for step in range(1, length):
            right, left = length - step + place, step - length + place
            if place < step and right not in order:
                order.append(right)
            if length - 1 - place < step and left not in order:
                order.append(left)
        order.append(place)
        orders.append(order)
    return np.array(orders, np.int32)


def flip(values, bit):
    count = lax.axis_size("expert")
    return lax.ppermute(values, "expert", [(i, i ^ bit) for i in range(count)])


def wide(values):
    return values.astype(jnp.float32)


def pick(candidates, slots, place):
    used = sorted({int(slot) for slot in slots if slot >= 0})
    chosen = candidates[used[0]]
    for slot in used[1:]:
        mask = np.array([s == slot for s in slots])
        chosen = jnp.where(jnp.asarray(mask)[place], candidates[slot], chosen)
    return chosen


def reduce_over_groups(chunk_of, group_count):
    length = group_count // INNER
    group = lax.axis_index("dp")
    place, side = group // INNER, group % INNER
    orders = line_plan(length)
    order_here = jnp.asarray(orders)[place]
    swap = [(i, i ^ 1) for i in range(group_count)]
    sums = []
    for slot in range(length):
        share = order_here[slot]
        sent = chunk_of(share * INNER + (1 - side))
        kept = chunk_of(share * INNER + side)
        sums.append(wide(kept) + wide(lax.ppermute(sent, "dp", swap)))
    slot_of = np.argsort(orders, axis=1)
    from_left = from_right = None
    for step in range(1, length):
        right_slots = [slot_of[p, length - step + p] if p < step else -1 for p in range(length)]
        left_slots = [
            slot_of[p, step - length + p] if length - 1 - p < step else -1 for p in range(length)
        ]
        to_right = pick(sums, right_slots, place)
        to_left = pick(sums, left_slots, place)
        if step > 1:
            to_right = to_right + wide(from_left)
            to_left = to_left + wide(from_right)
        right_pairs = [
            (p * INNER + s, (p + 1) * INNER + s) for p in range(step) for s in range(INNER)
        ]
        left_pairs = [
            (p * INNER + s, (p - 1) * INNER + s)
            for p in range(length - step, length)
            for s in range(INNER)
        ]
        from_left = lax.ppermute(to_right.astype(jnp.bfloat16), "dp", right_pairs)
        from_right = lax.ppermute(to_left.astype(jnp.bfloat16), "dp", left_pairs)
    return sums[-1] + wide(from_left) + wide(from_right)


def on_device(
    tokens, cotangent, expert_ids, gate_probs, gate_up_weight, down_weight, down_residual
):
    tok_rows, model_width = tokens.shape
    expert_count = lax.axis_size("expert")
    group_count = lax.axis_size("dp")
    gate_up, down_matrix = gate_up_weight[0], down_weight[0]
    hidden_units = down_matrix.shape[0]
    me = lax.axis_index("expert")
    expert_range = jnp.arange(expert_count, dtype=jnp.int32)
    route_hit = expert_ids[None, :, :] == expert_range[:, None, None]
    route = jnp.sum(jnp.where(route_hit, gate_probs[None, :, :], 0.0), axis=2)

    tokens_far = flip(tokens, 2)
    cotangent_far = flip(cotangent, 2)
    near_rows = jnp.concatenate([tokens, flip(tokens, 1)], axis=0)
    near_grads = jnp.concatenate([cotangent, flip(cotangent, 1)], axis=0)
    far_rows = jnp.concatenate([tokens_far, flip(tokens_far, 1)], axis=0)
    far_grads = jnp.concatenate([cotangent_far, flip(cotangent_far, 1)], axis=0)
    route_near = jnp.concatenate([route, flip(route, 1)], axis=1)
    route_all = jnp.concatenate([route_near, flip(route_near, 2)], axis=1)
    weight_here = lax.dynamic_index_in_dim(route_all, me, 0, keepdims=False)[:, None]

    def forward(rows):
        projected = jnp.dot(rows, gate_up, preferred_element_type=jnp.float32)
        gate_part, up_part = projected[:, :hidden_units], projected[:, hidden_units:]
        gate_sig = jax.nn.sigmoid(gate_part)
        activated = gate_part * gate_sig
        slope = up_part * gate_sig * (1.0 + gate_part * (1.0 - gate_sig))
        return (activated * up_part).astype(jnp.bfloat16), slope, activated

    def backward(grads, weight, slope, activated):
        scaled = (wide(grads) * weight).astype(jnp.bfloat16)
        back_hidden = jnp.dot(scaled, down_matrix.T, preferred_element_type=jnp.float32)
        back_both = jnp.concatenate([back_hidden * slope, back_hidden * activated], axis=1)
        return scaled, back_both.astype(jnp.bfloat16)

    near_count = near_rows.shape[0]
    hidden_near, slope_near, act_near = forward(near_rows)
    hidden_far, slope_far, act_far = forward(far_rows)
    scaled_near, back_near = backward(near_grads, weight_here[:near_count], slope_near, act_near)
    scaled_far, back_far = backward(far_grads, weight_here[near_count:], slope_far, act_far)
    all_rows = jnp.concatenate([near_rows, far_rows], axis=0)
    hidden = jnp.concatenate([hidden_near, hidden_far], axis=0)
    scaled = jnp.concatenate([scaled_near, scaled_far], axis=0)
    back_both = jnp.concatenate([back_near, back_far], axis=0)

    contract = (((0,), (0,)), ((), ()))
    gate_up_term = lax.dot_general(
        all_rows, back_both, contract, preferred_element_type=jnp.float32
    ).astype(jnp.bfloat16)
    down_term = lax.dot_general(hidden, scaled, contract, preferred_element_type=jnp.float32)
    down_term = (down_term + wide(down_residual[0, 0])).astype(jnp.bfloat16)
    gate_rows, down_rows = model_width // group_count, hidden_units // group_count
    width = 2 * hidden_units
    folds = model_width // width

    def chunk_of(share):
        gate_part = lax.dynamic_slice_in_dim(gate_up_term, share * gate_rows, gate_rows, 0)
        down_part = lax.dynamic_slice_in_dim(down_term, share * down_rows, down_rows, 0)
        parts = [down_part[:, f * width : (f + 1) * width] for f in range(folds)]
        return jnp.concatenate([gate_part, *parts], axis=0)

    total = reduce_over_groups(chunk_of, group_count) * (1.0 / group_count)
    grad_gate_up = total[:gate_rows]
    grad_down = jnp.concatenate(
        [total[gate_rows + f * down_rows : gate_rows + (f + 1) * down_rows] for f in range(folds)],
        axis=1,
    )

    token_part = jnp.dot(back_both, gate_up.T, preferred_element_type=jnp.float32).astype(
        jnp.bfloat16
    )
    blocks = token_part.reshape(expert_count, tok_rows, model_width)
    own, core, far, far_core = blocks[0], blocks[1], blocks[2], blocks[3]
    crossed = flip(jnp.stack([core, far_core]), 1)
    to_far = (wide(far) + wide(crossed[1])).astype(jnp.bfloat16)
    token_grad = (wide(own) + wide(crossed[0]) + wide(flip(to_far, 2))).astype(jnp.bfloat16)
    return (token_grad, grad_gate_up[None], grad_down[None])


def solution(mesh):
    placed = (
        P(("dp", "expert"), None),
        P(("dp", "expert"), None),
        P(("dp", "expert"), None),
        P(("dp", "expert"), None),
        P("expert", None, None),
        P("expert", None, None),
        P("dp", "expert", None, None),
    )
    return jax.shard_map(
        on_device,
        mesh=mesh,
        in_specs=placed,
        out_specs=(P(("dp", "expert"), None), P("expert", "dp", None), P("expert", "dp", None)),
        check_vma=False,
    )
```

```python
import jax
import jax.numpy as jnp
from jax import lax
from jax.sharding import PartitionSpec as P

LANES = 128


def wide(values):
    return values.astype(jnp.float32)


def narrow(values):
    return values.astype(jnp.bfloat16)


def flip(values, axis, bit):
    return lax.ppermute(values, axis, [(i, i ^ bit) for i in range(lax.axis_size(axis))])


def take(values, axis, index):
    return lax.dynamic_index_in_dim(values, index, axis, keepdims=False)


def with_routes(cotangent, expert_ids, gate_probs, expert_count):
    lane = jnp.arange(LANES, dtype=jnp.int32)[None, :]
    route = jnp.zeros((expert_ids.shape[0], LANES), jnp.float32)
    for k in range(expert_ids.shape[1]):
        hit = (lane < 3 * expert_count) & (lane // 3 == expert_ids[:, k : k + 1])
        route = route + jnp.where(hit, gate_probs[:, k : k + 1], 0.0)
    high = lax.reduce_precision(route, 8, 7)
    middle = lax.reduce_precision(route - high, 8, 7)
    low = (route - high) - middle
    part = lane % 3
    coded = jnp.where(part == 0, high, jnp.where(part == 1, middle, low))
    return jnp.concatenate([cotangent, narrow(coded)], axis=1)


def scaled_rows(carried, width, me):
    lane = jnp.arange(LANES, dtype=jnp.int32)[None, :]
    coded = wide(carried[:, width:])
    part = [
        jnp.sum(jnp.where(lane == 3 * me + k, coded, 0.0), axis=1, keepdims=True) for k in range(3)
    ]
    weight = (part[0] + part[1]) + part[2]
    return narrow(wide(carried[:, :width]) * weight)


def own_columns(values, group_count, parity):
    unit = values.shape[1] // group_count * 2
    blocks = [values[:, k * unit : (k + 1) * unit] for k in range(group_count // 2)]
    even, odd = jnp.concatenate(blocks[0::2], axis=1), jnp.concatenate(blocks[1::2], axis=1)
    return jnp.where(parity == 1, odd, even)


def on_device(
    tokens, cotangent, expert_ids, gate_probs, gate_up_weight, down_weight, down_residual
):
    tok_rows, model_width = tokens.shape
    expert_count = lax.axis_size("expert")
    group_count = lax.axis_size("dp")
    gate_up, down_matrix = gate_up_weight[0], down_weight[0]
    hidden_units = down_matrix.shape[0]
    me, group = lax.axis_index("expert"), lax.axis_index("dp")
    bit0, bit1, bit2 = group & 1, (group >> 1) & 1, (group >> 2) & 1
    high_count = group_count // 8
    half = tok_rows // 2

    tok_x, tok_n = flip(tokens, "expert", 2), flip(tokens, "dp", 2)
    tok_c = flip(tokens, "expert", 1)
    carried = with_routes(cotangent, expert_ids, gate_probs, expert_count)
    cot_x, cot_n = flip(carried, "expert", 2), flip(carried, "dp", 2)
    cot_c = flip(carried, "expert", 1)
    residual = down_residual[0, 0].reshape(high_count, 2, 2, 2, -1, model_width)
    res_got = flip(take(residual, 3, 1 - bit0), "dp", 1)
    tok_d = jnp.concatenate(
        [flip(tok_x[:half], "dp", 2), flip(tok_n[half:], "expert", 2)], axis=0
    )
    cot_d = jnp.concatenate(
        [flip(cot_x[:half], "dp", 2), flip(cot_n[half:], "expert", 2)], axis=0
    )

    def both_cores(values):
        return jnp.concatenate([values, flip(values, "expert", 1)], axis=0)

    rows = [jnp.concatenate([tokens, tok_c], axis=0)] + [both_cores(v) for v in (tok_x, tok_n, tok_d)]
    grads = [jnp.concatenate([carried, cot_c], axis=0)] + [
        both_cores(v) for v in (cot_x, cot_n, cot_d)
    ]

    def forward(token_rows):
        projected = jnp.dot(token_rows, gate_up, preferred_element_type=jnp.float32)
        gate_part, up_part = projected[:, :hidden_units], projected[:, hidden_units:]
        gate_sig = jax.nn.sigmoid(gate_part)
        activated = gate_part * gate_sig
        slope = up_part * gate_sig * (1.0 + gate_part * (1.0 - gate_sig))
        return narrow(activated * up_part), slope, activated

    def backward(grad_rows, slope, activated):
        scaled = scaled_rows(grad_rows, model_width, me)
        back_hidden = jnp.dot(scaled, down_matrix.T, preferred_element_type=jnp.float32)
        back_both = jnp.concatenate([back_hidden * slope, back_hidden * activated], axis=1)
        return scaled, narrow(back_both)

    def terms(token_rows, hidden, scaled, back_both):
        contract = (((0,), (0,)), ((), ()))
        gate = lax.dot_general(
            own_columns(token_rows, group_count, bit1),
            back_both,
            contract,
            preferred_element_type=jnp.float32,
        )
        down = lax.dot_general(
            own_columns(hidden, group_count, bit1),
            scaled,
            contract,
            preferred_element_type=jnp.float32,
        )
        return gate, down

    hidden, scaled, back = [], [], []
    for token_rows, grad_rows in zip(rows, grads):
        hidden_rows, slope, activated = forward(token_rows)
        scaled_here, back_here = backward(grad_rows, slope, activated)
        hidden.append(hidden_rows)
        scaled.append(scaled_here)
        back.append(back_here)
    joined = [jnp.concatenate(v[:3], axis=0) for v in (rows, hidden, scaled, back)]
    gate_early, down_early = terms(*joined)
    gate_late, down_late = terms(rows[3], hidden[3], scaled[3], back[3])
    gate_term = narrow(gate_early + gate_late).reshape(high_count, 2, 2, -1, 2 * hidden_units)
    down_term = narrow(down_early + down_late).reshape(high_count, 2, 2, -1, model_width)

    res_pair = wide(take(residual, 3, bit0)) + wide(res_got)
    res_send = narrow(take(res_pair, 2, 1 - bit1))
    res_send, _ = lax.optimization_barrier((res_send, cot_d))
    res_sum = take(res_pair, 2, bit1) + wide(flip(res_send, "dp", 2))

    def paired(term, side):
        mine = take(term, 1, side)
        return wide(take(mine, 1, bit0)) + wide(flip(take(mine, 1, 1 - bit0), "dp", 1))

    cut = gate_term.shape[3] // 2
    pieces = [gate_term[:, :, :, :cut], gate_term[:, :, :, cut:], down_term]
    far = [paired(piece, 1 - bit2) for piece in pieces]
    far[2] = far[2] + take(res_sum, 1, 1 - bit2)
    crossed = [flip(narrow(piece), "dp", 4) for piece in far]
    gate_sum = paired(gate_term, bit2) + wide(jnp.concatenate(crossed[:2], axis=1))
    down_sum = paired(down_term, bit2) + take(res_sum, 1, bit2) + wide(crossed[2])
    bit = 8
    while bit < group_count:
        side = (group // bit) & 1
        halves = [v.reshape(-1, 2, *v.shape[1:]) for v in (gate_sum, down_sum)]
        gate_sum, down_sum = [
            take(v, 1, side) + wide(flip(narrow(take(v, 1, 1 - side)), "dp", bit)) for v in halves
        ]
        bit *= 2
    factor = 1.0 / group_count
    grad_gate_up, grad_down = gate_sum * factor, down_sum * factor

    back_group = jnp.concatenate(back[:2], axis=0)
    token_part = narrow(jnp.dot(back_group, gate_up.T, preferred_element_type=jnp.float32))
    blocks = token_part.reshape(expert_count, tok_rows, model_width)
    core = flip(jnp.stack([blocks[1], blocks[3]]), "expert", 1)
    across = flip(narrow(wide(blocks[2]) + wide(core[1])), "expert", 2)
    token_grad = narrow(wide(blocks[0]) + wide(core[0]) + wide(across))
    return (token_grad, grad_gate_up, grad_down)


def solution(mesh):
    placed = (
        P(("dp", "expert"), None),
        P(("dp", "expert"), None),
        P(("dp", "expert"), None),
        P(("dp", "expert"), None),
        P("expert", None, None),
        P("expert", None, None),
        P("dp", "expert", None, None),
    )
    return jax.shard_map(
        on_device,
        mesh=mesh,
        in_specs=placed,
        out_specs=(P(("dp", "expert"), None), P("expert", "dp", None), P("expert", "dp", None)),
        check_vma=False,
    )
```

```python
import jax
import jax.numpy as jnp
from jax import lax
from jax.experimental import pallas as pl
from jax.experimental.pallas import tpu as pltpu
from jax.sharding import PartitionSpec as P

LANES = 128


def wide(values):
    return values.astype(jnp.float32)


def narrow(values):
    return values.astype(jnp.bfloat16)


def flip(values, axis, bit):
    return lax.ppermute(values, axis, [(i, i ^ bit) for i in range(lax.axis_size(axis))])


def take(values, axis, index):
    return lax.dynamic_index_in_dim(values, index, axis, keepdims=False)


def with_routes(cotangent, expert_ids, gate_probs, expert_count):
    lane = jnp.arange(LANES, dtype=jnp.int32)[None, :]
    route = jnp.zeros((expert_ids.shape[0], LANES), jnp.float32)
    for k in range(expert_ids.shape[1]):
        hit = (lane < 3 * expert_count) & (lane // 3 == expert_ids[:, k : k + 1])
        route = route + jnp.where(hit, gate_probs[:, k : k + 1], 0.0)
    high = lax.reduce_precision(route, 8, 7)
    middle = lax.reduce_precision(route - high, 8, 7)
    low = (route - high) - middle
    part = lane % 3
    coded = jnp.where(part == 0, high, jnp.where(part == 1, middle, low))
    return jnp.concatenate([cotangent, narrow(coded)], axis=1)


def expert_kernel(me, tok_a, tok_b, cot_a, cot_b, gate_up, down, hidden, scaled, back):
    width, units = gate_up.shape[0], down.shape[0]
    tile = units // 2
    lane = lax.broadcasted_iota(jnp.int32, (1, LANES), 1)
    for cot, at in ((cot_a, 0), (cot_b, cot_a.shape[0])):
        coded = wide(cot[:, width:])
        part = [
            jnp.sum(jnp.where(lane == 3 * me[0] + k, coded, 0.0), axis=1, keepdims=True)
            for k in range(3)
        ]
        weight = (part[0] + part[1]) + part[2]
        scaled[at : at + cot.shape[0], :] = narrow(wide(cot[:, :width]) * weight)
    rows = jnp.concatenate([tok_a[...], tok_b[...]], axis=0)
    grads = scaled[...]
    contract = (((1,), (1,)), ((), ()))
    for at in range(0, units, tile):
        gate = jnp.dot(rows, gate_up[:, at : at + tile], preferred_element_type=jnp.float32)
        up = jnp.dot(
            rows, gate_up[:, units + at : units + at + tile], preferred_element_type=jnp.float32
        )
        sig = jax.nn.sigmoid(gate)
        activated = gate * sig
        hidden[:, at : at + tile] = narrow(activated * up)
        back_hidden = lax.dot_general(
            grads, down[at : at + tile, :], contract, preferred_element_type=jnp.float32
        )
        slope = up * sig * (1.0 + gate * (1.0 - sig))
        back[:, at : at + tile] = narrow(back_hidden * slope)
        back[:, units + at : units + at + tile] = narrow(back_hidden * activated)


def expert_rows(me, tok_a, tok_b, cot_a, cot_b, gate_up, down):
    rows, width = 2 * tok_a.shape[0], tok_a.shape[1]
    units = down.shape[0]
    vmem = pl.BlockSpec(memory_space=pltpu.VMEM)
    return pl.pallas_call(
        expert_kernel,
        out_shape=(
            jax.ShapeDtypeStruct((rows, units), jnp.bfloat16),
            jax.ShapeDtypeStruct((rows, width), jnp.bfloat16),
            jax.ShapeDtypeStruct((rows, 2 * units), jnp.bfloat16),
        ),
        in_specs=[pl.BlockSpec(memory_space=pltpu.SMEM)] + [vmem] * 6,
        out_specs=(vmem, vmem, vmem),
        compiler_params=pltpu.CompilerParams(vmem_limit_bytes=24 << 20),
        cost_estimate=pl.CostEstimate(
            flops=6 * rows * width * units, bytes_accessed=12 << 20, transcendentals=rows * units
        ),
    )(me, tok_a, tok_b, cot_a, cot_b, gate_up, down)


def own_columns(values, group_count, parity):
    unit = values.shape[1] // group_count * 2
    blocks = [values[:, k * unit : (k + 1) * unit] for k in range(group_count // 2)]
    even, odd = jnp.concatenate(blocks[0::2], axis=1), jnp.concatenate(blocks[1::2], axis=1)
    return jnp.where(parity == 1, odd, even)


def on_device(
    tokens, cotangent, expert_ids, gate_probs, gate_up_weight, down_weight, down_residual
):
    tok_rows, model_width = tokens.shape
    expert_count = lax.axis_size("expert")
    group_count = lax.axis_size("dp")
    gate_up, down_matrix = gate_up_weight[0], down_weight[0]
    hidden_units = down_matrix.shape[0]
    me, group = lax.axis_index("expert"), lax.axis_index("dp")
    bit0, bit1, bit2 = group & 1, (group >> 1) & 1, (group >> 2) & 1
    high_count = group_count // 8

    tok_x, tok_c = flip(tokens, "expert", 2), flip(tokens, "expert", 1)
    carried = with_routes(cotangent, expert_ids, gate_probs, expert_count)
    cot_n, cot_c = flip(carried, "dp", 2), flip(carried, "expert", 1)
    tok_n, cot_x = flip(tokens, "dp", 2), flip(carried, "expert", 2)
    residual, tok_c = lax.optimization_barrier((down_residual, tok_c))
    residual = residual[0, 0].reshape(high_count, 2, 2, 2, -1, model_width)
    res_got = flip(take(residual, 3, 1 - bit0), "dp", 1)
    tok_d, cot_d = flip(tok_x, "dp", 2), flip(cot_n, "expert", 2)
    pairs = [(tokens, tok_c, carried, cot_c)] + [
        (tok, flip(tok, "expert", 1), cot, flip(cot, "expert", 1))
        for tok, cot in ((tok_x, cot_x), (tok_n, cot_n), (tok_d, cot_d))
    ]
    number = me.reshape(1).astype(jnp.int32)
    rows = [jnp.concatenate(pair[:2], axis=0) for pair in pairs]
    made = [expert_rows(number, *pair, gate_up, down_matrix) for pair in pairs]
    hidden, scaled, back = zip(*made)

    def terms(token_rows, hidden, scaled, back_both):
        contract = (((0,), (0,)), ((), ()))
        gate = lax.dot_general(
            own_columns(token_rows, group_count, bit1),
            back_both,
            contract,
            preferred_element_type=jnp.float32,
        )
        down = lax.dot_general(
            own_columns(hidden, group_count, bit1),
            scaled,
            contract,
            preferred_element_type=jnp.float32,
        )
        return gate, down

    joined = [jnp.concatenate(v[:3], axis=0) for v in (rows, hidden, scaled, back)]
    gate_early, down_early = terms(*joined)
    gate_late, down_late = terms(rows[3], hidden[3], scaled[3], back[3])
    gate_term = narrow(gate_early + gate_late).reshape(high_count, 2, 2, -1, 2 * hidden_units)
    down_term = narrow(down_early + down_late).reshape(high_count, 2, 2, -1, model_width)

    res_pair = wide(take(residual, 3, bit0)) + wide(res_got)
    res_send = narrow(take(res_pair, 2, 1 - bit1))
    res_send, _ = lax.optimization_barrier((res_send, cot_x))
    res_sum = take(res_pair, 2, bit1) + wide(flip(res_send, "dp", 2))

    def paired(term, side, after):
        mine = take(term, 1, side)
        sent, kept = take(mine, 1, 1 - bit0), take(mine, 1, bit0)
        if after is not None:
            sent, _ = lax.optimization_barrier((sent, after))
        got = flip(sent, "dp", 1)
        return wide(kept) + wide(got), got

    cut = gate_term.shape[3] // 2
    far_a, got_a = paired(gate_term[:, :, :, :cut], 1 - bit2, None)
    far_b, got_b = paired(gate_term[:, :, :, cut:], 1 - bit2, None)
    far_down, got_down = paired(down_term, 1 - bit2, got_a)
    far_down = far_down + take(res_sum, 1, 1 - bit2)
    crossed = [flip(narrow(piece), "dp", 4) for piece in (far_a, far_b, far_down)]
    near_gate, _ = paired(gate_term, bit2, got_b)
    near_down, _ = paired(down_term, bit2, got_down)
    gate_sum = near_gate + wide(jnp.concatenate(crossed[:2], axis=1))
    down_sum = near_down + take(res_sum, 1, bit2) + wide(crossed[2])
    bit = 8
    while bit < group_count:
        side = (group // bit) & 1
        halves = [v.reshape(-1, 2, *v.shape[1:]) for v in (gate_sum, down_sum)]
        gate_sum, down_sum = [
            take(v, 1, side) + wide(flip(narrow(take(v, 1, 1 - side)), "dp", bit)) for v in halves
        ]
        bit *= 2
    factor = 1.0 / group_count
    grad_gate_up, grad_down = gate_sum * factor, down_sum * factor

    back_group = jnp.concatenate(back[:2], axis=0)
    back_group, _ = lax.optimization_barrier((back_group, gate_term))
    token_part = narrow(jnp.dot(back_group, gate_up.T, preferred_element_type=jnp.float32))
    blocks = token_part.reshape(expert_count, tok_rows, model_width)
    core = flip(jnp.stack([blocks[1], blocks[3]]), "expert", 1)
    across = flip(narrow(wide(blocks[2]) + wide(core[1])), "expert", 2)
    token_grad = narrow(wide(blocks[0]) + wide(core[0]) + wide(across))
    return (token_grad, grad_gate_up, grad_down)


def solution(mesh):
    placed = (
        P(("dp", "expert"), None),
        P(("dp", "expert"), None),
        P(("dp", "expert"), None),
        P(("dp", "expert"), None),
        P("expert", None, None),
        P("expert", None, None),
        P("dp", "expert", None, None),
    )
    return jax.shard_map(
        on_device,
        mesh=mesh,
        in_specs=placed,
        out_specs=(P(("dp", "expert"), None), P("expert", "dp", None), P("expert", "dp", None)),
        check_vma=False,
    )
```

```python
import functools

import jax
import jax.numpy as jnp
from jax import lax
from jax.experimental import pallas as pl
from jax.experimental.pallas import tpu as pltpu
from jax.sharding import PartitionSpec as P

LANES = 128


def wide(values):
    return values.astype(jnp.float32)


def narrow(values):
    return values.astype(jnp.bfloat16)


def flip(values, axis, bit):
    return lax.ppermute(values, axis, [(i, i ^ bit) for i in range(lax.axis_size(axis))])


def take(values, axis, index):
    return lax.dynamic_index_in_dim(values, index, axis, keepdims=False)


def carry_kernel(expert_count, cotangent, expert_ids, gate_probs, carried):
    width = cotangent.shape[1]
    lane = lax.broadcasted_iota(jnp.int32, (1, LANES), 1)
    route = jnp.zeros((cotangent.shape[0], LANES), jnp.float32)
    for k in range(expert_ids.shape[1]):
        first = 3 * expert_ids[:, k : k + 1]
        hit = (lane >= first) & (lane < first + 3)
        route = route + jnp.where(hit, gate_probs[:, k : k + 1], 0.0)
    high = wide(narrow(route))
    middle = wide(narrow(route - high))
    low = (route - high) - middle
    part = lax.rem(lane, 3)
    coded = jnp.where(part == 0, high, jnp.where(part == 1, middle, low))
    carried[:, :width] = cotangent[...]
    carried[:, width:] = narrow(coded)


def with_routes(cotangent, expert_ids, gate_probs, expert_count):
    rows, width = cotangent.shape
    vmem = pl.BlockSpec(memory_space=pltpu.VMEM)
    return pl.pallas_call(
        functools.partial(carry_kernel, expert_count),
        out_shape=jax.ShapeDtypeStruct((rows, width + LANES), jnp.bfloat16),
        in_specs=[vmem] * 3,
        out_specs=vmem,
        cost_estimate=pl.CostEstimate(
            flops=rows * LANES, bytes_accessed=4 * rows * width, transcendentals=0
        ),
    )(cotangent, expert_ids, gate_probs)


def expert_kernel(me, tok_a, tok_b, cot_a, cot_b, gate_up, down, hidden, scaled, back):
    width, units = gate_up.shape[0], down.shape[0]
    tile = units // 2
    lane = lax.broadcasted_iota(jnp.int32, (1, LANES), 1)
    for cot, at in ((cot_a, 0), (cot_b, cot_a.shape[0])):
        coded = wide(cot[:, width:])
        part = [
            jnp.sum(jnp.where(lane == 3 * me[0] + k, coded, 0.0), axis=1, keepdims=True)
            for k in range(3)
        ]
        weight = (part[0] + part[1]) + part[2]
        scaled[at : at + cot.shape[0], :] = narrow(wide(cot[:, :width]) * weight)
    rows = jnp.concatenate([tok_a[...], tok_b[...]], axis=0)
    grads = scaled[...]
    contract = (((1,), (1,)), ((), ()))
    for at in range(0, units, tile):
        gate = jnp.dot(rows, gate_up[:, at : at + tile], preferred_element_type=jnp.float32)
        up = jnp.dot(
            rows, gate_up[:, units + at : units + at + tile], preferred_element_type=jnp.float32
        )
        sig = jax.nn.sigmoid(gate)
        activated = gate * sig
        hidden[:, at : at + tile] = narrow(activated * up)
        back_hidden = lax.dot_general(
            grads, down[at : at + tile, :], contract, preferred_element_type=jnp.float32
        )
        slope = up * sig * (1.0 + gate * (1.0 - sig))
        back[:, at : at + tile] = narrow(back_hidden * slope)
        back[:, units + at : units + at + tile] = narrow(back_hidden * activated)


def expert_rows(me, tok_a, tok_b, cot_a, cot_b, gate_up, down):
    rows, width = 2 * tok_a.shape[0], tok_a.shape[1]
    units = down.shape[0]
    vmem = pl.BlockSpec(memory_space=pltpu.VMEM)
    return pl.pallas_call(
        expert_kernel,
        out_shape=(
            jax.ShapeDtypeStruct((rows, units), jnp.bfloat16),
            jax.ShapeDtypeStruct((rows, width), jnp.bfloat16),
            jax.ShapeDtypeStruct((rows, 2 * units), jnp.bfloat16),
        ),
        in_specs=[pl.BlockSpec(memory_space=pltpu.SMEM)] + [vmem] * 6,
        out_specs=(vmem, vmem, vmem),
        compiler_params=pltpu.CompilerParams(vmem_limit_bytes=24 << 20),
        cost_estimate=pl.CostEstimate(
            flops=6 * rows * width * units, bytes_accessed=8 * rows * width, transcendentals=0
        ),
    )(me, tok_a, tok_b, cot_a, cot_b, gate_up, down)


def own_columns(values, group_count, parity):
    unit = values.shape[1] // group_count * 2
    blocks = [values[:, k * unit : (k + 1) * unit] for k in range(group_count // 2)]
    even, odd = jnp.concatenate(blocks[0::2], axis=1), jnp.concatenate(blocks[1::2], axis=1)
    return jnp.where(parity == 1, odd, even)


def on_device(
    tokens, cotangent, expert_ids, gate_probs, gate_up_weight, down_weight, down_residual
):
    tok_rows, model_width = tokens.shape
    expert_count = lax.axis_size("expert")
    group_count = lax.axis_size("dp")
    gate_up, down_matrix = gate_up_weight[0], down_weight[0]
    hidden_units = down_matrix.shape[0]
    me, group = lax.axis_index("expert"), lax.axis_index("dp")
    bit0, bit1, bit2 = group & 1, (group >> 1) & 1, (group >> 2) & 1
    high_count = group_count // 8

    residual = down_residual[0, 0].reshape(high_count, 2, 2, 2, -1, model_width)

    def residual_pair(parity, source):
        part = take(source, 2, parity)
        return wide(take(part, 2, bit0)) + wide(flip(take(part, 2, 1 - bit0), "dp", 1))

    tok_x, tok_c = flip(tokens, "expert", 2), flip(tokens, "expert", 1)
    carried = with_routes(cotangent, expert_ids, gate_probs, expert_count)
    cot_n, cot_c = flip(carried, "dp", 2), flip(carried, "expert", 1)
    res_other = narrow(residual_pair(1 - bit1, residual))
    tok_x, cot_n, res_other, tok_own, cot_own, residual = lax.optimization_barrier(
        (tok_x, cot_n, res_other, tokens, carried, residual)
    )
    tok_n, cot_x = flip(tok_own, "dp", 2), flip(cot_own, "expert", 2)
    tok_d, cot_d = flip(tok_x, "dp", 2), flip(cot_n, "expert", 2)
    tok_xc, cot_nc = flip(tok_x, "expert", 1), flip(cot_n, "expert", 1)
    res_mine = residual_pair(bit1, residual)
    number = me.reshape(1).astype(jnp.int32)
    pairs = [(tok_own, tok_c, cot_own, cot_c)]
    made = [expert_rows(number, *pairs[0], gate_up, down_matrix)]
    tok_n, cot_x, res_mine, res_other, made = lax.optimization_barrier(
        (tok_n, cot_x, res_mine, res_other, made)
    )
    pairs.append((tok_x, tok_xc, cot_x, flip(cot_x, "expert", 1)))
    pairs.append((tok_n, flip(tok_n, "expert", 1), cot_n, cot_nc))
    res_sum = res_mine + wide(flip(res_other, "dp", 2))
    made += [expert_rows(number, *pair, gate_up, down_matrix) for pair in pairs[1:]]
    pairs.append((tok_d, flip(tok_d, "expert", 1), cot_d, flip(cot_d, "expert", 1)))
    made += [expert_rows(number, *pairs[3], gate_up, down_matrix)]
    rows = [jnp.concatenate(pair[:2], axis=0) for pair in pairs]
    hidden, scaled, back = zip(*made)

    def terms(token_rows, hidden, scaled, back_both):
        contract = (((0,), (0,)), ((), ()))
        gate = lax.dot_general(
            own_columns(token_rows, group_count, bit1),
            back_both,
            contract,
            preferred_element_type=jnp.float32,
        )
        down = lax.dot_general(
            own_columns(hidden, group_count, bit1),
            scaled,
            contract,
            preferred_element_type=jnp.float32,
        )
        return gate, down

    joined = [jnp.concatenate(v[:3], axis=0) for v in (rows, hidden, scaled, back)]
    gate_early, down_early = terms(*joined)
    gate_late, down_late = terms(rows[3], hidden[3], scaled[3], back[3])
    gate_term = narrow(gate_early + gate_late).reshape(high_count, 2, 2, -1, 2 * hidden_units)
    down_term = narrow(down_early + down_late).reshape(high_count, 2, 2, -1, model_width)

    def paired(term, side, after):
        mine = take(term, 1, side)
        sent, kept = take(mine, 1, 1 - bit0), take(mine, 1, bit0)
        if after is not None:
            sent, _ = lax.optimization_barrier((sent, after))
        got = flip(sent, "dp", 1)
        return wide(kept) + wide(got), got

    count = gate_term.shape[3]
    edges = [0, count // 4, count // 2, count]
    far = [
        paired(gate_term[:, :, :, start:stop], 1 - bit2, None)
        for start, stop in zip(edges, edges[1:])
    ]
    far_down, got_down = paired(down_term, 1 - bit2, far[1][1])
    far_down = far_down + take(res_sum, 1, 1 - bit2)
    crossed = [flip(narrow(piece), "dp", 4) for piece, _ in far]
    crossed_down = flip(narrow(far_down), "dp", 4)

    back_group = jnp.concatenate(back[:2], axis=0)
    back_group, _ = lax.optimization_barrier((back_group, gate_term))
    token_part = narrow(jnp.dot(back_group, gate_up.T, preferred_element_type=jnp.float32))
    blocks = token_part.reshape(expert_count, tok_rows, model_width)
    core = flip(jnp.stack([blocks[1], blocks[3]]), "expert", 1)
    across = flip(narrow(wide(blocks[2]) + wide(core[1])), "expert", 2)
    token_grad = narrow(wide(blocks[0]) + wide(core[0]) + wide(across))

    near_gate, _ = paired(gate_term, bit2, far[2][1])
    near_down, _ = paired(down_term, bit2, (got_down, token_grad))
    gate_sum = near_gate + wide(jnp.concatenate(crossed, axis=1))
    down_sum = near_down + take(res_sum, 1, bit2) + wide(crossed_down)
    bit = 8
    while bit < group_count:
        side = (group // bit) & 1
        halves = [v.reshape(-1, 2, *v.shape[1:]) for v in (gate_sum, down_sum)]
        gate_sum, down_sum = [
            take(v, 1, side) + wide(flip(narrow(take(v, 1, 1 - side)), "dp", bit)) for v in halves
        ]
        bit *= 2
    factor = 1.0 / group_count
    grad_gate_up, grad_down = gate_sum * factor, down_sum * factor
    return (token_grad, grad_gate_up, grad_down)


def solution(mesh):
    placed = (
        P(("dp", "expert"), None),
        P(("dp", "expert"), None),
        P(("dp", "expert"), None),
        P(("dp", "expert"), None),
        P("expert", None, None),
        P("expert", None, None),
        P("dp", "expert", None, None),
    )
    return jax.shard_map(
        on_device,
        mesh=mesh,
        in_specs=placed,
        out_specs=(P(("dp", "expert"), None), P("expert", "dp", None), P("expert", "dp", None)),
        check_vma=False,
    )
```

```python
import functools

import jax
import jax.numpy as jnp
from jax import lax
from jax.experimental import pallas as pl
from jax.experimental.pallas import tpu as pltpu
from jax.sharding import PartitionSpec as P

LANES = 128


def wide(values):
    return values.astype(jnp.float32)


def narrow(values):
    return values.astype(jnp.bfloat16)


def flip(values, axis, bit):
    return lax.ppermute(values, axis, [(i, i ^ bit) for i in range(lax.axis_size(axis))])


def take(values, axis, index):
    return lax.dynamic_index_in_dim(values, index, axis, keepdims=False)


def with_routes(cotangent, expert_ids, gate_probs, expert_count):
    lane = jnp.arange(LANES, dtype=jnp.int32)[None, :]
    route = jnp.zeros((expert_ids.shape[0], LANES), jnp.float32)
    for k in range(expert_ids.shape[1]):
        hit = (lane < 3 * expert_count) & (lane // 3 == expert_ids[:, k : k + 1])
        route = route + jnp.where(hit, gate_probs[:, k : k + 1], 0.0)
    high = lax.reduce_precision(route, 8, 7)
    middle = lax.reduce_precision(route - high, 8, 7)
    low = (route - high) - middle
    part = lane % 3
    coded = jnp.where(part == 0, high, jnp.where(part == 1, middle, low))
    return jnp.concatenate([cotangent, narrow(coded)], axis=1)


def own_columns(values, group_count, parity):
    unit = values.shape[1] // group_count * 2
    blocks = [values[:, k * unit : (k + 1) * unit] for k in range(group_count // 2)]
    even, odd = jnp.concatenate(blocks[0::2], axis=1), jnp.concatenate(blocks[1::2], axis=1)
    return jnp.where(parity == 1, odd, even)


def expert_kernel(
    group_count, place, tok_a, tok_b, cot_a, cot_b, gate_up, down, tok_own, hid_own, scaled, back
):
    width, units = gate_up.shape[0], down.shape[0]
    tile = units // 2
    me, parity = place[0], place[1]
    lane = lax.broadcasted_iota(jnp.int32, (1, LANES), 1)
    for cot, at in ((cot_a, 0), (cot_b, cot_a.shape[0])):
        coded = wide(cot[:, width:])
        part = [
            jnp.sum(jnp.where(lane == 3 * me + k, coded, 0.0), axis=1, keepdims=True)
            for k in range(3)
        ]
        weight = (part[0] + part[1]) + part[2]
        scaled[at : at + cot.shape[0], :] = narrow(wide(cot[:, :width]) * weight)
    rows = jnp.concatenate([tok_a[...], tok_b[...]], axis=0)
    tok_own[...] = own_columns(rows, group_count, parity)
    grads = scaled[...]
    contract = (((1,), (1,)), ((), ()))
    hidden = []
    for at in range(0, units, tile):
        gate = jnp.dot(rows, gate_up[:, at : at + tile], preferred_element_type=jnp.float32)
        up = jnp.dot(
            rows, gate_up[:, units + at : units + at + tile], preferred_element_type=jnp.float32
        )
        sig = jax.nn.sigmoid(gate)
        activated = gate * sig
        hidden.append(narrow(activated * up))
        back_hidden = lax.dot_general(
            grads, down[at : at + tile, :], contract, preferred_element_type=jnp.float32
        )
        slope = up * sig * (1.0 + gate * (1.0 - sig))
        back[:, at : at + tile] = narrow(back_hidden * slope)
        back[:, units + at : units + at + tile] = narrow(back_hidden * activated)
    hid_own[...] = own_columns(jnp.concatenate(hidden, axis=1), group_count, parity)


def expert_rows(group_count, place, tok_a, tok_b, cot_a, cot_b, gate_up, down):
    rows, width = 2 * tok_a.shape[0], tok_a.shape[1]
    units = down.shape[0]
    vmem = pl.BlockSpec(memory_space=pltpu.VMEM)
    widths = (width // 2, units // 2, width, 2 * units)
    return pl.pallas_call(
        functools.partial(expert_kernel, group_count),
        out_shape=tuple(jax.ShapeDtypeStruct((rows, w), jnp.bfloat16) for w in widths),
        in_specs=[pl.BlockSpec(memory_space=pltpu.SMEM)] + [vmem] * 6,
        out_specs=(vmem,) * 4,
        compiler_params=pltpu.CompilerParams(vmem_limit_bytes=24 << 20),
        cost_estimate=pl.CostEstimate(flops=0, bytes_accessed=0, transcendentals=0),
    )(place, tok_a, tok_b, cot_a, cot_b, gate_up, down)


def on_device(
    tokens, cotangent, expert_ids, gate_probs, gate_up_weight, down_weight, down_residual
):
    tok_rows, model_width = tokens.shape
    expert_count = lax.axis_size("expert")
    group_count = lax.axis_size("dp")
    gate_up, down_matrix = gate_up_weight[0], down_weight[0]
    hidden_units = down_matrix.shape[0]
    me, group = lax.axis_index("expert"), lax.axis_index("dp")
    bit0, bit1, bit2 = group & 1, (group >> 1) & 1, (group >> 2) & 1
    high_count = group_count // 8

    tok_x, tok_n = flip(tokens, "expert", 2), flip(tokens, "dp", 2)
    tok_c = flip(tokens, "expert", 1)
    carried = with_routes(cotangent, expert_ids, gate_probs, expert_count)
    cot_x, cot_n = flip(carried, "expert", 2), flip(carried, "dp", 2)
    cot_c = flip(carried, "expert", 1)
    residual = down_residual[0, 0].reshape(high_count, 2, 2, 2, -1, model_width)
    res_got = flip(take(residual, 3, 1 - bit0), "dp", 1)
    tok_x, tok_n, tok_c, cot_x, cot_n, cot_c, res_got, tok_own, cot_own = lax.optimization_barrier(
        (tok_x, tok_n, tok_c, cot_x, cot_n, cot_c, res_got, tokens, carried)
    )
    tok_d, cot_d = flip(tok_x, "dp", 2), flip(cot_n, "expert", 2)
    place = jnp.stack([me, bit1]).astype(jnp.int32)

    def expert_on(tok, tok_other, cot, cot_other):
        return expert_rows(
            group_count, place, tok, tok_other, cot, cot_other, gate_up, down_matrix
        )

    def both_cores(tok, cot):
        return expert_on(tok, flip(tok, "expert", 1), cot, flip(cot, "expert", 1))

    made = [expert_on(tok_own, tok_c, cot_own, cot_c)]
    made += [both_cores(tok_x, cot_x), both_cores(tok_n, cot_n)]

    def terms(tok_cols, hid_cols, scaled, back):
        contract = (((0,), (0,)), ((), ()))
        gate = lax.dot_general(tok_cols, back, contract, preferred_element_type=jnp.float32)
        down = lax.dot_general(hid_cols, scaled, contract, preferred_element_type=jnp.float32)
        return gate, down

    early = [jnp.concatenate(v, axis=0) for v in zip(*made)]
    gate_early, down_early = terms(*early)
    tok_d, cot_d, gate_early, down_early = lax.optimization_barrier(
        (tok_d, cot_d, gate_early, down_early)
    )
    gate_late, down_late = terms(*both_cores(tok_d, cot_d))
    gate_term = narrow(gate_early + gate_late).reshape(high_count, 2, 2, -1, 2 * hidden_units)
    down_term = narrow(down_early + down_late).reshape(high_count, 2, 2, -1, model_width)

    res_pair = wide(take(residual, 3, bit0)) + wide(res_got)
    res_send = narrow(take(res_pair, 2, 1 - bit1))
    res_send, _ = lax.optimization_barrier((res_send, gate_term))
    res_sum = take(res_pair, 2, bit1) + wide(flip(res_send, "dp", 2))

    def paired(term, side, after):
        mine = take(term, 1, side)
        sent, kept = take(mine, 1, 1 - bit0), take(mine, 1, bit0)
        if after is not None:
            sent, _ = lax.optimization_barrier((sent, after))
        got = flip(sent, "dp", 1)
        return wide(kept) + wide(got), got

    count = gate_term.shape[3]
    edges = [0, count // 4, count // 2, count]
    far = [
        paired(gate_term[:, :, :, start:stop], 1 - bit2, None)
        for start, stop in zip(edges, edges[1:])
    ]
    far_down, got_down = paired(down_term, 1 - bit2, far[1][1])
    far_down = far_down + take(res_sum, 1, 1 - bit2)
    crossed = [flip(narrow(piece), "dp", 4) for piece, _ in far]
    crossed_down = flip(narrow(far_down), "dp", 4)

    back_group = jnp.concatenate([made[0][3], made[1][3]], axis=0)
    back_group, _ = lax.optimization_barrier((back_group, far[0][1]))
    token_part = narrow(jnp.dot(back_group, gate_up.T, preferred_element_type=jnp.float32))
    blocks = token_part.reshape(expert_count, tok_rows, model_width)
    core = flip(jnp.stack([blocks[1], blocks[3]]), "expert", 1)
    across = flip(narrow(wide(blocks[2]) + wide(core[1])), "expert", 2)
    token_grad = narrow(wide(blocks[0]) + wide(core[0]) + wide(across))

    near_gate, _ = paired(gate_term, bit2, far[2][1])
    near_down, _ = paired(down_term, bit2, (got_down, token_grad))
    gate_sum = near_gate + wide(jnp.concatenate(crossed, axis=1))
    down_sum = near_down + take(res_sum, 1, bit2) + wide(crossed_down)
    bit = 8
    while bit < group_count:
        side = (group // bit) & 1
        halves = [v.reshape(-1, 2, *v.shape[1:]) for v in (gate_sum, down_sum)]
        gate_sum, down_sum = [
            take(v, 1, side) + wide(flip(narrow(take(v, 1, 1 - side)), "dp", bit)) for v in halves
        ]
        bit *= 2
    factor = 1.0 / group_count
    grad_gate_up, grad_down = gate_sum * factor, down_sum * factor
    return (token_grad, grad_gate_up, grad_down)


def solution(mesh):
    placed = (
        P(("dp", "expert"), None),
        P(("dp", "expert"), None),
        P(("dp", "expert"), None),
        P(("dp", "expert"), None),
        P("expert", None, None),
        P("expert", None, None),
        P("dp", "expert", None, None),
    )
    return jax.shard_map(
        on_device,
        mesh=mesh,
        in_specs=placed,
        out_specs=(P(("dp", "expert"), None), P("expert", "dp", None), P("expert", "dp", None)),
        check_vma=False,
    )
```

```python
import functools

import jax
import jax.numpy as jnp
from jax import lax
from jax.experimental import pallas as pl
from jax.experimental.pallas import tpu as pltpu
from jax.sharding import PartitionSpec as P

LANES = 128


def wide(values):
    return values.astype(jnp.float32)


def narrow(values):
    return values.astype(jnp.bfloat16)


def flip(values, axis, bit):
    return lax.ppermute(values, axis, [(i, i ^ bit) for i in range(lax.axis_size(axis))])


def take(values, axis, index):
    return lax.dynamic_index_in_dim(values, index, axis, keepdims=False)


def with_routes(cotangent, expert_ids, gate_probs, expert_count):
    lane = jnp.arange(LANES, dtype=jnp.int32)[None, :]
    route = jnp.zeros((expert_ids.shape[0], LANES), jnp.float32)
    for k in range(expert_ids.shape[1]):
        hit = (lane < 3 * expert_count) & (lane // 3 == expert_ids[:, k : k + 1])
        route = route + jnp.where(hit, gate_probs[:, k : k + 1], 0.0)
    high = lax.reduce_precision(route, 8, 7)
    middle = lax.reduce_precision(route - high, 8, 7)
    low = (route - high) - middle
    part = lane % 3
    coded = jnp.where(part == 0, high, jnp.where(part == 1, middle, low))
    return jnp.concatenate([cotangent, narrow(coded)], axis=1)


def own_columns(values, group_count, parity):
    unit = values.shape[1] // group_count * 2
    blocks = [values[:, k * unit : (k + 1) * unit] for k in range(group_count // 2)]
    even, odd = jnp.concatenate(blocks[0::2], axis=1), jnp.concatenate(blocks[1::2], axis=1)
    return jnp.where(parity == 1, odd, even)


def expert_rows(place, group_count, toks, cots, gate_up, down, scaled, back):
    width, units = gate_up.shape[0], down.shape[0]
    tile = units // 2
    lane = lax.broadcasted_iota(jnp.int32, (1, LANES), 1)
    at = 0
    for cot in cots:
        coded = wide(cot[:, width:])
        part = [
            jnp.sum(jnp.where(lane == 3 * place[0] + k, coded, 0.0), axis=1, keepdims=True)
            for k in range(3)
        ]
        weight = (part[0] + part[1]) + part[2]
        scaled[at : at + cot.shape[0], :] = narrow(wide(cot[:, :width]) * weight)
        at += cot.shape[0]
    rows = jnp.concatenate([tok[...] for tok in toks], axis=0)
    grads = scaled[...]
    contract = (((1,), (1,)), ((), ()))
    hidden = []
    for at in range(0, units, tile):
        gate = jnp.dot(rows, gate_up[:, at : at + tile], preferred_element_type=jnp.float32)
        up = jnp.dot(
            rows, gate_up[:, units + at : units + at + tile], preferred_element_type=jnp.float32
        )
        sig = jax.nn.sigmoid(gate)
        activated = gate * sig
        hidden.append(narrow(activated * up))
        back_hidden = lax.dot_general(
            grads, down[at : at + tile, :], contract, preferred_element_type=jnp.float32
        )
        slope = up * sig * (1.0 + gate * (1.0 - sig))
        back[:, at : at + tile] = narrow(back_hidden * slope)
        back[:, units + at : units + at + tile] = narrow(back_hidden * activated)
    hid_cols = own_columns(jnp.concatenate(hidden, axis=1), group_count, place[1])
    return own_columns(rows, group_count, place[1]), hid_cols


ROWS = (((0,), (0,)), ((), ()))


def early_kernel(group_count, place, *refs):
    pairs, (gate_up, down, gate_sum, down_sum, back_group, scaled, back) = refs[:12], refs[12:]
    rows = scaled.shape[0]
    for k in range(3):
        tok_a, tok_b, cot_a, cot_b = pairs[4 * k : 4 * k + 4]
        here = back_group.at[k * rows : (k + 1) * rows, :] if k < 2 else back
        tok_cols, hid_cols = expert_rows(
            place, group_count, (tok_a, tok_b), (cot_a, cot_b), gate_up, down, scaled, here
        )
        gate = lax.dot_general(tok_cols, here[...], ROWS, preferred_element_type=jnp.float32)
        down_part = lax.dot_general(hid_cols, scaled[...], ROWS, preferred_element_type=jnp.float32)
        gate_sum[...] = gate if k == 0 else gate_sum[...] + gate
        down_sum[...] = down_part if k == 0 else down_sum[...] + down_part


def early_terms(group_count, place, pairs, gate_up, down):
    rows, width = 2 * pairs[0][0].shape[0], pairs[0][0].shape[1]
    units = down.shape[0]
    vmem = pl.BlockSpec(memory_space=pltpu.VMEM)
    return pl.pallas_call(
        functools.partial(early_kernel, group_count),
        out_shape=(
            jax.ShapeDtypeStruct((width // 2, 2 * units), jnp.float32),
            jax.ShapeDtypeStruct((units // 2, width), jnp.float32),
            jax.ShapeDtypeStruct((2 * rows, 2 * units), jnp.bfloat16),
        ),
        in_specs=[pl.BlockSpec(memory_space=pltpu.SMEM)] + [vmem] * 14,
        out_specs=(vmem,) * 3,
        scratch_shapes=[
            pltpu.VMEM((rows, width), jnp.bfloat16),
            pltpu.VMEM((rows, 2 * units), jnp.bfloat16),
        ],
        compiler_params=pltpu.CompilerParams(vmem_limit_bytes=30 << 20),
        cost_estimate=pl.CostEstimate(flops=0, bytes_accessed=0, transcendentals=0),
    )(place, *[v for pair in pairs for v in pair], gate_up, down)


def last_kernel(group_count, cuts, place, *refs):
    tok_a, tok_b, cot_a, cot_b, gate_up, down, gate_sum, hid_own, scaled = refs[:9]
    pieces, (back, total) = refs[9:-2], refs[-2:]
    tok_cols, hid_own[...] = expert_rows(
        place, group_count, (tok_a, tok_b), (cot_a, cot_b), gate_up, down, scaled, back
    )
    term = lax.dot_general(tok_cols, back[...], ROWS, preferred_element_type=jnp.float32)
    total[...] = gate_sum[...] + term
    bit0, bit2 = place[2], place[3]
    count = total.shape[0] // (group_count // 2)
    sides = ((1 - bit2, 1 - bit0), (1 - bit2, bit0), (bit2, 1 - bit0), (bit2, bit0))
    at = 0
    for (third, first), splits in zip(sides, (cuts, cuts, (0, count), (0, count))):
        for start, stop in zip(splits, splits[1:]):
            for high in range(group_count // 8):
                row = (high * 4 + third * 2 + first) * count + start
                row = pl.multiple_of(row, 8)
                pieces[at][high] = narrow(total[pl.ds(row, stop - start), :])
            at += 1


def last_terms(group_count, cuts, place, pair, gate_up, down, gate_sum):
    rows, width = 2 * pair[0].shape[0], pair[0].shape[1]
    units, high_count, count = down.shape[0], group_count // 8, cuts[-1]
    sizes = [b - a for a, b in zip(cuts, cuts[1:])] * 2 + [count] * 2
    vmem = pl.BlockSpec(memory_space=pltpu.VMEM)
    shapes = [(rows, units // 2), (rows, width)]
    shapes += [(high_count, size, 2 * units) for size in sizes]
    return pl.pallas_call(
        functools.partial(last_kernel, group_count, cuts),
        out_shape=tuple(jax.ShapeDtypeStruct(shape, jnp.bfloat16) for shape in shapes),
        in_specs=[pl.BlockSpec(memory_space=pltpu.SMEM)] + [vmem] * 7,
        out_specs=(vmem,) * len(shapes),
        scratch_shapes=[
            pltpu.VMEM((rows, 2 * units), jnp.bfloat16),
            pltpu.VMEM((width // 2, 2 * units), jnp.float32),
        ],
        compiler_params=pltpu.CompilerParams(vmem_limit_bytes=30 << 20),
        cost_estimate=pl.CostEstimate(flops=0, bytes_accessed=0, transcendentals=0),
    )(place, *pair, gate_up, down, gate_sum)


def on_device(
    tokens, cotangent, expert_ids, gate_probs, gate_up_weight, down_weight, down_residual
):
    tok_rows, model_width = tokens.shape
    expert_count = lax.axis_size("expert")
    group_count = lax.axis_size("dp")
    gate_up, down_matrix = gate_up_weight[0], down_weight[0]
    hidden_units = down_matrix.shape[0]
    me, group = lax.axis_index("expert"), lax.axis_index("dp")
    bit0, bit1, bit2 = group & 1, (group >> 1) & 1, (group >> 2) & 1
    high_count = group_count // 8

    residual = down_residual[0, 0].reshape(high_count, 2, 2, 2, -1, model_width)

    def residual_pair(source, parity):
        part = take(source, 2, parity)
        return take(part, 2, bit0), flip(take(part, 2, 1 - bit0), "dp", 1)

    tok_x, tok_n = flip(tokens, "expert", 2), flip(tokens, "dp", 2)
    tok_c = flip(tokens, "expert", 1)
    carried = with_routes(cotangent, expert_ids, gate_probs, expert_count)
    cot_x, cot_n = flip(carried, "expert", 2), flip(carried, "dp", 2)
    cot_c = flip(carried, "expert", 1)
    res_other = residual_pair(residual, 1 - bit1)
    tok_x, tok_n, tok_c, cot_x, cot_n, cot_c, tok_own, cot_own, res_other, residual = (
        lax.optimization_barrier(
            (tok_x, tok_n, tok_c, cot_x, cot_n, cot_c, tokens, carried, res_other, residual)
        )
    )
    tok_d, cot_d = flip(tok_x, "dp", 2), flip(cot_n, "expert", 2)
    res_mine = residual_pair(residual, bit1)
    place = jnp.stack([me, bit1, bit0, bit2]).astype(jnp.int32)

    def both_cores(tok, cot):
        return tok, flip(tok, "expert", 1), cot, flip(cot, "expert", 1)

    pairs = ((tok_own, tok_c, cot_own, cot_c), both_cores(tok_x, cot_x), both_cores(tok_n, cot_n))
    gate_sum, down_sum, back_group = early_terms(group_count, place, pairs, gate_up, down_matrix)
    tok_d, cot_d, gate_sum, down_sum, res_mine = lax.optimization_barrier(
        (tok_d, cot_d, gate_sum, down_sum, res_mine)
    )
    count = model_width // group_count
    first = max(count // 4, 16)
    cuts = (0, first, count // 2, count) if first < count // 2 else (0, first, count)
    hid_cols, scaled, *gate_pieces = last_terms(
        group_count, cuts, place, both_cores(tok_d, cot_d), gate_up, down_matrix, gate_sum
    )
    down_term = lax.dot_general(hid_cols, scaled, ROWS, preferred_element_type=jnp.float32)
    down_term = narrow(down_sum + down_term).reshape(high_count, 2, 2, -1, model_width)

    parts = len(cuts) - 1
    far_sent, far_kept = gate_pieces[:parts], gate_pieces[parts : 2 * parts]
    near_sent, near_kept = gate_pieces[2 * parts :]
    got = [flip(far_sent[0], "dp", 1)]
    second, down_term = lax.optimization_barrier((far_sent[1], down_term))
    got.append(flip(second, "dp", 1))
    for piece in far_sent[2:]:
        piece, _ = lax.optimization_barrier((piece, got[0]))
        got.append(flip(piece, "dp", 1))
    crossed = [
        flip(narrow(wide(kept) + wide(piece)), "dp", 4) for kept, piece in zip(far_kept, got)
    ]

    def down_side(third, side):
        return take(take(down_term, 1, third), 1, side)

    res_send = narrow(wide(res_other[0]) + wide(res_other[1]))
    res_send, _ = lax.optimization_barrier((res_send, got[0]))
    res_sum = wide(res_mine[0]) + wide(res_mine[1]) + wide(flip(res_send, "dp", 2))
    down_sent, _ = lax.optimization_barrier((down_side(1 - bit2, 1 - bit0), got[1]))
    got_down = flip(down_sent, "dp", 1)
    far_down = wide(down_side(1 - bit2, bit0)) + wide(got_down) + take(res_sum, 1, 1 - bit2)
    crossed_down = flip(narrow(far_down), "dp", 4)

    back_group, _ = lax.optimization_barrier((back_group, got[-1]))
    token_part = narrow(jnp.dot(back_group, gate_up.T, preferred_element_type=jnp.float32))
    blocks = token_part.reshape(expert_count, tok_rows, model_width)
    core = flip(jnp.stack([blocks[1], blocks[3]]), "expert", 1)
    across = flip(narrow(wide(blocks[2]) + wide(core[1])), "expert", 2)
    token_grad = narrow(wide(blocks[0]) + wide(core[0]) + wide(across))

    near_sent, _ = lax.optimization_barrier((near_sent, got[-1]))
    near_gate = wide(near_kept) + wide(flip(near_sent, "dp", 1))
    down_sent, _ = lax.optimization_barrier((down_side(bit2, 1 - bit0), got_down))
    near_down = wide(down_side(bit2, bit0)) + wide(flip(down_sent, "dp", 1))
    crossed, token_grad = lax.optimization_barrier((crossed, token_grad))
    gate_sum = near_gate + wide(jnp.concatenate(crossed, axis=1))
    down_sum = near_down + take(res_sum, 1, bit2) + wide(crossed_down)
    bit = 8
    while bit < group_count:
        side = (group // bit) & 1
        halves = [v.reshape(-1, 2, *v.shape[1:]) for v in (gate_sum, down_sum)]
        gate_sum, down_sum = [
            take(v, 1, side) + wide(flip(narrow(take(v, 1, 1 - side)), "dp", bit)) for v in halves
        ]
        bit *= 2
    factor = 1.0 / group_count
    grad_gate_up, grad_down = gate_sum * factor, down_sum * factor
    return (token_grad, grad_gate_up, grad_down)


def solution(mesh):
    placed = (
        P(("dp", "expert"), None),
        P(("dp", "expert"), None),
        P(("dp", "expert"), None),
        P(("dp", "expert"), None),
        P("expert", None, None),
        P("expert", None, None),
        P("dp", "expert", None, None),
    )
    return jax.shard_map(
        on_device,
        mesh=mesh,
        in_specs=placed,
        out_specs=(P(("dp", "expert"), None), P("expert", "dp", None), P("expert", "dp", None)),
        check_vma=False,
    )
```

```python
import functools

import jax
import jax.numpy as jnp
from jax import lax
from jax.experimental import pallas as pl
from jax.experimental.pallas import tpu as pltpu
from jax.sharding import PartitionSpec as P

LANES = 128


def wide(values):
    return values.astype(jnp.float32)


def narrow(values):
    return values.astype(jnp.bfloat16)


def flip(values, axis, bit):
    return lax.ppermute(values, axis, [(i, i ^ bit) for i in range(lax.axis_size(axis))])


def take(values, axis, index):
    return lax.dynamic_index_in_dim(values, index, axis, keepdims=False)


def with_routes(cotangent, expert_ids, gate_probs, expert_count):
    lane = jnp.arange(LANES, dtype=jnp.int32)[None, :]
    route = jnp.zeros((expert_ids.shape[0], LANES), jnp.float32)
    for k in range(expert_ids.shape[1]):
        hit = (lane < 3 * expert_count) & (lane // 3 == expert_ids[:, k : k + 1])
        route = route + jnp.where(hit, gate_probs[:, k : k + 1], 0.0)
    high = lax.reduce_precision(route, 8, 7)
    middle = lax.reduce_precision(route - high, 8, 7)
    low = (route - high) - middle
    part = lane % 3
    coded = jnp.where(part == 0, high, jnp.where(part == 1, middle, low))
    return jnp.concatenate([cotangent, narrow(coded)], axis=1)


def own_columns(values, group_count, parity):
    unit = values.shape[1] // group_count * 2
    blocks = [values[:, k * unit : (k + 1) * unit] for k in range(group_count // 2)]
    even, odd = jnp.concatenate(blocks[0::2], axis=1), jnp.concatenate(blocks[1::2], axis=1)
    return jnp.where(parity == 1, odd, even)


def expert_rows(place, group_count, toks, cots, gate_up, down, scaled, back):
    width, units = gate_up.shape[0], down.shape[0]
    tile = units // 2
    lane = lax.broadcasted_iota(jnp.int32, (1, LANES), 1)
    at = 0
    for cot in cots:
        coded = wide(cot[:, width:])
        part = [
            jnp.sum(jnp.where(lane == 3 * place[0] + k, coded, 0.0), axis=1, keepdims=True)
            for k in range(3)
        ]
        weight = (part[0] + part[1]) + part[2]
        scaled[at : at + cot.shape[0], :] = narrow(wide(cot[:, :width]) * weight)
        at += cot.shape[0]
    rows = jnp.concatenate([tok[...] for tok in toks], axis=0)
    grads = scaled[...]
    contract = (((1,), (1,)), ((), ()))
    hidden = []
    for at in range(0, units, tile):
        gate = jnp.dot(rows, gate_up[:, at : at + tile], preferred_element_type=jnp.float32)
        up = jnp.dot(
            rows, gate_up[:, units + at : units + at + tile], preferred_element_type=jnp.float32
        )
        sig = jax.nn.sigmoid(gate)
        activated = gate * sig
        hidden.append(narrow(activated * up))
        back_hidden = lax.dot_general(
            grads, down[at : at + tile, :], contract, preferred_element_type=jnp.float32
        )
        slope = up * sig * (1.0 + gate * (1.0 - sig))
        back[:, at : at + tile] = narrow(back_hidden * slope)
        back[:, units + at : units + at + tile] = narrow(back_hidden * activated)
    hid_cols = own_columns(jnp.concatenate(hidden, axis=1), group_count, place[1])
    return own_columns(rows, group_count, place[1]), hid_cols


ROWS = (((0,), (0,)), ((), ()))


def own_kernel(group_count, place, tok_a, tok_b, cot_a, cot_b, gate_up, down, _, *made):
    tok_cols, hid_cols, scaled, back = made
    tok_cols[...], hid_cols[...] = expert_rows(
        place, group_count, (tok_a, tok_b), (cot_a, cot_b), gate_up, down, scaled, back
    )


def own_rows(group_count, place, pair, gate_up, down, awaited):
    rows, width = 2 * pair[0].shape[0], pair[0].shape[1]
    units = down.shape[0]
    vmem = pl.BlockSpec(memory_space=pltpu.VMEM)
    widths = (width // 2, units // 2, width, 2 * units)
    return pl.pallas_call(
        functools.partial(own_kernel, group_count),
        out_shape=tuple(jax.ShapeDtypeStruct((rows, w), jnp.bfloat16) for w in widths),
        in_specs=[pl.BlockSpec(memory_space=pltpu.SMEM)]
        + [vmem] * 6
        + [pl.BlockSpec(memory_space=pl.ANY)],
        out_specs=(vmem,) * 4,
        compiler_params=pltpu.CompilerParams(vmem_limit_bytes=24 << 20),
        cost_estimate=pl.CostEstimate(flops=0, bytes_accessed=0, transcendentals=0),
    )(place, *pair, gate_up, down, awaited)


def early_kernel(group_count, place, *refs):
    own, pairs, (gate_up, down, gate_sum, down_sum, back_group) = refs[:4], refs[4:12], refs[12:17]
    tok_cols, hid_cols, scaled, back = refs[17:]
    rows = own[0].shape[0]
    for kept, made in zip((tok_cols, hid_cols, scaled, back), own):
        kept[:rows, :] = made[...]
    for k in range(2):
        tok_a, tok_b, cot_a, cot_b = pairs[4 * k : 4 * k + 4]
        here = slice((k + 1) * rows, (k + 2) * rows)
        tok_cols[here, :], hid_cols[here, :] = expert_rows(
            place,
            group_count,
            (tok_a, tok_b),
            (cot_a, cot_b),
            gate_up,
            down,
            scaled.at[here, :],
            back.at[here, :],
        )
    back_group[...] = back[: 2 * rows, :]
    gate_sum[...] = lax.dot_general(
        tok_cols[...], back[...], ROWS, preferred_element_type=jnp.float32
    )
    down_sum[...] = lax.dot_general(
        hid_cols[...], scaled[...], ROWS, preferred_element_type=jnp.float32
    )


def early_terms(group_count, place, own, pairs, gate_up, down):
    rows, width = own[2].shape
    units = down.shape[0]
    vmem = pl.BlockSpec(memory_space=pltpu.VMEM)
    return pl.pallas_call(
        functools.partial(early_kernel, group_count),
        out_shape=(
            jax.ShapeDtypeStruct((width // 2, 2 * units), jnp.float32),
            jax.ShapeDtypeStruct((units // 2, width), jnp.float32),
            jax.ShapeDtypeStruct((2 * rows, 2 * units), jnp.bfloat16),
        ),
        in_specs=[pl.BlockSpec(memory_space=pltpu.SMEM)] + [vmem] * 14,
        out_specs=(vmem,) * 3,
        scratch_shapes=[pltpu.VMEM((3 * rows, v.shape[1]), jnp.bfloat16) for v in own],
        compiler_params=pltpu.CompilerParams(vmem_limit_bytes=30 << 20),
        cost_estimate=pl.CostEstimate(flops=0, bytes_accessed=0, transcendentals=0),
    )(place, *own, *[v for pair in pairs for v in pair], gate_up, down)


def last_kernel(group_count, cuts, place, *refs):
    tok_a, tok_b, cot_a, cot_b, gate_up, down, gate_sum, _, hid_own, scaled = refs[:10]
    pieces, (back, total) = refs[10:-2], refs[-2:]
    tok_cols, hid_own[...] = expert_rows(
        place, group_count, (tok_a, tok_b), (cot_a, cot_b), gate_up, down, scaled, back
    )
    term = lax.dot_general(tok_cols, back[...], ROWS, preferred_element_type=jnp.float32)
    total[...] = gate_sum[...] + term
    bit0, bit2 = place[2], place[3]
    count = total.shape[0] // (group_count // 2)
    sides = ((1 - bit2, 1 - bit0), (1 - bit2, bit0), (bit2, 1 - bit0), (bit2, bit0))
    at = 0
    for (third, first), splits in zip(sides, (cuts, cuts, (0, count), (0, count))):
        for start, stop in zip(splits, splits[1:]):
            for high in range(group_count // 8):
                row = (high * 4 + third * 2 + first) * count + start
                row = pl.multiple_of(row, 8)
                pieces[at][high] = narrow(total[pl.ds(row, stop - start), :])
            at += 1


def last_terms(group_count, cuts, place, pair, gate_up, down, gate_sum, awaited):
    rows, width = 2 * pair[0].shape[0], pair[0].shape[1]
    units, high_count, count = down.shape[0], group_count // 8, cuts[-1]
    sizes = [b - a for a, b in zip(cuts, cuts[1:])] * 2 + [count] * 2
    vmem = pl.BlockSpec(memory_space=pltpu.VMEM)
    shapes = [(rows, units // 2), (rows, width)]
    shapes += [(high_count, size, 2 * units) for size in sizes]
    return pl.pallas_call(
        functools.partial(last_kernel, group_count, cuts),
        out_shape=tuple(jax.ShapeDtypeStruct(shape, jnp.bfloat16) for shape in shapes),
        in_specs=[pl.BlockSpec(memory_space=pltpu.SMEM)]
        + [vmem] * 7
        + [pl.BlockSpec(memory_space=pl.ANY)],
        out_specs=(vmem,) * len(shapes),
        scratch_shapes=[
            pltpu.VMEM((rows, 2 * units), jnp.bfloat16),
            pltpu.VMEM((width // 2, 2 * units), jnp.float32),
        ],
        compiler_params=pltpu.CompilerParams(vmem_limit_bytes=30 << 20),
        cost_estimate=pl.CostEstimate(flops=0, bytes_accessed=0, transcendentals=0),
    )(place, *pair, gate_up, down, gate_sum, awaited)


def join_kernel(factor, parts, kept, got, *refs):
    at = 0
    for piece in refs[:parts]:
        here = slice(at, at + piece.shape[1])
        total = wide(kept[:, here]) + wide(got[:, here]) + wide(piece[...])
        refs[-1][:, here] = total * factor
        at += piece.shape[1]


def join(factor, kept, got, pieces, awaited):
    vmem = pl.BlockSpec(memory_space=pltpu.VMEM)
    return pl.pallas_call(
        functools.partial(join_kernel, factor, len(pieces)),
        out_shape=jax.ShapeDtypeStruct(kept.shape, jnp.float32),
        in_specs=[vmem] * (2 + len(pieces)) + [pl.BlockSpec(memory_space=pl.ANY)] * len(awaited),
        out_specs=vmem,
        cost_estimate=pl.CostEstimate(flops=0, bytes_accessed=0, transcendentals=0),
    )(kept, got, *pieces, *awaited)


def on_device(
    tokens, cotangent, expert_ids, gate_probs, gate_up_weight, down_weight, down_residual
):
    tok_rows, model_width = tokens.shape
    expert_count = lax.axis_size("expert")
    group_count = lax.axis_size("dp")
    gate_up, down_matrix = gate_up_weight[0], down_weight[0]
    hidden_units = down_matrix.shape[0]
    me, group = lax.axis_index("expert"), lax.axis_index("dp")
    bit0, bit1, bit2 = group & 1, (group >> 1) & 1, (group >> 2) & 1
    high_count = group_count // 8

    corners = []

    def after(values, *arrays):
        seen = [v[(0,) * (v.ndim - 2)][:8, :LANES] for v in arrays]
        values, seen = lax.optimization_barrier((values, seen))
        corners.extend(seen)
        return values

    place = jnp.stack([me, bit1, bit0, bit2]).astype(jnp.int32)
    residual = down_residual[0, 0].reshape(high_count, 2, 2, 2, -1, model_width)

    def residual_pair(parity):
        part = take(residual, 2, parity)
        return take(part, 2, bit0), flip(take(part, 2, 1 - bit0), "dp", 1)

    tok_x, tok_n = flip(tokens, "expert", 2), flip(tokens, "dp", 2)
    tok_c = flip(tokens, "expert", 1)
    carried = with_routes(cotangent, expert_ids, gate_probs, expert_count)
    cot_x, cot_n = flip(carried, "expert", 2), flip(carried, "dp", 2)
    cot_c = flip(carried, "expert", 1)
    res_other, res_mine = residual_pair(1 - bit1), residual_pair(bit1)
    own = own_rows(
        group_count,
        place,
        (tokens, tok_c, carried, cot_c),
        gate_up,
        down_matrix,
        res_other[1],
    )
    tok_d, cot_d = flip(tok_x, "dp", 2), flip(cot_n, "expert", 2)

    def both_cores(tok, cot):
        return tok, flip(tok, "expert", 1), cot, flip(cot, "expert", 1)

    tok_n, cot_x = after((tok_n, cot_x), own[3])
    pairs = (both_cores(tok_x, cot_x), both_cores(tok_n, cot_n))
    gate_sum, down_sum, back_group = early_terms(
        group_count, place, own, pairs, gate_up, down_matrix
    )
    tok_d, cot_d = after((tok_d, cot_d), back_group)
    count = model_width // group_count
    first = max(count // 4, 16)
    cuts = (0, first, count // 2, count) if first < count // 2 else (0, first, count)
    hid_cols, scaled, *gate_pieces = last_terms(
        group_count,
        cuts,
        place,
        both_cores(tok_d, cot_d),
        gate_up,
        down_matrix,
        gate_sum,
        res_mine[1],
    )
    down_term = lax.dot_general(hid_cols, scaled, ROWS, preferred_element_type=jnp.float32)
    down_term = narrow(down_sum + down_term).reshape(high_count, 2, 2, -1, model_width)

    parts = len(cuts) - 1
    far_sent, far_kept = gate_pieces[:parts], gate_pieces[parts : 2 * parts]
    near_sent, near_kept = gate_pieces[2 * parts :]
    got = [flip(far_sent[0], "dp", 1)]
    got += [flip(after(piece, got[0]), "dp", 1) for piece in far_sent[1:]]
    crossed = [
        flip(narrow(wide(kept) + wide(piece)), "dp", 4) for kept, piece in zip(far_kept, got)
    ]

    def down_side(third, side):
        return take(take(down_term, 1, third), 1, side)

    res_send = narrow(wide(res_other[0]) + wide(res_other[1]))
    res_send = after(res_send, tok_d)
    res_sum = wide(res_mine[0]) + wide(res_mine[1]) + wide(flip(res_send, "dp", 2))
    down_sent = after(down_side(1 - bit2, 1 - bit0), got[1])
    got_down = flip(down_sent, "dp", 1)
    far_down = wide(down_side(1 - bit2, bit0)) + wide(got_down) + take(res_sum, 1, 1 - bit2)
    crossed_down = flip(narrow(far_down), "dp", 4)

    token_part = narrow(jnp.dot(back_group, gate_up.T, preferred_element_type=jnp.float32))
    blocks = token_part.reshape(expert_count, tok_rows, model_width)
    core = flip(jnp.stack([blocks[1], blocks[3]]), "expert", 1)
    across = flip(narrow(wide(blocks[2]) + wide(core[1])), "expert", 2)
    token_grad = narrow(wide(blocks[0]) + wide(core[0]) + wide(across))

    near_sent = after(near_sent, crossed[1])
    near_got = flip(near_sent, "dp", 1)
    down_sent = after(down_side(bit2, 1 - bit0), crossed[-1], across)
    near_down = wide(down_side(bit2, bit0)) + wide(flip(down_sent, "dp", 1))
    factor = 1.0 / group_count
    gate_sum = join(factor, near_kept, near_got, crossed, corners)
    down_sum = (near_down + take(res_sum, 1, bit2) + wide(crossed_down)) * factor
    bit = 8
    while bit < group_count:
        side = (group // bit) & 1
        halves = [v.reshape(-1, 2, *v.shape[1:]) for v in (gate_sum, down_sum)]
        gate_sum, down_sum = [
            take(v, 1, side) + wide(flip(narrow(take(v, 1, 1 - side)), "dp", bit)) for v in halves
        ]
        bit *= 2
    return (token_grad, gate_sum, down_sum)


def solution(mesh):
    placed = (
        P(("dp", "expert"), None),
        P(("dp", "expert"), None),
        P(("dp", "expert"), None),
        P(("dp", "expert"), None),
        P("expert", None, None),
        P("expert", None, None),
        P("dp", "expert", None, None),
    )
    return jax.shard_map(
        on_device,
        mesh=mesh,
        in_specs=placed,
        out_specs=(P(("dp", "expert"), None), P("expert", "dp", None), P("expert", "dp", None)),
        check_vma=False,
    )
```

```python
import functools

import jax
import jax.numpy as jnp
from jax import lax
from jax.experimental import pallas as pl
from jax.experimental.pallas import tpu as pltpu
from jax.sharding import PartitionSpec as P

LANES = 128


def wide(values):
    return values.astype(jnp.float32)


def narrow(values):
    return values.astype(jnp.bfloat16)


def flip(values, axis, bit):
    return lax.ppermute(values, axis, [(i, i ^ bit) for i in range(lax.axis_size(axis))])


def take(values, axis, index):
    return lax.dynamic_index_in_dim(values, index, axis, keepdims=False)


def with_routes(cotangent, expert_ids, gate_probs, expert_count):
    lane = jnp.arange(LANES, dtype=jnp.int32)[None, :]
    route = jnp.zeros((expert_ids.shape[0], LANES), jnp.float32)
    for k in range(expert_ids.shape[1]):
        hit = (lane < 3 * expert_count) & (lane // 3 == expert_ids[:, k : k + 1])
        route = route + jnp.where(hit, gate_probs[:, k : k + 1], 0.0)
    high = lax.reduce_precision(route, 8, 7)
    middle = lax.reduce_precision(route - high, 8, 7)
    low = (route - high) - middle
    part = lane % 3
    coded = jnp.where(part == 0, high, jnp.where(part == 1, middle, low))
    return jnp.concatenate([cotangent, narrow(coded)], axis=1)


def own_columns(values, group_count, parity):
    unit = values.shape[1] // group_count * 2
    blocks = [values[:, k * unit : (k + 1) * unit] for k in range(group_count // 2)]
    even, odd = jnp.concatenate(blocks[0::2], axis=1), jnp.concatenate(blocks[1::2], axis=1)
    return jnp.where(parity == 1, odd, even)


def expert_rows(place, group_count, ready, tok, cot, gate_up, down, scaled, back):
    width, units = gate_up.shape[0], down.shape[0]
    tile = units // 2
    lane = lax.broadcasted_iota(jnp.int32, (1, LANES), 1)
    coded = wide(cot[:, width:])
    part = [
        jnp.sum(jnp.where(lane == 3 * place[0] + k, coded, 0.0), axis=1, keepdims=True)
        for k in range(3)
    ]
    weight = (part[0] + part[1]) + part[2]
    scaled[...] = narrow(wide(cot[:, :width]) * weight)
    contract = (((1,), (1,)), ((), ()))
    hidden = []
    for k in range(2):
        lower, upper = slice(k * tile, (k + 1) * tile), slice(units + k * tile, units + (k + 1) * tile)
        ready(3 * k)
        gate = jnp.dot(tok[...], gate_up[:, lower], preferred_element_type=jnp.float32)
        ready(3 * k + 1)
        up = jnp.dot(tok[...], gate_up[:, upper], preferred_element_type=jnp.float32)
        sig = jax.nn.sigmoid(gate)
        activated = gate * sig
        hidden.append(narrow(activated * up))
        ready(3 * k + 2)
        back_hidden = lax.dot_general(
            scaled[...], down[lower, :], contract, preferred_element_type=jnp.float32
        )
        slope = up * sig * (1.0 + gate * (1.0 - sig))
        back[:, lower] = narrow(back_hidden * slope)
        back[:, upper] = narrow(back_hidden * activated)
    hid_cols = own_columns(jnp.concatenate(hidden, axis=1), group_count, place[1])
    return own_columns(tok[...], group_count, place[1]), hid_cols


ROWS = (((0,), (0,)), ((), ()))
FREE = pl.CostEstimate(flops=0, bytes_accessed=0, transcendentals=0)
HERE = pl.BlockSpec(memory_space=pl.ANY)
VMEM = pl.BlockSpec(memory_space=pltpu.VMEM)
SMEM = pl.BlockSpec(memory_space=pltpu.SMEM)


def hold(values, awaited):
    return pl.pallas_call(
        lambda *refs: None,
        out_shape=tuple(jax.ShapeDtypeStruct(v.shape, v.dtype) for v in values),
        in_specs=[HERE] * (len(values) + len(awaited)),
        out_specs=(HERE,) * len(values),
        input_output_aliases={k: k for k in range(len(values))},
        cost_estimate=FREE,
    )(*values, *awaited)


def weight_tiles(gate_up, down, gate_up_here, down_here):
    units = down.shape[0]
    tile = units // 2
    moves = []
    for k in range(2):
        for start in (k * tile, units + k * tile):
            here = (slice(None), slice(start, start + tile))
            moves.append((gate_up.at[here], gate_up_here.at[here]))
        here = (slice(k * tile, (k + 1) * tile), slice(None))
        moves.append((down.at[here], down_here.at[here]))
    return moves


def begin(moves, sems):
    copies = [pltpu.make_async_copy(src, dst, sems.at[k]) for k, (src, dst) in enumerate(moves)]
    for copy in copies:
        copy.start()
    return copies


def rows_in(pairs, tok_here, cot_here):
    moves, at = [], 0
    for tok_a, tok_b, cot_a, cot_b in pairs:
        for tok, cot in ((tok_a, cot_a), (tok_b, cot_b)):
            here = slice(at, at + tok.shape[0])
            moves += [(cot, cot_here.at[here, :]), (tok, tok_here.at[here, :])]
            at += tok.shape[0]
    return moves


def early_kernel(group_count, place, *refs):
    ins, (gate_sum, down_sum, back_group), scratch = refs[:14], refs[14:17], refs[17:]
    tok_here, cot_here, gate_up, down, scaled, back, sems = scratch
    rows = scaled.shape[0]
    arriving = rows_in([ins[4 * k : 4 * k + 4] for k in range(3)], tok_here, cot_here)
    tiles = weight_tiles(ins[12], ins[13], gate_up, down)
    copies = begin(arriving[:4] + tiles + arriving[4:], sems)
    pair_copies = [copies[:4], copies[10:14], copies[14:]]
    tile_copies = copies[4:10]
    for k in range(3):
        for copy in pair_copies[k]:
            copy.wait()
        here = slice(k * rows, (k + 1) * rows)
        back_here = back_group.at[here, :] if k < 2 else back
        tok_cols, hid_cols = expert_rows(
            place,
            group_count,
            (lambda i: tile_copies[i].wait()) if k == 0 else (lambda i: None),
            tok_here.at[here, :],
            cot_here.at[here, :],
            gate_up,
            down,
            scaled,
            back_here,
        )
        gate = lax.dot_general(tok_cols, back_here[...], ROWS, preferred_element_type=jnp.float32)
        down_part = lax.dot_general(hid_cols, scaled[...], ROWS, preferred_element_type=jnp.float32)
        gate_sum[...] = gate if k == 0 else gate_sum[...] + gate
        down_sum[...] = down_part if k == 0 else down_sum[...] + down_part


def early_terms(group_count, place, pairs, gate_up, down):
    rows, width = 2 * pairs[0][0].shape[0], pairs[0][0].shape[1]
    units, carried = down.shape[0], pairs[0][2].shape[1]
    shapes = [(3 * rows, width), (3 * rows, carried), gate_up.shape, down.shape]
    shapes += [(rows, width), (rows, 2 * units)]
    return pl.pallas_call(
        functools.partial(early_kernel, group_count),
        out_shape=(
            jax.ShapeDtypeStruct((width // 2, 2 * units), jnp.float32),
            jax.ShapeDtypeStruct((units // 2, width), jnp.float32),
            jax.ShapeDtypeStruct((2 * rows, 2 * units), jnp.bfloat16),
        ),
        in_specs=[SMEM] + [HERE] * 14,
        out_specs=(VMEM,) * 3,
        scratch_shapes=[pltpu.VMEM(shape, jnp.bfloat16) for shape in shapes]
        + [pltpu.SemaphoreType.DMA((18,))],
        compiler_params=pltpu.CompilerParams(vmem_limit_bytes=40 << 20),
        cost_estimate=FREE,
    )(place, *[v for pair in pairs for v in pair], gate_up, down)


def last_kernel(group_count, cuts, place, *refs):
    pair, (gate_up_in, down_in, gate_sum, hid_own, scaled) = refs[:4], refs[4:9]
    pieces, (tok_here, cot_here, gate_up, down, back, total, sems) = refs[9:-7], refs[-7:]
    arriving = rows_in([pair], tok_here, cot_here)
    tiles = weight_tiles(gate_up_in, down_in, gate_up, down)
    copies = begin(arriving + tiles + [(gate_sum, total)], sems)
    for copy in copies[:4]:
        copy.wait()
    tok_cols, hid_own[...] = expert_rows(
        place,
        group_count,
        lambda i: copies[4 + i].wait(),
        tok_here,
        cot_here,
        gate_up,
        down,
        scaled,
        back,
    )
    term = lax.dot_general(tok_cols, back[...], ROWS, preferred_element_type=jnp.float32)
    copies[10].wait()
    total[...] = total[...] + term
    bit0, bit2 = place[2], place[3]
    count = total.shape[0] // (group_count // 2)
    sides = ((1 - bit2, 1 - bit0), (1 - bit2, bit0), (bit2, 1 - bit0), (bit2, bit0))
    at = 0
    for (third, first), splits in zip(sides, (cuts, cuts, (0, count), (0, count))):
        for start, stop in zip(splits, splits[1:]):
            for high in range(group_count // 8):
                row = (high * 4 + third * 2 + first) * count + start
                row = pl.multiple_of(row, 8)
                pieces[at][high] = narrow(total[pl.ds(row, stop - start), :])
            at += 1


def last_terms(group_count, cuts, place, pair, gate_up, down, gate_sum):
    rows, width = 2 * pair[0].shape[0], pair[0].shape[1]
    units, high_count, count = down.shape[0], group_count // 8, cuts[-1]
    sizes = [b - a for a, b in zip(cuts, cuts[1:])] * 2 + [count] * 2
    shapes = [(rows, units // 2), (rows, width)]
    shapes += [(high_count, size, 2 * units) for size in sizes]
    inner = [(rows, width), (rows, pair[2].shape[1]), gate_up.shape, down.shape]
    inner += [(rows, 2 * units)]
    return pl.pallas_call(
        functools.partial(last_kernel, group_count, cuts),
        out_shape=tuple(jax.ShapeDtypeStruct(shape, jnp.bfloat16) for shape in shapes),
        in_specs=[SMEM] + [HERE] * 7,
        out_specs=(VMEM,) * len(shapes),
        scratch_shapes=[pltpu.VMEM(shape, jnp.bfloat16) for shape in inner]
        + [pltpu.VMEM(gate_sum.shape, jnp.float32), pltpu.SemaphoreType.DMA((11,))],
        compiler_params=pltpu.CompilerParams(vmem_limit_bytes=40 << 20),
        cost_estimate=FREE,
    )(place, *pair, gate_up, down, gate_sum)


def on_device(
    tokens, cotangent, expert_ids, gate_probs, gate_up_weight, down_weight, down_residual
):
    tok_rows, model_width = tokens.shape
    expert_count = lax.axis_size("expert")
    group_count = lax.axis_size("dp")
    gate_up, down_matrix = gate_up_weight[0], down_weight[0]
    hidden_units = down_matrix.shape[0]
    me, group = lax.axis_index("expert"), lax.axis_index("dp")
    bit0, bit1, bit2 = group & 1, (group >> 1) & 1, (group >> 2) & 1
    high_count = group_count // 8

    place = jnp.stack([me, bit1, bit0, bit2]).astype(jnp.int32)
    tok_x, tok_n = flip(tokens, "expert", 2), flip(tokens, "dp", 2)
    tok_c = flip(tokens, "expert", 1)
    carried = with_routes(cotangent, expert_ids, gate_probs, expert_count)
    cot_x, cot_n = flip(carried, "expert", 2), flip(carried, "dp", 2)
    cot_c = flip(carried, "expert", 1)
    residual = down_residual[0, 0].reshape(high_count, 2, 2, 2, -1, model_width)
    res_got = flip(take(residual, 3, 1 - bit0), "dp", 1)
    tok_x, tok_n, cot_x, cot_n, res_got = hold(
        (tok_x, tok_n, cot_x, cot_n, res_got), (tok_c, cot_c)
    )
    tok_d, cot_d = flip(tok_x, "dp", 2), flip(cot_n, "expert", 2)

    def both_cores(tok, cot):
        return tok, flip(tok, "expert", 1), cot, flip(cot, "expert", 1)

    pairs = ((tokens, tok_c, carried, cot_c), both_cores(tok_x, cot_x), both_cores(tok_n, cot_n))
    gate_sum, down_sum, back_group = early_terms(group_count, place, pairs, gate_up, down_matrix)
    res_pair = wide(take(residual, 3, bit0)) + wide(res_got)
    res_send = narrow(take(res_pair, 2, 1 - bit1))
    tok_d, cot_d, res_send = hold((tok_d, cot_d, res_send), (back_group,))
    count = model_width // group_count
    first = max(count // 4, 16)
    cuts = (0, first, count // 2, count) if first < count // 2 else (0, first, count)
    hid_cols, scaled, *gate_pieces = last_terms(
        group_count, cuts, place, both_cores(tok_d, cot_d), gate_up, down_matrix, gate_sum
    )
    down_term = lax.dot_general(hid_cols, scaled, ROWS, preferred_element_type=jnp.float32)
    down_term = narrow(down_sum + down_term).reshape(high_count, 2, 2, -1, model_width)

    parts = len(cuts) - 1
    far_sent, far_kept = gate_pieces[:parts], gate_pieces[parts : 2 * parts]
    near_sent, near_kept = gate_pieces[2 * parts :]
    got = [flip(piece, "dp", 1) for piece in far_sent]
    crossed = [
        flip(narrow(wide(kept) + wide(piece)), "dp", 4) for kept, piece in zip(far_kept, got)
    ]

    def down_side(third, side):
        return take(take(down_term, 1, third), 1, side)

    res_sum = take(res_pair, 2, bit1) + wide(flip(res_send, "dp", 2))
    down_sent = down_side(1 - bit2, 1 - bit0)
    got_down = flip(down_sent, "dp", 1)
    far_down = wide(down_side(1 - bit2, bit0)) + wide(got_down) + take(res_sum, 1, 1 - bit2)
    crossed_down = flip(narrow(far_down), "dp", 4)

    token_part = narrow(jnp.dot(back_group, gate_up.T, preferred_element_type=jnp.float32))
    blocks = token_part.reshape(expert_count, tok_rows, model_width)
    core = flip(jnp.stack([blocks[1], blocks[3]]), "expert", 1)
    across = flip(narrow(wide(blocks[2]) + wide(core[1])), "expert", 2)
    token_grad = narrow(wide(blocks[0]) + wide(core[0]) + wide(across))

    (near_sent,) = hold((near_sent,), (across,))
    near_gate = wide(near_kept) + wide(flip(near_sent, "dp", 1))
    down_sent = down_side(bit2, 1 - bit0)
    near_down = wide(down_side(bit2, bit0)) + wide(flip(down_sent, "dp", 1))
    factor = 1.0 / group_count
    gate_sum = (near_gate + wide(jnp.concatenate(crossed, axis=1))) * factor
    down_sum = (near_down + take(res_sum, 1, bit2) + wide(crossed_down)) * factor
    bit = 8
    while bit < group_count:
        side = (group // bit) & 1
        halves = [v.reshape(-1, 2, *v.shape[1:]) for v in (gate_sum, down_sum)]
        gate_sum, down_sum = [
            take(v, 1, side) + wide(flip(narrow(take(v, 1, 1 - side)), "dp", bit)) for v in halves
        ]
        bit *= 2
    return (token_grad, gate_sum, down_sum)


def solution(mesh):
    placed = (
        P(("dp", "expert"), None),
        P(("dp", "expert"), None),
        P(("dp", "expert"), None),
        P(("dp", "expert"), None),
        P("expert", None, None),
        P("expert", None, None),
        P("dp", "expert", None, None),
    )
    return jax.shard_map(
        on_device,
        mesh=mesh,
        in_specs=placed,
        out_specs=(P(("dp", "expert"), None), P("expert", "dp", None), P("expert", "dp", None)),
        check_vma=False,
    )
```

```python
import functools

import jax
import jax.numpy as jnp
from jax import lax
from jax.experimental import pallas as pl
from jax.experimental.pallas import tpu as pltpu
from jax.sharding import PartitionSpec as P

LANES = 128


def wide(values):
    return values.astype(jnp.float32)


def narrow(values):
    return values.astype(jnp.bfloat16)


def flip(values, axis, bit):
    return lax.ppermute(values, axis, [(i, i ^ bit) for i in range(lax.axis_size(axis))])


def take(values, axis, index):
    return lax.dynamic_index_in_dim(values, index, axis, keepdims=False)


def with_routes(cotangent, expert_ids, gate_probs, expert_count):
    lane = jnp.arange(LANES, dtype=jnp.int32)[None, :]
    route = jnp.zeros((expert_ids.shape[0], LANES), jnp.float32)
    for k in range(expert_ids.shape[1]):
        hit = (lane < 3 * expert_count) & (lane // 3 == expert_ids[:, k : k + 1])
        route = route + jnp.where(hit, gate_probs[:, k : k + 1], 0.0)
    high = lax.reduce_precision(route, 8, 7)
    middle = lax.reduce_precision(route - high, 8, 7)
    low = (route - high) - middle
    part = lane % 3
    coded = jnp.where(part == 0, high, jnp.where(part == 1, middle, low))
    return jnp.concatenate([cotangent, narrow(coded)], axis=1)


def own_columns(values, group_count, parity):
    unit = values.shape[1] // group_count * 2
    blocks = [values[:, k * unit : (k + 1) * unit] for k in range(group_count // 2)]
    even, odd = jnp.concatenate(blocks[0::2], axis=1), jnp.concatenate(blocks[1::2], axis=1)
    return jnp.where(parity == 1, odd, even)


def expert_kernel(
    group_count, place, tok_a, tok_b, cot_a, cot_b, gate_up, down, tok_own, hid_own, scaled, back
):
    width, units = gate_up.shape[0], down.shape[0]
    tile = units // 2
    me, parity = place[0], place[1]
    lane = lax.broadcasted_iota(jnp.int32, (1, LANES), 1)
    for cot, at in ((cot_a, 0), (cot_b, cot_a.shape[0])):
        coded = wide(cot[:, width:])
        part = [
            jnp.sum(jnp.where(lane == 3 * me + k, coded, 0.0), axis=1, keepdims=True)
            for k in range(3)
        ]
        weight = (part[0] + part[1]) + part[2]
        scaled[at : at + cot.shape[0], :] = narrow(wide(cot[:, :width]) * weight)
    rows = jnp.concatenate([tok_a[...], tok_b[...]], axis=0)
    tok_own[...] = own_columns(rows, group_count, parity)
    grads = scaled[...]
    contract = (((1,), (1,)), ((), ()))
    hidden = []
    for at in range(0, units, tile):
        gate = jnp.dot(rows, gate_up[:, at : at + tile], preferred_element_type=jnp.float32)
        up = jnp.dot(
            rows, gate_up[:, units + at : units + at + tile], preferred_element_type=jnp.float32
        )
        sig = jax.nn.sigmoid(gate)
        activated = gate * sig
        hidden.append(narrow(activated * up))
        back_hidden = lax.dot_general(
            grads, down[at : at + tile, :], contract, preferred_element_type=jnp.float32
        )
        slope = up * sig * (1.0 + gate * (1.0 - sig))
        back[:, at : at + tile] = narrow(back_hidden * slope)
        back[:, units + at : units + at + tile] = narrow(back_hidden * activated)
    hid_own[...] = own_columns(jnp.concatenate(hidden, axis=1), group_count, parity)


def expert_rows(group_count, place, tok_a, tok_b, cot_a, cot_b, gate_up, down):
    rows, width = 2 * tok_a.shape[0], tok_a.shape[1]
    units = down.shape[0]
    vmem = pl.BlockSpec(memory_space=pltpu.VMEM)
    widths = (width // 2, units // 2, width, 2 * units)
    return pl.pallas_call(
        functools.partial(expert_kernel, group_count),
        out_shape=tuple(jax.ShapeDtypeStruct((rows, w), jnp.bfloat16) for w in widths),
        in_specs=[pl.BlockSpec(memory_space=pltpu.SMEM)] + [vmem] * 6,
        out_specs=(vmem,) * 4,
        compiler_params=pltpu.CompilerParams(vmem_limit_bytes=24 << 20),
        cost_estimate=FREE,
    )(place, tok_a, tok_b, cot_a, cot_b, gate_up, down)


ROWS = (((0,), (0,)), ((), ()))
FREE = pl.CostEstimate(flops=0, bytes_accessed=0, transcendentals=0)


def hold(values, awaited):
    here = pl.BlockSpec(memory_space=pl.ANY)
    return pl.pallas_call(
        lambda *refs: None,
        out_shape=tuple(jax.ShapeDtypeStruct(v.shape, v.dtype) for v in values),
        in_specs=[here] * (len(values) + len(awaited)),
        out_specs=(here,) * len(values),
        input_output_aliases={k: k for k in range(len(values))},
        cost_estimate=FREE,
    )(*values, *awaited)


def terms_kernel(*refs):
    blocks, (gate_sum, down_sum) = refs[:-2], refs[-2:]
    for at in range(0, len(blocks), 4):
        tok_cols, hid_cols, scaled, back = [block[...] for block in blocks[at : at + 4]]
        gate = lax.dot_general(tok_cols, back, ROWS, preferred_element_type=jnp.float32)
        down = lax.dot_general(hid_cols, scaled, ROWS, preferred_element_type=jnp.float32)
        gate_sum[...] = gate if at == 0 else gate_sum[...] + gate
        down_sum[...] = down if at == 0 else down_sum[...] + down


def early_terms(made):
    tok_cols, hid_cols, scaled, back = made[0]
    vmem = pl.BlockSpec(memory_space=pltpu.VMEM)
    return pl.pallas_call(
        terms_kernel,
        out_shape=(
            jax.ShapeDtypeStruct((tok_cols.shape[1], back.shape[1]), jnp.float32),
            jax.ShapeDtypeStruct((hid_cols.shape[1], scaled.shape[1]), jnp.float32),
        ),
        in_specs=[vmem] * (4 * len(made)),
        out_specs=(vmem, vmem),
        compiler_params=pltpu.CompilerParams(vmem_limit_bytes=24 << 20),
        cost_estimate=FREE,
    )(*[v for block in made for v in block])


def on_device(
    tokens, cotangent, expert_ids, gate_probs, gate_up_weight, down_weight, down_residual
):
    tok_rows, model_width = tokens.shape
    expert_count = lax.axis_size("expert")
    group_count = lax.axis_size("dp")
    gate_up, down_matrix = gate_up_weight[0], down_weight[0]
    hidden_units = down_matrix.shape[0]
    me, group = lax.axis_index("expert"), lax.axis_index("dp")
    bit0, bit1, bit2 = group & 1, (group >> 1) & 1, (group >> 2) & 1
    high_count = group_count // 8

    tok_x, tok_n = flip(tokens, "expert", 2), flip(tokens, "dp", 2)
    tok_c = flip(tokens, "expert", 1)
    carried = with_routes(cotangent, expert_ids, gate_probs, expert_count)
    cot_x, cot_n = flip(carried, "expert", 2), flip(carried, "dp", 2)
    cot_c = flip(carried, "expert", 1)
    residual = down_residual[0, 0].reshape(high_count, 2, 2, 2, -1, model_width)
    res_got = flip(take(residual, 3, 1 - bit0), "dp", 1)
    place = jnp.stack([me, bit1]).astype(jnp.int32)

    def expert_on(tok, tok_other, cot, cot_other):
        return expert_rows(
            group_count, place, tok, tok_other, cot, cot_other, gate_up, down_matrix
        )

    def both_cores(tok, cot):
        return expert_on(tok, flip(tok, "expert", 1), cot, flip(cot, "expert", 1))

    tok_x, tok_n, cot_x, cot_n, res_got, place = hold(
        (tok_x, tok_n, cot_x, cot_n, res_got, place), (tok_c, cot_c)
    )
    tok_d, cot_d = flip(tok_x, "dp", 2), flip(cot_n, "expert", 2)
    made = [expert_on(tokens, tok_c, carried, cot_c)]
    made += [both_cores(tok_x, cot_x), both_cores(tok_n, cot_n)]
    gate_early, down_early = early_terms(made)
    tok_d, cot_d, *back_group = hold((tok_d, cot_d, made[0][3], made[1][3]), (gate_early,))

    def terms(tok_cols, hid_cols, scaled, back):
        gate = lax.dot_general(tok_cols, back, ROWS, preferred_element_type=jnp.float32)
        down = lax.dot_general(hid_cols, scaled, ROWS, preferred_element_type=jnp.float32)
        return gate, down

    gate_late, down_late = terms(*both_cores(tok_d, cot_d))
    gate_term = narrow(gate_early + gate_late).reshape(high_count, 2, 2, -1, 2 * hidden_units)
    down_term = narrow(down_early + down_late).reshape(high_count, 2, 2, -1, model_width)

    res_pair = wide(take(residual, 3, bit0)) + wide(res_got)
    res_send = narrow(take(res_pair, 2, 1 - bit1))
    res_send, _ = lax.optimization_barrier((res_send, gate_term))
    res_sum = take(res_pair, 2, bit1) + wide(flip(res_send, "dp", 2))

    def paired(term, side, after):
        mine = take(term, 1, side)
        sent, kept = take(mine, 1, 1 - bit0), take(mine, 1, bit0)
        if after is not None:
            sent, _ = lax.optimization_barrier((sent, after))
        got = flip(sent, "dp", 1)
        return wide(kept) + wide(got), got

    count = gate_term.shape[3]
    edges = [0, count // 4, count // 2, count]
    far = [
        paired(gate_term[:, :, :, start:stop], 1 - bit2, None)
        for start, stop in zip(edges, edges[1:])
    ]
    far_down, got_down = paired(down_term, 1 - bit2, far[1][1])
    far_down = far_down + take(res_sum, 1, 1 - bit2)
    crossed = [flip(narrow(piece), "dp", 4) for piece, _ in far]
    crossed_down = flip(narrow(far_down), "dp", 4)

    def input_part(start):
        rows = [back[start : start + tok_rows] for back in back_group]
        part = jnp.dot(jnp.concatenate(rows), gate_up.T, preferred_element_type=jnp.float32)
        return narrow(part)

    core = flip(input_part(tok_rows), "expert", 1)
    total = wide(input_part(0)) + wide(core)
    across = flip(narrow(total[tok_rows:]), "expert", 2)
    token_grad = narrow(total[:tok_rows] + wide(across))

    near_gate, _ = paired(gate_term, bit2, far[2][1])
    near_down, _ = paired(down_term, bit2, (got_down, token_grad))
    gate_sum = near_gate + wide(jnp.concatenate(crossed, axis=1))
    down_sum = near_down + take(res_sum, 1, bit2) + wide(crossed_down)
    bit = 8
    while bit < group_count:
        side = (group // bit) & 1
        halves = [v.reshape(-1, 2, *v.shape[1:]) for v in (gate_sum, down_sum)]
        gate_sum, down_sum = [
            take(v, 1, side) + wide(flip(narrow(take(v, 1, 1 - side)), "dp", bit)) for v in halves
        ]
        bit *= 2
    factor = 1.0 / group_count
    grad_gate_up, grad_down = gate_sum * factor, down_sum * factor
    return (token_grad, grad_gate_up, grad_down)


def solution(mesh):
    placed = (
        P(("dp", "expert"), None),
        P(("dp", "expert"), None),
        P(("dp", "expert"), None),
        P(("dp", "expert"), None),
        P("expert", None, None),
        P("expert", None, None),
        P("dp", "expert", None, None),
    )
    return jax.shard_map(
        on_device,
        mesh=mesh,
        in_specs=placed,
        out_specs=(P(("dp", "expert"), None), P("expert", "dp", None), P("expert", "dp", None)),
        check_vma=False,
    )
```

```python
import functools

import jax
import jax.numpy as jnp
from jax import lax
from jax.experimental import pallas as pl
from jax.experimental.pallas import tpu as pltpu
from jax.sharding import PartitionSpec as P

LANES = 128


def wide(values):
    return values.astype(jnp.float32)


def narrow(values):
    return values.astype(jnp.bfloat16)


def flip(values, axis, bit):
    return lax.ppermute(values, axis, [(i, i ^ bit) for i in range(lax.axis_size(axis))])


def take(values, axis, index):
    return lax.dynamic_index_in_dim(values, index, axis, keepdims=False)


def packed(tokens, cotangent, expert_ids, gate_probs, expert_count):
    lane = jnp.arange(LANES, dtype=jnp.int32)[None, :]
    route = jnp.zeros((expert_ids.shape[0], LANES), jnp.float32)
    for k in range(expert_ids.shape[1]):
        hit = (lane < 3 * expert_count) & (lane // 3 == expert_ids[:, k : k + 1])
        route = route + jnp.where(hit, gate_probs[:, k : k + 1], 0.0)
    high = lax.reduce_precision(route, 8, 7)
    middle = lax.reduce_precision(route - high, 8, 7)
    low = (route - high) - middle
    part = lane % 3
    coded = jnp.where(part == 0, high, jnp.where(part == 1, middle, low))
    return jnp.concatenate([tokens, cotangent, narrow(coded)], axis=1)


def own_columns(values, group_count, parity):
    unit = values.shape[1] // group_count * 2
    blocks = [values[:, k * unit : (k + 1) * unit] for k in range(group_count // 2)]
    even, odd = jnp.concatenate(blocks[0::2], axis=1), jnp.concatenate(blocks[1::2], axis=1)
    return jnp.where(parity == 1, odd, even)


def expert_kernel(group_count, place, *refs):
    blocks, (gate_up, down), made = refs[:-7], refs[-7:-5], refs[-5:]
    tok_own, hid_own, scaled, back_first, back_second = made
    width, units = gate_up.shape[0], down.shape[0]
    tile, split = units // 2, back_first.shape[0]
    me, parity = place[0], place[1]
    lane = lax.broadcasted_iota(jnp.int32, (1, LANES), 1)
    at = 0
    for block in blocks:
        coded = wide(block[:, 2 * width :])
        part = [
            jnp.sum(jnp.where(lane == 3 * me + k, coded, 0.0), axis=1, keepdims=True)
            for k in range(3)
        ]
        weight = (part[0] + part[1]) + part[2]
        here = slice(at, at + block.shape[0])
        scaled[here, :] = narrow(wide(block[:, width : 2 * width]) * weight)
        at += block.shape[0]
    rows = jnp.concatenate([block[:, :width] for block in blocks], axis=0)
    tok_own[...] = own_columns(rows, group_count, parity)
    grads = scaled[...]
    contract = (((1,), (1,)), ((), ()))
    hidden = []
    for at in range(0, units, tile):
        gate = jnp.dot(rows, gate_up[:, at : at + tile], preferred_element_type=jnp.float32)
        up = jnp.dot(
            rows, gate_up[:, units + at : units + at + tile], preferred_element_type=jnp.float32
        )
        sig = jax.nn.sigmoid(gate)
        activated = gate * sig
        hidden.append(narrow(activated * up))
        back_hidden = lax.dot_general(
            grads, down[at : at + tile, :], contract, preferred_element_type=jnp.float32
        )
        slope = up * sig * (1.0 + gate * (1.0 - sig))
        back_gate, back_up = narrow(back_hidden * slope), narrow(back_hidden * activated)
        for back, here in ((back_first, slice(0, split)), (back_second, slice(split, None))):
            back[:, at : at + tile] = back_gate[here]
            back[:, units + at : units + at + tile] = back_up[here]
    hid_own[...] = own_columns(jnp.concatenate(hidden, axis=1), group_count, parity)


def expert_rows(group_count, place, blocks, gate_up, down):
    rows, width = sum(block.shape[0] for block in blocks), gate_up.shape[0]
    units = down.shape[0]
    vmem = pl.BlockSpec(memory_space=pltpu.VMEM)
    shapes = [(rows, width // 2), (rows, units // 2), (rows, width)]
    shapes += [(rows // 2, 2 * units)] * 2
    return pl.pallas_call(
        functools.partial(expert_kernel, group_count),
        out_shape=tuple(jax.ShapeDtypeStruct(shape, jnp.bfloat16) for shape in shapes),
        in_specs=[pl.BlockSpec(memory_space=pltpu.SMEM)] + [vmem] * (len(blocks) + 2),
        out_specs=(vmem,) * 5,
        compiler_params=pltpu.CompilerParams(vmem_limit_bytes=24 << 20),
        cost_estimate=FREE,
    )(place, *blocks, gate_up, down)


ROWS = (((0,), (0,)), ((), ()))
FREE = pl.CostEstimate(flops=0, bytes_accessed=0, transcendentals=0)


def hold(values, awaited):
    here = pl.BlockSpec(memory_space=pl.ANY)
    return pl.pallas_call(
        lambda *refs: None,
        out_shape=tuple(jax.ShapeDtypeStruct(v.shape, v.dtype) for v in values),
        in_specs=[here] * (len(values) + len(awaited)),
        out_specs=(here,) * len(values),
        input_output_aliases={k: k for k in range(len(values))},
        cost_estimate=FREE,
    )(*values, *awaited)


def terms_kernel(*refs):
    blocks, (gate_sum, down_sum, sent, mark) = refs[:-4], refs[-4:]
    for k in range(len(blocks) // 5):
        tok_cols, hid_cols, scaled, *halves = [block[...] for block in blocks[5 * k : 5 * k + 5]]
        back = jnp.concatenate(halves, axis=0)
        gate = lax.dot_general(tok_cols, back, ROWS, preferred_element_type=jnp.float32)
        down = lax.dot_general(hid_cols, scaled, ROWS, preferred_element_type=jnp.float32)
        gate_sum[...] = gate if k == 0 else gate_sum[...] + gate
        down_sum[...] = down if k == 0 else down_sum[...] + down
        if k < 2:
            count = halves[1].shape[0]
            sent[k * count : (k + 1) * count, :] = halves[1]
    mark[...] = jnp.zeros_like(mark)


def early_terms(made):
    tok_cols, hid_cols, scaled, back, _ = made[0]
    vmem = pl.BlockSpec(memory_space=pltpu.VMEM)
    return pl.pallas_call(
        terms_kernel,
        out_shape=(
            jax.ShapeDtypeStruct((tok_cols.shape[1], back.shape[1]), jnp.float32),
            jax.ShapeDtypeStruct((hid_cols.shape[1], scaled.shape[1]), jnp.float32),
            jax.ShapeDtypeStruct((2 * back.shape[0], back.shape[1]), jnp.bfloat16),
            jax.ShapeDtypeStruct((8, LANES), jnp.float32),
        ),
        in_specs=[vmem] * (5 * len(made)),
        out_specs=(vmem,) * 4,
        compiler_params=pltpu.CompilerParams(vmem_limit_bytes=24 << 20),
        cost_estimate=FREE,
    )(*[v for block in made for v in block])


def on_device(
    tokens, cotangent, expert_ids, gate_probs, gate_up_weight, down_weight, down_residual
):
    tok_rows, model_width = tokens.shape
    expert_count = lax.axis_size("expert")
    group_count = lax.axis_size("dp")
    gate_up, down_matrix = gate_up_weight[0], down_weight[0]
    hidden_units = down_matrix.shape[0]
    me, group = lax.axis_index("expert"), lax.axis_index("dp")
    bit0, bit1, bit2 = group & 1, (group >> 1) & 1, (group >> 2) & 1
    high_count, half = group_count // 8, tok_rows // 2

    rows_own = packed(tokens, cotangent, expert_ids, gate_probs, expert_count)
    rows_c = flip(rows_own, "expert", 1)
    rows_x, rows_n = flip(rows_own, "expert", 2), flip(rows_own, "dp", 2)
    residual = down_residual[0, 0].reshape(high_count, 2, 2, 2, -1, model_width)
    res_got = flip(take(residual, 3, 1 - bit0), "dp", 1)
    place = jnp.stack([me, bit1]).astype(jnp.int32)

    def expert_on(*blocks):
        return expert_rows(group_count, place, blocks, gate_up, down_matrix)

    made = [expert_on(rows_own, rows_c)]
    rows_x, rows_n, res_got = hold((rows_x, rows_n, res_got), (made[0][1],))
    diagonal = [flip(rows_x[:half], "dp", 2), flip(rows_n[half:], "expert", 2)]
    made += [expert_on(rows, flip(rows, "expert", 1)) for rows in (rows_x, rows_n)]
    gate_early, down_early, back_sent, mark = early_terms(made)
    *diagonal, back_sent = hold((*diagonal, back_sent), (mark,))
    diagonal += [flip(rows, "expert", 1) for rows in diagonal]

    def terms(tok_cols, hid_cols, scaled, back):
        gate = lax.dot_general(tok_cols, back, ROWS, preferred_element_type=jnp.float32)
        down = lax.dot_general(hid_cols, scaled, ROWS, preferred_element_type=jnp.float32)
        return gate, down

    tok_late, hid_late, scaled_late, *back_late = expert_on(*diagonal)
    gate_late, down_late = terms(
        tok_late, hid_late, scaled_late, jnp.concatenate(back_late, axis=0)
    )
    gate_term = narrow(gate_early + gate_late).reshape(high_count, 2, 2, -1, 2 * hidden_units)
    down_term = narrow(down_early + down_late).reshape(high_count, 2, 2, -1, model_width)

    def side(term, third, first):
        return take(take(term, 1, third), 1, first)

    def pair_sum(kept, got):
        return wide(kept) + wide(got)

    count = gate_term.shape[3]
    first = max(count * 3 // 8, 16)
    edges = [0, first, count]
    far_sent, far_kept = [
        [side(gate_term[:, :, :, i:j], 1 - bit2, bit) for i, j in zip(edges, edges[1:])]
        for bit in (1 - bit0, bit0)
    ]
    far_got = [flip(piece, "dp", 1) for piece in far_sent]
    crossed = [
        flip(narrow(pair_sum(kept, got)), "dp", 4) for kept, got in zip(far_kept, far_got)
    ]
    res_pair = pair_sum(take(residual, 3, bit0), res_got)
    res_near = flip(narrow(take(res_pair, 2, 1 - bit1)), "dp", 2)
    res_near, near_sent = hold((res_near, side(gate_term, bit2, 1 - bit0)), (far_got[0],))
    res_sum = take(res_pair, 2, bit1) + wide(res_near)
    far_down = pair_sum(
        side(down_term, 1 - bit2, bit0), flip(side(down_term, 1 - bit2, 1 - bit0), "dp", 1)
    )
    crossed_down = flip(narrow(far_down + take(res_sum, 1, 1 - bit2)), "dp", 4)

    def input_part(back):
        return narrow(jnp.dot(back, gate_up.T, preferred_element_type=jnp.float32))

    core = flip(input_part(back_sent), "expert", 1)
    back_kept = jnp.concatenate([made[0][3], made[1][3]], axis=0)
    total = wide(input_part(back_kept)) + wide(core)
    across = flip(narrow(total[tok_rows:]), "expert", 2)
    token_grad = narrow(total[:tok_rows] + wide(across))

    near_gate = pair_sum(side(gate_term, bit2, bit0), flip(near_sent, "dp", 1))
    (near_sent,) = hold((side(down_term, bit2, 1 - bit0),), (across,))
    near_down = pair_sum(side(down_term, bit2, bit0), flip(near_sent, "dp", 1))
    gate_sum = near_gate + wide(jnp.concatenate(crossed, axis=1))
    down_sum = near_down + take(res_sum, 1, bit2) + wide(crossed_down)
    bit = 8
    while bit < group_count:
        mine = (group // bit) & 1
        halves = [v.reshape(-1, 2, *v.shape[1:]) for v in (gate_sum, down_sum)]
        gate_sum, down_sum = [
            take(v, 1, mine) + wide(flip(narrow(take(v, 1, 1 - mine)), "dp", bit)) for v in halves
        ]
        bit *= 2
    factor = 1.0 / group_count
    grad_gate_up, grad_down = gate_sum * factor, down_sum * factor
    return (token_grad, grad_gate_up, grad_down)


def solution(mesh):
    placed = (
        P(("dp", "expert"), None),
        P(("dp", "expert"), None),
        P(("dp", "expert"), None),
        P(("dp", "expert"), None),
        P("expert", None, None),
        P("expert", None, None),
        P("dp", "expert", None, None),
    )
    return jax.shard_map(
        on_device,
        mesh=mesh,
        in_specs=placed,
        out_specs=(P(("dp", "expert"), None), P("expert", "dp", None), P("expert", "dp", None)),
        check_vma=False,
    )
```

```python
import functools

import jax
import jax.numpy as jnp
from jax import lax
from jax.experimental import pallas as pl
from jax.experimental.pallas import tpu as pltpu
from jax.sharding import PartitionSpec as P

LANES = 128
FREE = pl.CostEstimate(flops=0, bytes_accessed=0, transcendentals=0)


def wide(values):
    return values.astype(jnp.float32)


def narrow(values):
    return values.astype(jnp.bfloat16)


def flip(values, axis, bit):
    return lax.ppermute(values, axis, [(i, i ^ bit) for i in range(lax.axis_size(axis))])


def take(values, axis, index):
    return lax.dynamic_index_in_dim(values, index, axis, keepdims=False)


def pack_kernel(expert_count, tokens, cotangent, ids, probs, packed, coded, sems):
    width = tokens.shape[1]
    moves = [(tokens, packed.at[:, :width]), (cotangent, packed.at[:, width : 2 * width])]
    copies = [pltpu.make_async_copy(src, dst, sems.at[k]) for k, (src, dst) in enumerate(moves)]
    for copy in copies:
        copy.start()
    line = lax.broadcasted_iota(jnp.int32, (LANES, tokens.shape[0]), 0)
    route = jnp.zeros(line.shape, jnp.float32)
    for k in range(ids.shape[0]):
        first = 3 * ids[k : k + 1, :]
        hit = (line >= first) & (line < first + 3)
        route = route + jnp.where(hit, probs[k : k + 1, :], 0.0)
    high = wide(narrow(route))
    middle = wide(narrow(route - high))
    low = (route - high) - middle
    part = lax.rem(line, 3)
    lines = jnp.where(part == 0, high, jnp.where(part == 1, middle, low))
    coded[...] = narrow(lines.T)
    last = pltpu.make_async_copy(coded, packed.at[:, 2 * width :], sems.at[2])
    last.start()
    for copy in (*copies, last):
        copy.wait()


def packed(tokens, cotangent, expert_ids, gate_probs, expert_count):
    rows, width = tokens.shape
    here, vmem = pl.BlockSpec(memory_space=pl.ANY), pl.BlockSpec(memory_space=pltpu.VMEM)
    return pl.pallas_call(
        functools.partial(pack_kernel, expert_count),
        out_shape=jax.ShapeDtypeStruct((rows, 2 * width + LANES), jnp.bfloat16),
        in_specs=[here, here, vmem, vmem],
        out_specs=here,
        scratch_shapes=[pltpu.VMEM((rows, LANES), jnp.bfloat16), pltpu.SemaphoreType.DMA((3,))],
        compiler_params=pltpu.CompilerParams(vmem_limit_bytes=4 << 20),
        cost_estimate=FREE,
    )(tokens, cotangent, expert_ids.T, gate_probs.T)


def own_columns(values, group_count, parity):
    unit = values.shape[1] // group_count * 2
    blocks = [values[:, k * unit : (k + 1) * unit] for k in range(group_count // 2)]
    even, odd = jnp.concatenate(blocks[0::2], axis=1), jnp.concatenate(blocks[1::2], axis=1)
    return jnp.where(parity == 1, odd, even)


def expert_kernel(group_count, place, *refs):
    blocks, (gate_up, down), made = refs[:-7], refs[-7:-5], refs[-5:]
    tok_own, hid_own, scaled, back_first, back_second = made
    width, units = gate_up.shape[0], down.shape[0]
    tile, split = units // 2, back_first.shape[0]
    me, parity = place[0], place[1]
    lane = lax.broadcasted_iota(jnp.int32, (1, LANES), 1)
    at = 0
    for block in blocks:
        coded = wide(block[:, 2 * width :])
        part = [
            jnp.sum(jnp.where(lane == 3 * me + k, coded, 0.0), axis=1, keepdims=True)
            for k in range(3)
        ]
        weight = (part[0] + part[1]) + part[2]
        here = slice(at, at + block.shape[0])
        scaled[here, :] = narrow(wide(block[:, width : 2 * width]) * weight)
        at += block.shape[0]
    rows = jnp.concatenate([block[:, :width] for block in blocks], axis=0)
    tok_own[...] = own_columns(rows, group_count, parity)
    grads = scaled[...]
    contract = (((1,), (1,)), ((), ()))
    hidden = []
    for at in range(0, units, tile):
        gate = jnp.dot(rows, gate_up[:, at : at + tile], preferred_element_type=jnp.float32)
        up = jnp.dot(
            rows, gate_up[:, units + at : units + at + tile], preferred_element_type=jnp.float32
        )
        sig = jax.nn.sigmoid(gate)
        activated = gate * sig
        hidden.append(narrow(activated * up))
        back_hidden = lax.dot_general(
            grads, down[at : at + tile, :], contract, preferred_element_type=jnp.float32
        )
        slope = up * sig * (1.0 + gate * (1.0 - sig))
        back_gate, back_up = narrow(back_hidden * slope), narrow(back_hidden * activated)
        for back, here in ((back_first, slice(0, split)), (back_second, slice(split, None))):
            back[:, at : at + tile] = back_gate[here]
            back[:, units + at : units + at + tile] = back_up[here]
    hid_own[...] = own_columns(jnp.concatenate(hidden, axis=1), group_count, parity)


def expert_rows(group_count, place, blocks, gate_up, down):
    rows, width = sum(block.shape[0] for block in blocks), gate_up.shape[0]
    units = down.shape[0]
    vmem = pl.BlockSpec(memory_space=pltpu.VMEM)
    shapes = [(rows, width // 2), (rows, units // 2), (rows, width)]
    shapes += [(rows // 2, 2 * units)] * 2
    return pl.pallas_call(
        functools.partial(expert_kernel, group_count),
        out_shape=tuple(jax.ShapeDtypeStruct(shape, jnp.bfloat16) for shape in shapes),
        in_specs=[pl.BlockSpec(memory_space=pltpu.SMEM)] + [vmem] * (len(blocks) + 2),
        out_specs=(vmem,) * 5,
        compiler_params=pltpu.CompilerParams(vmem_limit_bytes=24 << 20),
        cost_estimate=FREE,
    )(place, *blocks, gate_up, down)


ROWS = (((0,), (0,)), ((), ()))


def hold(values, awaited):
    here = pl.BlockSpec(memory_space=pl.ANY)
    return pl.pallas_call(
        lambda *refs: None,
        out_shape=tuple(jax.ShapeDtypeStruct(v.shape, v.dtype) for v in values),
        in_specs=[here] * (len(values) + len(awaited)),
        out_specs=(here,) * len(values),
        input_output_aliases={k: k for k in range(len(values))},
        compiler_params=pltpu.CompilerParams(vmem_limit_bytes=1 << 20),
        cost_estimate=FREE,
    )(*values, *awaited)


def terms_kernel(*refs):
    blocks, (gate_sum, down_sum, sent, mark) = refs[:-4], refs[-4:]
    for k in range(len(blocks) // 5):
        tok_cols, hid_cols, scaled, *halves = [block[...] for block in blocks[5 * k : 5 * k + 5]]
        back = jnp.concatenate(halves, axis=0)
        gate = lax.dot_general(tok_cols, back, ROWS, preferred_element_type=jnp.float32)
        down = lax.dot_general(hid_cols, scaled, ROWS, preferred_element_type=jnp.float32)
        gate_sum[...] = gate if k == 0 else gate_sum[...] + gate
        down_sum[...] = down if k == 0 else down_sum[...] + down
        if k < 2:
            count = halves[1].shape[0]
            sent[k * count : (k + 1) * count, :] = halves[1]
    mark[...] = jnp.zeros_like(mark)


def early_terms(made):
    tok_cols, hid_cols, scaled, back, _ = made[0]
    vmem = pl.BlockSpec(memory_space=pltpu.VMEM)
    return pl.pallas_call(
        terms_kernel,
        out_shape=(
            jax.ShapeDtypeStruct((tok_cols.shape[1], back.shape[1]), jnp.float32),
            jax.ShapeDtypeStruct((hid_cols.shape[1], scaled.shape[1]), jnp.float32),
            jax.ShapeDtypeStruct((2 * back.shape[0], back.shape[1]), jnp.bfloat16),
            jax.ShapeDtypeStruct((8, LANES), jnp.float32),
        ),
        in_specs=[vmem] * (5 * len(made)),
        out_specs=(vmem,) * 4,
        compiler_params=pltpu.CompilerParams(vmem_limit_bytes=24 << 20),
        cost_estimate=FREE,
    )(*[v for block in made for v in block])


def on_device(
    tokens, cotangent, expert_ids, gate_probs, gate_up_weight, down_weight, down_residual
):
    tok_rows, model_width = tokens.shape
    expert_count = lax.axis_size("expert")
    group_count = lax.axis_size("dp")
    gate_up, down_matrix = gate_up_weight[0], down_weight[0]
    hidden_units = down_matrix.shape[0]
    me, group = lax.axis_index("expert"), lax.axis_index("dp")
    bit0, bit1, bit2 = group & 1, (group >> 1) & 1, (group >> 2) & 1
    high_count, half = group_count // 8, tok_rows // 2

    rows_own = packed(tokens, cotangent, expert_ids, gate_probs, expert_count)
    rows_c = flip(rows_own, "expert", 1)
    rows_x, rows_n = flip(rows_own, "expert", 2), flip(rows_own, "dp", 2)
    residual = down_residual[0, 0].reshape(high_count, 2, 2, 2, -1, model_width)


    def residual_side(parity, first):
        return take(take(residual, 2, parity), 2, first)

    res_other = flip(residual_side(1 - bit1, 1 - bit0), "dp", 1)
    res_mine = residual_side(bit1, 1 - bit0)
    place = jnp.stack([me, bit1]).astype(jnp.int32)

    def expert_on(*blocks):
        return expert_rows(group_count, place, blocks, gate_up, down_matrix)

    made = [expert_on(rows_own, rows_c)]
    rows_x, rows_n, res_other, res_mine = hold(
        (rows_x, rows_n, res_other, res_mine), (made[0][1],)
    )
    diagonal = [flip(rows_x[:half], "dp", 2), flip(rows_n[half:], "expert", 2)]
    made += [expert_on(rows, flip(rows, "expert", 1)) for rows in (rows_x, rows_n)]
    res_mine = flip(res_mine, "dp", 1)
    gate_early, down_early, back_sent, mark = early_terms(made)
    *diagonal, back_sent, res_other, res_mine = hold(
        (*diagonal, back_sent, res_other, res_mine), (mark,)
    )
    diagonal += [flip(rows, "expert", 1) for rows in diagonal]

    def terms(tok_cols, hid_cols, scaled, back):
        gate = lax.dot_general(tok_cols, back, ROWS, preferred_element_type=jnp.float32)
        down = lax.dot_general(hid_cols, scaled, ROWS, preferred_element_type=jnp.float32)
        return gate, down

    tok_late, hid_late, scaled_late, *back_late = expert_on(*diagonal)
    gate_late, down_late = terms(
        tok_late, hid_late, scaled_late, jnp.concatenate(back_late, axis=0)
    )
    gate_term = narrow(gate_early + gate_late).reshape(high_count, 2, 2, -1, 2 * hidden_units)
    down_term = narrow(down_early + down_late).reshape(high_count, 2, 2, -1, model_width)

    def side(term, third, first):
        return take(take(term, 1, third), 1, first)

    def pair_sum(kept, got):
        return wide(kept) + wide(got)

    count = gate_term.shape[3]
    first = max(count * 3 // 8, 16)
    edges = [0, first, count]
    far_sent, far_kept = [
        [side(gate_term[:, :, :, i:j], 1 - bit2, bit) for i, j in zip(edges, edges[1:])]
        for bit in (1 - bit0, bit0)
    ]
    far_got = [flip(piece, "dp", 1) for piece in far_sent]
    crossed = [
        flip(narrow(pair_sum(kept, got)), "dp", 4) for kept, got in zip(far_kept, far_got)
    ]
    res_near = flip(narrow(pair_sum(residual_side(1 - bit1, bit0), res_other)), "dp", 2)
    res_near, down_sent = hold(
        (res_near, side(down_term, 1 - bit2, 1 - bit0)), (far_got[0],)
    )
    (near_sent,) = hold((side(gate_term, bit2, 1 - bit0),), (far_got[1],))
    res_sum = pair_sum(residual_side(bit1, bit0), res_mine) + wide(res_near)
    far_down = pair_sum(side(down_term, 1 - bit2, bit0), flip(down_sent, "dp", 1))
    crossed_down = flip(narrow(far_down + take(res_sum, 1, 1 - bit2)), "dp", 4)

    def input_part(back):
        return narrow(jnp.dot(back, gate_up.T, preferred_element_type=jnp.float32))

    core = flip(input_part(back_sent), "expert", 1)
    back_kept = jnp.concatenate([made[0][3], made[1][3]], axis=0)
    total = wide(input_part(back_kept)) + wide(core)
    across = flip(narrow(total[tok_rows:]), "expert", 2)
    token_grad = narrow(total[:tok_rows] + wide(across))

    near_gate = pair_sum(side(gate_term, bit2, bit0), flip(near_sent, "dp", 1))
    (near_sent,) = hold((side(down_term, bit2, 1 - bit0),), (across,))
    near_down = pair_sum(side(down_term, bit2, bit0), flip(near_sent, "dp", 1))
    gate_sum = near_gate + wide(jnp.concatenate(crossed, axis=1))
    down_sum = near_down + take(res_sum, 1, bit2) + wide(crossed_down)
    bit = 8
    while bit < group_count:
        mine = (group // bit) & 1
        halves = [v.reshape(-1, 2, *v.shape[1:]) for v in (gate_sum, down_sum)]
        gate_sum, down_sum = [
            take(v, 1, mine) + wide(flip(narrow(take(v, 1, 1 - mine)), "dp", bit)) for v in halves
        ]
        bit *= 2
    factor = 1.0 / group_count
    grad_gate_up, grad_down = gate_sum * factor, down_sum * factor
    return (token_grad, grad_gate_up, grad_down)


def solution(mesh):
    placed = (
        P(("dp", "expert"), None),
        P(("dp", "expert"), None),
        P(("dp", "expert"), None),
        P(("dp", "expert"), None),
        P("expert", None, None),
        P("expert", None, None),
        P("dp", "expert", None, None),
    )
    return jax.shard_map(
        on_device,
        mesh=mesh,
        in_specs=placed,
        out_specs=(P(("dp", "expert"), None), P("expert", "dp", None), P("expert", "dp", None)),
        check_vma=False,
    )
```

```python
import functools

import jax
import jax.numpy as jnp
from jax import lax
from jax.experimental import pallas as pl
from jax.experimental.pallas import tpu as pltpu
from jax.sharding import PartitionSpec as P

LANES = 128
HERE = pl.BlockSpec(memory_space=pl.ANY)
FREE = pl.CostEstimate(flops=0, bytes_accessed=0, transcendentals=0)


def wide(values):
    return values.astype(jnp.float32)


def narrow(values):
    return values.astype(jnp.bfloat16)


def flip(values, axis, bit):
    return lax.ppermute(values, axis, [(i, i ^ bit) for i in range(lax.axis_size(axis))])


def take(values, axis, index):
    return lax.dynamic_index_in_dim(values, index, axis, keepdims=False)


def begin(moves, sems):
    copies = [pltpu.make_async_copy(src, dst, sems.at[k]) for k, (src, dst) in enumerate(moves)]
    for copy in copies:
        copy.start()
    return copies


def pack_kernel(tokens, cotangent, ids_in, probs_in, packed, coded, ids, probs, sems):
    width = tokens.shape[1]
    small = begin([(ids_in, ids), (probs_in, probs)], sems)
    moves = [(tokens, packed.at[:, :width]), (cotangent, packed.at[:, width : 2 * width])]
    large = begin(moves, sems.at[2:4])
    for copy in small:
        copy.wait()
    line = lax.broadcasted_iota(jnp.int32, (LANES, tokens.shape[0]), 0)
    route = jnp.zeros(line.shape, jnp.float32)
    for k in range(ids.shape[0]):
        first = 3 * ids[k : k + 1, :]
        hit = (line >= first) & (line < first + 3)
        route = route + jnp.where(hit, probs[k : k + 1, :], 0.0)
    high = wide(narrow(route))
    middle = wide(narrow(route - high))
    low = (route - high) - middle
    part = lax.rem(line, 3)
    lines = jnp.where(part == 0, high, jnp.where(part == 1, middle, low))
    coded[...] = narrow(lines.T)
    last = begin([(coded, packed.at[:, 2 * width :])], sems.at[4:5])
    for copy in (*large, *last):
        copy.wait()


def packed(tokens, cotangent, expert_ids, gate_probs):
    rows, width = tokens.shape
    top = expert_ids.shape[1]
    return pl.pallas_call(
        pack_kernel,
        out_shape=jax.ShapeDtypeStruct((rows, 2 * width + LANES), jnp.bfloat16),
        in_specs=[HERE] * 4,
        out_specs=HERE,
        scratch_shapes=[
            pltpu.VMEM((rows, LANES), jnp.bfloat16),
            pltpu.VMEM((top, rows), jnp.int32),
            pltpu.VMEM((top, rows), jnp.float32),
            pltpu.SemaphoreType.DMA((5,)),
        ],
        compiler_params=pltpu.CompilerParams(vmem_limit_bytes=48 << 20),
        cost_estimate=FREE,
    )(tokens, cotangent, expert_ids.T, gate_probs.T)


def own_columns(values, group_count, parity):
    unit = values.shape[1] // group_count * 2
    blocks = [values[:, k * unit : (k + 1) * unit] for k in range(group_count // 2)]
    even, odd = jnp.concatenate(blocks[0::2], axis=1), jnp.concatenate(blocks[1::2], axis=1)
    return jnp.where(parity == 1, odd, even)


def expert_kernel(group_count, place, *refs):
    blocks, (gate_up, down), made = refs[:-7], refs[-7:-5], refs[-5:]
    tok_own, hid_own, scaled, back_first, back_second = made
    width, units = gate_up.shape[0], down.shape[0]
    tile, split = units // 2, back_first.shape[0]
    me, parity = place[0], place[1]
    lane = lax.broadcasted_iota(jnp.int32, (1, LANES), 1)
    at = 0
    for block in blocks:
        coded = wide(block[:, 2 * width :])
        part = [
            jnp.sum(jnp.where(lane == 3 * me + k, coded, 0.0), axis=1, keepdims=True)
            for k in range(3)
        ]
        weight = (part[0] + part[1]) + part[2]
        here = slice(at, at + block.shape[0])
        scaled[here, :] = narrow(wide(block[:, width : 2 * width]) * weight)
        at += block.shape[0]
    rows = jnp.concatenate([block[:, :width] for block in blocks], axis=0)
    tok_own[...] = own_columns(rows, group_count, parity)
    grads = scaled[...]
    contract = (((1,), (1,)), ((), ()))
    hidden = []
    for at in range(0, units, tile):
        gate = jnp.dot(rows, gate_up[:, at : at + tile], preferred_element_type=jnp.float32)
        up = jnp.dot(
            rows, gate_up[:, units + at : units + at + tile], preferred_element_type=jnp.float32
        )
        sig = jax.nn.sigmoid(gate)
        activated = gate * sig
        hidden.append(narrow(activated * up))
        back_hidden = lax.dot_general(
            grads, down[at : at + tile, :], contract, preferred_element_type=jnp.float32
        )
        slope = up * sig * (1.0 + gate * (1.0 - sig))
        back_gate, back_up = narrow(back_hidden * slope), narrow(back_hidden * activated)
        for back, here in ((back_first, slice(0, split)), (back_second, slice(split, None))):
            back[:, at : at + tile] = back_gate[here]
            back[:, units + at : units + at + tile] = back_up[here]
    hid_own[...] = own_columns(jnp.concatenate(hidden, axis=1), group_count, parity)


def expert_rows(group_count, place, blocks, gate_up, down):
    rows, width = sum(block.shape[0] for block in blocks), gate_up.shape[0]
    units = down.shape[0]
    vmem = pl.BlockSpec(memory_space=pltpu.VMEM)
    shapes = [(rows, width // 2), (rows, units // 2), (rows, width)]
    shapes += [(rows // 2, 2 * units)] * 2
    return pl.pallas_call(
        functools.partial(expert_kernel, group_count),
        out_shape=tuple(jax.ShapeDtypeStruct(shape, jnp.bfloat16) for shape in shapes),
        in_specs=[pl.BlockSpec(memory_space=pltpu.SMEM)] + [vmem] * (len(blocks) + 2),
        out_specs=(vmem,) * 5,
        compiler_params=pltpu.CompilerParams(vmem_limit_bytes=18 << 20),
        cost_estimate=FREE,
    )(place, *blocks, gate_up, down)


ROWS = (((0,), (0,)), ((), ()))


def hold_kernel(cuts, count, *refs):
    values, cut_refs, sems = refs[:count], refs[-1 - len(cuts) : -1], refs[-1]
    moves = [(values[k].at[rows, :], cut) for (k, rows), cut in zip(cuts, cut_refs)]
    for copy in begin(moves, sems):
        copy.wait()


def hold(values, awaited, cuts=()):
    like = [jax.ShapeDtypeStruct(v.shape, v.dtype) for v in values]
    for k, rows in cuts:
        shape = (rows.stop - rows.start, *values[k].shape[1:])
        like.append(jax.ShapeDtypeStruct(shape, values[k].dtype))
    return pl.pallas_call(
        functools.partial(hold_kernel, cuts, len(values)),
        out_shape=tuple(like),
        in_specs=[HERE] * (len(values) + len(awaited)),
        out_specs=(HERE,) * len(like),
        input_output_aliases={k: k for k in range(len(values))},
        scratch_shapes=[pltpu.SemaphoreType.DMA((max(len(cuts), 1),))],
        compiler_params=pltpu.CompilerParams(vmem_limit_bytes=1 << 20),
        cost_estimate=FREE,
    )(*values, *awaited)


def terms_kernel(*refs):
    blocks, (gate_sum, down_sum, sent, mark) = refs[:-4], refs[-4:]
    for k in range(len(blocks) // 5):
        tok_cols, hid_cols, scaled, *halves = [block[...] for block in blocks[5 * k : 5 * k + 5]]
        back = jnp.concatenate(halves, axis=0)
        gate = lax.dot_general(tok_cols, back, ROWS, preferred_element_type=jnp.float32)
        down = lax.dot_general(hid_cols, scaled, ROWS, preferred_element_type=jnp.float32)
        gate_sum[...] = gate if k == 0 else gate_sum[...] + gate
        down_sum[...] = down if k == 0 else down_sum[...] + down
        if k < 2:
            count = halves[1].shape[0]
            sent[k * count : (k + 1) * count, :] = halves[1]
    mark[...] = jnp.zeros_like(mark)


def early_terms(made):
    tok_cols, hid_cols, scaled, back, _ = made[0]
    vmem = pl.BlockSpec(memory_space=pltpu.VMEM)
    return pl.pallas_call(
        terms_kernel,
        out_shape=(
            jax.ShapeDtypeStruct((tok_cols.shape[1], back.shape[1]), jnp.float32),
            jax.ShapeDtypeStruct((hid_cols.shape[1], scaled.shape[1]), jnp.float32),
            jax.ShapeDtypeStruct((2 * back.shape[0], back.shape[1]), jnp.bfloat16),
            jax.ShapeDtypeStruct((8, LANES), jnp.float32),
        ),
        in_specs=[vmem] * (5 * len(made)),
        out_specs=(vmem,) * 4,
        compiler_params=pltpu.CompilerParams(vmem_limit_bytes=24 << 20),
        cost_estimate=FREE,
    )(*[v for block in made for v in block])


def on_device(
    tokens, cotangent, expert_ids, gate_probs, gate_up_weight, down_weight, down_residual
):
    tok_rows, model_width = tokens.shape
    expert_count = lax.axis_size("expert")
    group_count = lax.axis_size("dp")
    gate_up, down_matrix = gate_up_weight[0], down_weight[0]
    hidden_units = down_matrix.shape[0]
    me, group = lax.axis_index("expert"), lax.axis_index("dp")
    bit0, bit1, bit2 = group & 1, (group >> 1) & 1, (group >> 2) & 1
    high_count, half = group_count // 8, tok_rows // 2

    rows_own = packed(tokens, cotangent, expert_ids, gate_probs)
    rows_c = flip(rows_own, "expert", 1)
    rows_x, rows_n = flip(rows_own, "expert", 2), flip(rows_own, "dp", 2)
    residual = down_residual[0, 0].reshape(high_count, 2, 2, 2, -1, model_width)


    def pair_sum(kept, got):
        return wide(kept) + wide(got)

    def residual_side(parity, first):
        return take(take(residual, 2, parity), 2, first)

    res_other = flip(residual_side(1 - bit1, 1 - bit0), "dp", 1)
    res_mine = residual_side(bit1, 1 - bit0)
    place = jnp.stack([me, bit1]).astype(jnp.int32)

    def expert_on(*blocks):
        return expert_rows(group_count, place, blocks, gate_up, down_matrix)

    made = [expert_on(rows_own, rows_c)]
    res_send = narrow(pair_sum(residual_side(1 - bit1, bit0), res_other))
    rows_x, rows_n, res_send, res_mine, cut_x, cut_n = hold(
        (rows_x, rows_n, res_send, res_mine),
        (made[0][1],),
        ((0, slice(0, half)), (1, slice(half, tok_rows))),
    )
    diagonal = [flip(cut_x, "dp", 2), flip(cut_n, "expert", 2)]
    made += [expert_on(rows, flip(rows, "expert", 1)) for rows in (rows_x, rows_n)]
    res_mine = flip(res_mine, "dp", 1)
    gate_early, down_early, back_sent, mark = early_terms(made)
    *diagonal, back_sent, res_send, res_mine = hold(
        (*diagonal, back_sent, res_send, res_mine), (mark,)
    )
    diagonal += [flip(rows, "expert", 1) for rows in diagonal]

    def terms(tok_cols, hid_cols, scaled, back):
        gate = lax.dot_general(tok_cols, back, ROWS, preferred_element_type=jnp.float32)
        down = lax.dot_general(hid_cols, scaled, ROWS, preferred_element_type=jnp.float32)
        return gate, down

    tok_late, hid_late, scaled_late, *back_late = expert_on(*diagonal)
    gate_late, down_late = terms(
        tok_late, hid_late, scaled_late, jnp.concatenate(back_late, axis=0)
    )
    gate_term = narrow(gate_early + gate_late).reshape(high_count, 2, 2, -1, 2 * hidden_units)
    down_term = narrow(down_early + down_late).reshape(high_count, 2, 2, -1, model_width)

    def side(term, third, first):
        return take(take(term, 1, third), 1, first)

    count = gate_term.shape[3]
    first = max(count * 3 // 8, 16)
    edges = [0, first, count]
    far_sent, far_kept = [
        [side(gate_term[:, :, :, i:j], 1 - bit2, bit) for i, j in zip(edges, edges[1:])]
        for bit in (1 - bit0, bit0)
    ]
    far_got = [flip(piece, "dp", 1) for piece in far_sent]
    crossed = [
        flip(narrow(pair_sum(kept, got)), "dp", 4) for kept, got in zip(far_kept, far_got)
    ]
    res_near = flip(res_send, "dp", 2)
    res_near, down_sent = hold(
        (res_near, side(down_term, 1 - bit2, 1 - bit0)), (far_got[0],)
    )
    (near_sent,) = hold((side(gate_term, bit2, 1 - bit0),), (far_got[1],))
    res_sum = pair_sum(residual_side(bit1, bit0), res_mine) + wide(res_near)
    far_down = pair_sum(side(down_term, 1 - bit2, bit0), flip(down_sent, "dp", 1))
    crossed_down = flip(narrow(far_down + take(res_sum, 1, 1 - bit2)), "dp", 4)

    def input_part(back):
        return narrow(jnp.dot(back, gate_up.T, preferred_element_type=jnp.float32))

    core = flip(input_part(back_sent), "expert", 1)
    back_kept = jnp.concatenate([made[0][3], made[1][3]], axis=0)
    total = wide(input_part(back_kept)) + wide(core)
    across = flip(narrow(total[tok_rows:]), "expert", 2)
    token_grad = narrow(total[:tok_rows] + wide(across))

    near_gate = pair_sum(side(gate_term, bit2, bit0), flip(near_sent, "dp", 1))
    (near_sent,) = hold((side(down_term, bit2, 1 - bit0),), (across,))
    near_down = pair_sum(side(down_term, bit2, bit0), flip(near_sent, "dp", 1))
    crossed[-1] = hold((crossed[-1],), (near_sent,))[0]
    gate_sum = near_gate + wide(jnp.concatenate(crossed, axis=1))
    down_sum = near_down + take(res_sum, 1, bit2) + wide(crossed_down)
    bit = 8
    while bit < group_count:
        mine = (group // bit) & 1
        halves = [v.reshape(-1, 2, *v.shape[1:]) for v in (gate_sum, down_sum)]
        gate_sum, down_sum = [
            take(v, 1, mine) + wide(flip(narrow(take(v, 1, 1 - mine)), "dp", bit)) for v in halves
        ]
        bit *= 2
    factor = 1.0 / group_count
    grad_gate_up, grad_down = gate_sum * factor, down_sum * factor
    return (token_grad, grad_gate_up, grad_down)


def solution(mesh):
    placed = (
        P(("dp", "expert"), None),
        P(("dp", "expert"), None),
        P(("dp", "expert"), None),
        P(("dp", "expert"), None),
        P("expert", None, None),
        P("expert", None, None),
        P("dp", "expert", None, None),
    )
    return jax.shard_map(
        on_device,
        mesh=mesh,
        in_specs=placed,
        out_specs=(P(("dp", "expert"), None), P("expert", "dp", None), P("expert", "dp", None)),
        check_vma=False,
    )
```

```python
import functools

import jax
import jax.numpy as jnp
from jax import lax
from jax.experimental import pallas as pl
from jax.experimental.pallas import tpu as pltpu
from jax.sharding import PartitionSpec as P

LANES = 128
HERE = pl.BlockSpec(memory_space=pl.ANY)
FREE = pl.CostEstimate(flops=0, bytes_accessed=0, transcendentals=0)


def wide(values):
    return values.astype(jnp.float32)


def narrow(values):
    return values.astype(jnp.bfloat16)


def flip(values, axis, bit):
    return lax.ppermute(values, axis, [(i, i ^ bit) for i in range(lax.axis_size(axis))])


def take(values, axis, index):
    return lax.dynamic_index_in_dim(values, index, axis, keepdims=False)


def begin(moves, sems):
    copies = [pltpu.make_async_copy(src, dst, sems.at[k]) for k, (src, dst) in enumerate(moves)]
    for copy in copies:
        copy.start()
    return copies


def pack_kernel(tokens, cotangent, ids_in, probs_in, packed, coded, ids, probs, sems):
    width = tokens.shape[1]
    small = begin([(ids_in, ids), (probs_in, probs)], sems)
    moves = [(tokens, packed.at[:, :width]), (cotangent, packed.at[:, width : 2 * width])]
    large = begin(moves, sems.at[2:4])
    for copy in small:
        copy.wait()
    line = lax.broadcasted_iota(jnp.int32, (LANES, tokens.shape[0]), 0)
    route = jnp.zeros(line.shape, jnp.float32)
    for k in range(ids.shape[0]):
        first = 3 * ids[k : k + 1, :]
        hit = (line >= first) & (line < first + 3)
        route = route + jnp.where(hit, probs[k : k + 1, :], 0.0)
    high = wide(narrow(route))
    middle = wide(narrow(route - high))
    low = (route - high) - middle
    part = lax.rem(line, 3)
    lines = jnp.where(part == 0, high, jnp.where(part == 1, middle, low))
    coded[...] = narrow(lines.T)
    last = begin([(coded, packed.at[:, 2 * width :])], sems.at[4:5])
    for copy in (*large, *last):
        copy.wait()


def packed(tokens, cotangent, expert_ids, gate_probs):
    rows, width = tokens.shape
    top = expert_ids.shape[1]
    return pl.pallas_call(
        pack_kernel,
        out_shape=jax.ShapeDtypeStruct((rows, 2 * width + LANES), jnp.bfloat16),
        in_specs=[pl.BlockSpec(memory_space=pltpu.HBM)] * 4,
        out_specs=pl.BlockSpec(memory_space=pltpu.HBM),
        scratch_shapes=[
            pltpu.VMEM((rows, LANES), jnp.bfloat16),
            pltpu.VMEM((top, rows), jnp.int32),
            pltpu.VMEM((top, rows), jnp.float32),
            pltpu.SemaphoreType.DMA((5,)),
        ],
        compiler_params=pltpu.CompilerParams(vmem_limit_bytes=1 << 20),
        cost_estimate=FREE,
    )(tokens, cotangent, expert_ids.T, gate_probs.T)


def own_columns(values, group_count, parity):
    unit = values.shape[1] // group_count * 2
    blocks = [values[:, k * unit : (k + 1) * unit] for k in range(group_count // 2)]
    even, odd = jnp.concatenate(blocks[0::2], axis=1), jnp.concatenate(blocks[1::2], axis=1)
    return jnp.where(parity == 1, odd, even)


def expert_kernel(group_count, place, *refs):
    blocks, (gate_up, down), made = refs[:-7], refs[-7:-5], refs[-5:]
    tok_own, hid_own, scaled, back_first, back_second = made
    width, units = gate_up.shape[0], down.shape[0]
    tile, split = units // 2, back_first.shape[0]
    me, parity = place[0], place[1]
    lane = lax.broadcasted_iota(jnp.int32, (1, LANES), 1)
    at = 0
    for block in blocks:
        coded = wide(block[:, 2 * width :])
        part = [
            jnp.sum(jnp.where(lane == 3 * me + k, coded, 0.0), axis=1, keepdims=True)
            for k in range(3)
        ]
        weight = (part[0] + part[1]) + part[2]
        here = slice(at, at + block.shape[0])
        scaled[here, :] = narrow(wide(block[:, width : 2 * width]) * weight)
        at += block.shape[0]
    rows = jnp.concatenate([block[:, :width] for block in blocks], axis=0)
    tok_own[...] = own_columns(rows, group_count, parity)
    grads = scaled[...]
    contract = (((1,), (1,)), ((), ()))
    hidden = []
    for at in range(0, units, tile):
        gate = jnp.dot(rows, gate_up[:, at : at + tile], preferred_element_type=jnp.float32)
        up = jnp.dot(
            rows, gate_up[:, units + at : units + at + tile], preferred_element_type=jnp.float32
        )
        sig = jax.nn.sigmoid(gate)
        activated = gate * sig
        hidden.append(narrow(activated * up))
        back_hidden = lax.dot_general(
            grads, down[at : at + tile, :], contract, preferred_element_type=jnp.float32
        )
        slope = up * sig * (1.0 + gate * (1.0 - sig))
        back_gate, back_up = narrow(back_hidden * slope), narrow(back_hidden * activated)
        for back, here in ((back_first, slice(0, split)), (back_second, slice(split, None))):
            back[:, at : at + tile] = back_gate[here]
            back[:, units + at : units + at + tile] = back_up[here]
    hid_own[...] = own_columns(jnp.concatenate(hidden, axis=1), group_count, parity)


def expert_rows(group_count, place, blocks, gate_up, down):
    rows, width = sum(block.shape[0] for block in blocks), gate_up.shape[0]
    units = down.shape[0]
    vmem = pl.BlockSpec(memory_space=pltpu.VMEM)
    shapes = [(rows, width // 2), (rows, units // 2), (rows, width)]
    shapes += [(rows // 2, 2 * units)] * 2
    return pl.pallas_call(
        functools.partial(expert_kernel, group_count),
        out_shape=tuple(jax.ShapeDtypeStruct(shape, jnp.bfloat16) for shape in shapes),
        in_specs=[pl.BlockSpec(memory_space=pltpu.SMEM)] + [vmem] * (len(blocks) + 2),
        out_specs=(vmem,) * 5,
        compiler_params=pltpu.CompilerParams(vmem_limit_bytes=14 << 20),
        cost_estimate=FREE,
    )(place, *blocks, gate_up, down)


ROWS = (((0,), (0,)), ((), ()))


def hold_kernel(cuts, count, *refs):
    values, cut_refs, sems = refs[:count], refs[-1 - len(cuts) : -1], refs[-1]
    moves = [(values[k].at[rows, :], cut) for (k, rows), cut in zip(cuts, cut_refs)]
    for copy in begin(moves, sems):
        copy.wait()


def hold(values, awaited, cuts=()):
    like = [jax.ShapeDtypeStruct(v.shape, v.dtype) for v in values]
    for k, rows in cuts:
        shape = (rows.stop - rows.start, *values[k].shape[1:])
        like.append(jax.ShapeDtypeStruct(shape, values[k].dtype))
    return pl.pallas_call(
        functools.partial(hold_kernel, cuts, len(values)),
        out_shape=tuple(like),
        in_specs=[HERE] * (len(values) + len(awaited)),
        out_specs=(HERE,) * len(like),
        input_output_aliases={k: k for k in range(len(values))},
        scratch_shapes=[pltpu.SemaphoreType.DMA((max(len(cuts), 1),))],
        compiler_params=pltpu.CompilerParams(vmem_limit_bytes=1 << 20),
        cost_estimate=FREE,
    )(*values, *awaited)


def terms_kernel(*refs):
    blocks, (gate_sum, down_sum, sent, mark) = refs[:-4], refs[-4:]
    for k in range(len(blocks) // 5):
        tok_cols, hid_cols, scaled, *halves = [block[...] for block in blocks[5 * k : 5 * k + 5]]
        back = jnp.concatenate(halves, axis=0)
        gate = lax.dot_general(tok_cols, back, ROWS, preferred_element_type=jnp.float32)
        down = lax.dot_general(hid_cols, scaled, ROWS, preferred_element_type=jnp.float32)
        gate_sum[...] = gate if k == 0 else gate_sum[...] + gate
        down_sum[...] = down if k == 0 else down_sum[...] + down
        if k < 2:
            count = halves[1].shape[0]
            sent[k * count : (k + 1) * count, :] = halves[1]
    mark[...] = jnp.zeros_like(mark)


def early_terms(made):
    tok_cols, hid_cols, scaled, back, _ = made[0]
    vmem = pl.BlockSpec(memory_space=pltpu.VMEM)
    return pl.pallas_call(
        terms_kernel,
        out_shape=(
            jax.ShapeDtypeStruct((tok_cols.shape[1], back.shape[1]), jnp.float32),
            jax.ShapeDtypeStruct((hid_cols.shape[1], scaled.shape[1]), jnp.float32),
            jax.ShapeDtypeStruct((2 * back.shape[0], back.shape[1]), jnp.bfloat16),
            jax.ShapeDtypeStruct((8, LANES), jnp.float32),
        ),
        in_specs=[vmem] * (5 * len(made)),
        out_specs=(vmem,) * 4,
        compiler_params=pltpu.CompilerParams(vmem_limit_bytes=16 << 20),
        cost_estimate=FREE,
    )(*[v for block in made for v in block])


def on_device(
    tokens, cotangent, expert_ids, gate_probs, gate_up_weight, down_weight, down_residual
):
    tok_rows, model_width = tokens.shape
    expert_count = lax.axis_size("expert")
    group_count = lax.axis_size("dp")
    gate_up, down_matrix = gate_up_weight[0], down_weight[0]
    hidden_units = down_matrix.shape[0]
    me, group = lax.axis_index("expert"), lax.axis_index("dp")
    bit0, bit1, bit2 = group & 1, (group >> 1) & 1, (group >> 2) & 1
    high_count, half = group_count // 8, tok_rows // 2

    rows_own = packed(tokens, cotangent, expert_ids, gate_probs)
    rows_c = flip(rows_own, "expert", 1)
    rows_x, rows_n = flip(rows_own, "expert", 2), flip(rows_own, "dp", 2)
    residual = down_residual[0, 0].reshape(high_count, 2, 2, 2, -1, model_width)


    def pair_sum(kept, got):
        return wide(kept) + wide(got)

    def residual_side(parity, first):
        return take(take(residual, 2, parity), 2, first)

    res_other = flip(residual_side(1 - bit1, 1 - bit0), "dp", 1)
    res_mine = residual_side(bit1, 1 - bit0)
    place = jnp.stack([me, bit1]).astype(jnp.int32)

    def expert_on(*blocks):
        return expert_rows(group_count, place, blocks, gate_up, down_matrix)

    made = [expert_on(rows_own, rows_c)]
    res_send = narrow(pair_sum(residual_side(1 - bit1, bit0), res_other))
    rows_x, rows_n, res_send, res_mine, cut_x, cut_n = hold(
        (rows_x, rows_n, res_send, res_mine),
        (made[0][1],),
        ((0, slice(0, half)), (1, slice(half, tok_rows))),
    )
    diagonal = [flip(cut_x, "dp", 2), flip(cut_n, "expert", 2)]
    made += [expert_on(rows, flip(rows, "expert", 1)) for rows in (rows_x, rows_n)]
    res_mine = flip(res_mine, "dp", 1)
    gate_early, down_early, back_sent, mark = early_terms(made)
    *diagonal, back_sent, res_send, res_mine = hold(
        (*diagonal, back_sent, res_send, res_mine), (mark,)
    )
    diagonal += [flip(rows, "expert", 1) for rows in diagonal]

    def terms(tok_cols, hid_cols, scaled, back):
        gate = lax.dot_general(tok_cols, back, ROWS, preferred_element_type=jnp.float32)
        down = lax.dot_general(hid_cols, scaled, ROWS, preferred_element_type=jnp.float32)
        return gate, down

    tok_late, hid_late, scaled_late, *back_late = expert_on(*diagonal)
    gate_late, down_late = terms(
        tok_late, hid_late, scaled_late, jnp.concatenate(back_late, axis=0)
    )
    gate_term = narrow(gate_early + gate_late).reshape(high_count, 2, 2, -1, 2 * hidden_units)
    down_term = narrow(down_early + down_late).reshape(high_count, 2, 2, -1, model_width)

    def side(term, third, first):
        return take(take(term, 1, third), 1, first)

    count = gate_term.shape[3]
    first = max(count * 3 // 8, 16)
    edges = [0, first, count]
    far_sent, far_kept = [
        [side(gate_term[:, :, :, i:j], 1 - bit2, bit) for i, j in zip(edges, edges[1:])]
        for bit in (1 - bit0, bit0)
    ]
    far_got = [flip(piece, "dp", 1) for piece in far_sent]
    crossed = [
        flip(narrow(pair_sum(kept, got)), "dp", 4) for kept, got in zip(far_kept, far_got)
    ]
    res_near = flip(res_send, "dp", 2)
    res_near, down_sent = hold(
        (res_near, side(down_term, 1 - bit2, 1 - bit0)), (far_got[0],)
    )
    (near_sent,) = hold((side(gate_term, bit2, 1 - bit0),), (far_got[1],))
    res_sum = pair_sum(residual_side(bit1, bit0), res_mine) + wide(res_near)
    far_down = pair_sum(side(down_term, 1 - bit2, bit0), flip(down_sent, "dp", 1))
    crossed_down = flip(narrow(far_down + take(res_sum, 1, 1 - bit2)), "dp", 4)

    def input_part(back):
        return narrow(jnp.dot(back, gate_up.T, preferred_element_type=jnp.float32))

    core = flip(input_part(back_sent), "expert", 1)
    back_kept = jnp.concatenate([made[0][3], made[1][3]], axis=0)
    total = wide(input_part(back_kept)) + wide(core)
    across = flip(narrow(total[tok_rows:]), "expert", 2)
    token_grad = narrow(total[:tok_rows] + wide(across))

    near_gate = pair_sum(side(gate_term, bit2, bit0), flip(near_sent, "dp", 1))
    (near_sent,) = hold((side(down_term, bit2, 1 - bit0),), (across,))
    near_down = pair_sum(side(down_term, bit2, bit0), flip(near_sent, "dp", 1))
    crossed[-1] = hold((crossed[-1],), (near_sent,))[0]
    gate_sum = near_gate + wide(jnp.concatenate(crossed, axis=1))
    down_sum = near_down + take(res_sum, 1, bit2) + wide(crossed_down)
    bit = 8
    while bit < group_count:
        mine = (group // bit) & 1
        halves = [v.reshape(-1, 2, *v.shape[1:]) for v in (gate_sum, down_sum)]
        gate_sum, down_sum = [
            take(v, 1, mine) + wide(flip(narrow(take(v, 1, 1 - mine)), "dp", bit)) for v in halves
        ]
        bit *= 2
    factor = 1.0 / group_count
    grad_gate_up, grad_down = gate_sum * factor, down_sum * factor
    return (token_grad, grad_gate_up, grad_down)


def solution(mesh):
    placed = (
        P(("dp", "expert"), None),
        P(("dp", "expert"), None),
        P(("dp", "expert"), None),
        P(("dp", "expert"), None),
        P("expert", None, None),
        P("expert", None, None),
        P("dp", "expert", None, None),
    )
    return jax.shard_map(
        on_device,
        mesh=mesh,
        in_specs=placed,
        out_specs=(P(("dp", "expert"), None), P("expert", "dp", None), P("expert", "dp", None)),
        check_vma=False,
    )
```

```python
import functools

import jax
import jax.numpy as jnp
from jax import lax
from jax.experimental import pallas as pl
from jax.experimental.pallas import tpu as pltpu
from jax.sharding import PartitionSpec as P

LANES = 128
FREE = pl.CostEstimate(flops=0, bytes_accessed=0, transcendentals=0)


def wide(values):
    return values.astype(jnp.float32)


def narrow(values):
    return values.astype(jnp.bfloat16)


def flip(values, axis, bit):
    return lax.ppermute(values, axis, [(i, i ^ bit) for i in range(lax.axis_size(axis))])


def take(values, axis, index):
    return lax.dynamic_index_in_dim(values, index, axis, keepdims=False)


def pack_kernel(expert_count, tokens, cotangent, ids, probs, packed, coded, sems):
    width = tokens.shape[1]
    moves = [(tokens, packed.at[:, :width]), (cotangent, packed.at[:, width : 2 * width])]
    copies = [pltpu.make_async_copy(src, dst, sems.at[k]) for k, (src, dst) in enumerate(moves)]
    for copy in copies:
        copy.start()
    line = lax.broadcasted_iota(jnp.int32, (LANES, tokens.shape[0]), 0)
    route = jnp.zeros(line.shape, jnp.float32)
    for k in range(ids.shape[0]):
        first = 3 * ids[k : k + 1, :]
        hit = (line >= first) & (line < first + 3)
        route = route + jnp.where(hit, probs[k : k + 1, :], 0.0)
    high = wide(narrow(route))
    middle = wide(narrow(route - high))
    low = (route - high) - middle
    part = lax.rem(line, 3)
    lines = jnp.where(part == 0, high, jnp.where(part == 1, middle, low))
    coded[...] = narrow(lines.T)
    last = pltpu.make_async_copy(coded, packed.at[:, 2 * width :], sems.at[2])
    last.start()
    for copy in (*copies, last):
        copy.wait()


def packed(tokens, cotangent, expert_ids, gate_probs, expert_count):
    rows, width = tokens.shape
    here, vmem = pl.BlockSpec(memory_space=pl.ANY), pl.BlockSpec(memory_space=pltpu.VMEM)
    return pl.pallas_call(
        functools.partial(pack_kernel, expert_count),
        out_shape=jax.ShapeDtypeStruct((rows, 2 * width + LANES), jnp.bfloat16),
        in_specs=[here, here, vmem, vmem],
        out_specs=here,
        scratch_shapes=[pltpu.VMEM((rows, LANES), jnp.bfloat16), pltpu.SemaphoreType.DMA((3,))],
        compiler_params=pltpu.CompilerParams(vmem_limit_bytes=4 << 20),
        cost_estimate=FREE,
    )(tokens, cotangent, expert_ids.T, gate_probs.T)


def own_columns(values, group_count, parity):
    unit = values.shape[1] // group_count * 2
    blocks = [values[:, k * unit : (k + 1) * unit] for k in range(group_count // 2)]
    even, odd = jnp.concatenate(blocks[0::2], axis=1), jnp.concatenate(blocks[1::2], axis=1)
    return jnp.where(parity == 1, odd, even)


def expert_kernel(group_count, place, *refs):
    blocks, (gate_up, down), made = refs[:-7], refs[-7:-5], refs[-5:]
    tok_own, hid_own, scaled, back_first, back_second = made
    width, units = gate_up.shape[0], down.shape[0]
    tile, split = units // 2, back_first.shape[0]
    me, parity = place[0], place[1]
    lane = lax.broadcasted_iota(jnp.int32, (1, LANES), 1)
    at = 0
    for block in blocks:
        coded = wide(block[:, 2 * width :])
        part = [
            jnp.sum(jnp.where(lane == 3 * me + k, coded, 0.0), axis=1, keepdims=True)
            for k in range(3)
        ]
        weight = (part[0] + part[1]) + part[2]
        here = slice(at, at + block.shape[0])
        scaled[here, :] = narrow(wide(block[:, width : 2 * width]) * weight)
        at += block.shape[0]
    rows = jnp.concatenate([block[:, :width] for block in blocks], axis=0)
    tok_own[...] = own_columns(rows, group_count, parity)
    grads = scaled[...]
    contract = (((1,), (1,)), ((), ()))
    hidden = []
    for at in range(0, units, tile):
        gate = jnp.dot(rows, gate_up[:, at : at + tile], preferred_element_type=jnp.float32)
        up = jnp.dot(
            rows, gate_up[:, units + at : units + at + tile], preferred_element_type=jnp.float32
        )
        sig = jax.nn.sigmoid(gate)
        activated = gate * sig
        hidden.append(narrow(activated * up))
        back_hidden = lax.dot_general(
            grads, down[at : at + tile, :], contract, preferred_element_type=jnp.float32
        )
        slope = up * sig * (1.0 + gate * (1.0 - sig))
        back_gate, back_up = narrow(back_hidden * slope), narrow(back_hidden * activated)
        for back, here in ((back_first, slice(0, split)), (back_second, slice(split, None))):
            back[:, at : at + tile] = back_gate[here]
            back[:, units + at : units + at + tile] = back_up[here]
    hid_own[...] = own_columns(jnp.concatenate(hidden, axis=1), group_count, parity)


def expert_rows(group_count, place, blocks, gate_up, down):
    rows, width = sum(block.shape[0] for block in blocks), gate_up.shape[0]
    units = down.shape[0]
    vmem = pl.BlockSpec(memory_space=pltpu.VMEM)
    shapes = [(rows, width // 2), (rows, units // 2), (rows, width)]
    shapes += [(rows // 2, 2 * units)] * 2
    return pl.pallas_call(
        functools.partial(expert_kernel, group_count),
        out_shape=tuple(jax.ShapeDtypeStruct(shape, jnp.bfloat16) for shape in shapes),
        in_specs=[pl.BlockSpec(memory_space=pltpu.SMEM)] + [vmem] * (len(blocks) + 2),
        out_specs=(vmem,) * 5,
        compiler_params=pltpu.CompilerParams(vmem_limit_bytes=24 << 20),
        cost_estimate=FREE,
    )(place, *blocks, gate_up, down)


ROWS = (((0,), (0,)), ((), ()))


def hold(values, awaited):
    here = pl.BlockSpec(memory_space=pl.ANY)
    return pl.pallas_call(
        lambda *refs: None,
        out_shape=tuple(jax.ShapeDtypeStruct(v.shape, v.dtype) for v in values),
        in_specs=[here] * (len(values) + len(awaited)),
        out_specs=(here,) * len(values),
        input_output_aliases={k: k for k in range(len(values))},
        compiler_params=pltpu.CompilerParams(vmem_limit_bytes=1 << 20),
        cost_estimate=FREE,
    )(*values, *awaited)


def terms_kernel(*refs):
    blocks, (gate_sum, down_sum, sent, mark) = refs[:-4], refs[-4:]
    for k in range(len(blocks) // 5):
        tok_cols, hid_cols, scaled, *halves = [block[...] for block in blocks[5 * k : 5 * k + 5]]
        back = jnp.concatenate(halves, axis=0)
        gate = lax.dot_general(tok_cols, back, ROWS, preferred_element_type=jnp.float32)
        down = lax.dot_general(hid_cols, scaled, ROWS, preferred_element_type=jnp.float32)
        gate_sum[...] = gate if k == 0 else gate_sum[...] + gate
        down_sum[...] = down if k == 0 else down_sum[...] + down
        if k < 2:
            count = halves[1].shape[0]
            sent[k * count : (k + 1) * count, :] = halves[1]
    mark[...] = jnp.zeros_like(mark)


def early_terms(made):
    tok_cols, hid_cols, scaled, back, _ = made[0]
    vmem = pl.BlockSpec(memory_space=pltpu.VMEM)
    return pl.pallas_call(
        terms_kernel,
        out_shape=(
            jax.ShapeDtypeStruct((tok_cols.shape[1], back.shape[1]), jnp.float32),
            jax.ShapeDtypeStruct((hid_cols.shape[1], scaled.shape[1]), jnp.float32),
            jax.ShapeDtypeStruct((2 * back.shape[0], back.shape[1]), jnp.bfloat16),
            jax.ShapeDtypeStruct((8, LANES), jnp.float32),
        ),
        in_specs=[vmem] * (5 * len(made)),
        out_specs=(vmem,) * 4,
        compiler_params=pltpu.CompilerParams(vmem_limit_bytes=24 << 20),
        cost_estimate=FREE,
    )(*[v for block in made for v in block])


def on_device(
    tokens, cotangent, expert_ids, gate_probs, gate_up_weight, down_weight, down_residual
):
    tok_rows, model_width = tokens.shape
    expert_count = lax.axis_size("expert")
    group_count = lax.axis_size("dp")
    gate_up, down_matrix = gate_up_weight[0], down_weight[0]
    hidden_units = down_matrix.shape[0]
    me, group = lax.axis_index("expert"), lax.axis_index("dp")
    bit0, bit1, bit2 = group & 1, (group >> 1) & 1, (group >> 2) & 1
    high_count, half = group_count // 8, tok_rows // 2

    rows_own = packed(tokens, cotangent, expert_ids, gate_probs, expert_count)
    rows_c = flip(rows_own, "expert", 1)
    rows_x, rows_n = flip(rows_own, "expert", 2), flip(rows_own, "dp", 2)
    residual = down_residual[0, 0].reshape(high_count, 2, 2, 2, -1, model_width)


    def pair_sum(kept, got):
        return wide(kept) + wide(got)

    def residual_side(parity, first):
        return take(take(residual, 2, parity), 2, first)

    res_other = flip(residual_side(1 - bit1, 1 - bit0), "dp", 1)
    res_mine = residual_side(bit1, 1 - bit0)
    place = jnp.stack([me, bit1]).astype(jnp.int32)

    def expert_on(*blocks):
        return expert_rows(group_count, place, blocks, gate_up, down_matrix)

    made = [expert_on(rows_own, rows_c)]
    res_send = narrow(pair_sum(residual_side(1 - bit1, bit0), res_other))
    rows_x, rows_n, res_send, res_mine = hold(
        (rows_x, rows_n, res_send, res_mine), (made[0][1],)
    )
    diagonal = [flip(rows_x[:half], "dp", 2), flip(rows_n[half:], "expert", 2)]
    made += [expert_on(rows, flip(rows, "expert", 1)) for rows in (rows_x, rows_n)]
    res_mine = flip(res_mine, "dp", 1)
    gate_early, down_early, back_sent, mark = early_terms(made)
    *diagonal, res_send, res_mine = hold((*diagonal, res_send, res_mine), (mark,))
    diagonal += [flip(rows, "expert", 1) for rows in diagonal]

    def terms(tok_cols, hid_cols, scaled, back):
        gate = lax.dot_general(tok_cols, back, ROWS, preferred_element_type=jnp.float32)
        down = lax.dot_general(hid_cols, scaled, ROWS, preferred_element_type=jnp.float32)
        return gate, down

    tok_late, hid_late, scaled_late, *back_late = expert_on(*diagonal)
    gate_late, down_late = terms(
        tok_late, hid_late, scaled_late, jnp.concatenate(back_late, axis=0)
    )
    gate_term = narrow(gate_early + gate_late).reshape(high_count, 2, 2, -1, 2 * hidden_units)
    down_term = narrow(down_early + down_late).reshape(high_count, 2, 2, -1, model_width)

    def side(term, third, first):
        return take(take(term, 1, third), 1, first)

    count = gate_term.shape[3]
    first = max(count * 3 // 8, 16)
    edges = [0, first, count]
    far_sent, far_kept = [
        [side(gate_term[:, :, :, i:j], 1 - bit2, bit) for i, j in zip(edges, edges[1:])]
        for bit in (1 - bit0, bit0)
    ]
    far_got = [flip(piece, "dp", 1) for piece in far_sent]
    crossed = [
        flip(narrow(pair_sum(kept, got)), "dp", 4) for kept, got in zip(far_kept, far_got)
    ]
    res_near = flip(res_send, "dp", 2)
    res_near, down_sent = hold(
        (res_near, side(down_term, 1 - bit2, 1 - bit0)), (far_got[0],)
    )
    (near_sent,) = hold((side(gate_term, bit2, 1 - bit0),), (far_got[1],))
    res_sum = pair_sum(residual_side(bit1, bit0), res_mine) + wide(res_near)
    far_down = pair_sum(side(down_term, 1 - bit2, bit0), flip(down_sent, "dp", 1))
    crossed_down = flip(narrow(far_down + take(res_sum, 1, 1 - bit2)), "dp", 4)

    def input_part(back):
        return narrow(jnp.dot(back, gate_up.T, preferred_element_type=jnp.float32))

    (back_sent,) = hold((back_sent,), (far_sent[0],))
    core = flip(input_part(back_sent), "expert", 1)
    back_kept = jnp.concatenate([made[0][3], made[1][3]], axis=0)
    total = wide(input_part(back_kept)) + wide(core)
    across = flip(narrow(total[tok_rows:]), "expert", 2)
    token_grad = narrow(total[:tok_rows] + wide(across))

    near_gate = pair_sum(side(gate_term, bit2, bit0), flip(near_sent, "dp", 1))
    (near_sent,) = hold((side(down_term, bit2, 1 - bit0),), (across,))
    near_down = pair_sum(side(down_term, bit2, bit0), flip(near_sent, "dp", 1))
    crossed[-1] = hold((crossed[-1],), (near_sent,))[0]
    gate_sum = near_gate + wide(jnp.concatenate(crossed, axis=1))
    down_sum = near_down + take(res_sum, 1, bit2) + wide(crossed_down)
    bit = 8
    while bit < group_count:
        mine = (group // bit) & 1
        halves = [v.reshape(-1, 2, *v.shape[1:]) for v in (gate_sum, down_sum)]
        gate_sum, down_sum = [
            take(v, 1, mine) + wide(flip(narrow(take(v, 1, 1 - mine)), "dp", bit)) for v in halves
        ]
        bit *= 2
    factor = 1.0 / group_count
    grad_gate_up, grad_down = gate_sum * factor, down_sum * factor
    return (token_grad, grad_gate_up, grad_down)


def solution(mesh):
    placed = (
        P(("dp", "expert"), None),
        P(("dp", "expert"), None),
        P(("dp", "expert"), None),
        P(("dp", "expert"), None),
        P("expert", None, None),
        P("expert", None, None),
        P("dp", "expert", None, None),
    )
    return jax.shard_map(
        on_device,
        mesh=mesh,
        in_specs=placed,
        out_specs=(P(("dp", "expert"), None), P("expert", "dp", None), P("expert", "dp", None)),
        check_vma=False,
    )
```

```python
import functools

import jax
import jax.numpy as jnp
import numpy as np
from jax import lax
from jax.experimental import pallas as pl
from jax.experimental.pallas import tpu as pltpu
from jax.sharding import PartitionSpec as P

LANES = 128
FREE = pl.CostEstimate(flops=0, bytes_accessed=0, transcendentals=0)


def wide(values):
    return values.astype(jnp.float32)


def narrow(values):
    return values.astype(jnp.bfloat16)


def flip(values, axis, bit):
    return lax.ppermute(values, axis, [(i, i ^ bit) for i in range(lax.axis_size(axis))])


def take(values, axis, index):
    starts = [np.uint32(0)] * values.ndim
    starts[axis] = index
    sizes = [1 if k == axis else size for k, size in enumerate(values.shape)]
    return lax.squeeze(lax.dynamic_slice(values, starts, sizes), (axis,))


def pack_kernel(expert_count, tokens, cotangent, ids, probs, packed, coded, sems):
    width = tokens.shape[1]
    moves = [(tokens, packed.at[:, :width]), (cotangent, packed.at[:, width : 2 * width])]
    copies = [pltpu.make_async_copy(src, dst, sems.at[k]) for k, (src, dst) in enumerate(moves)]
    for copy in copies:
        copy.start()
    line = lax.broadcasted_iota(jnp.int32, (LANES, tokens.shape[0]), 0)
    route = jnp.zeros(line.shape, jnp.float32)
    for k in range(ids.shape[0]):
        first = 3 * ids[k : k + 1, :]
        hit = (line >= first) & (line < first + 3)
        route = route + jnp.where(hit, probs[k : k + 1, :], 0.0)
    high = wide(narrow(route))
    middle = wide(narrow(route - high))
    low = (route - high) - middle
    part = lax.rem(line, 3)
    lines = jnp.where(part == 0, high, jnp.where(part == 1, middle, low))
    coded[...] = narrow(lines.T)
    last = pltpu.make_async_copy(coded, packed.at[:, 2 * width :], sems.at[2])
    last.start()
    for copy in (*copies, last):
        copy.wait()


def packed(tokens, cotangent, expert_ids, gate_probs, expert_count):
    rows, width = tokens.shape
    here, vmem = pl.BlockSpec(memory_space=pl.ANY), pl.BlockSpec(memory_space=pltpu.VMEM)
    return pl.pallas_call(
        functools.partial(pack_kernel, expert_count),
        out_shape=jax.ShapeDtypeStruct((rows, 2 * width + LANES), jnp.bfloat16),
        in_specs=[here, here, vmem, vmem],
        out_specs=here,
        scratch_shapes=[pltpu.VMEM((rows, LANES), jnp.bfloat16), pltpu.SemaphoreType.DMA((3,))],
        compiler_params=pltpu.CompilerParams(vmem_limit_bytes=4 << 20),
        cost_estimate=FREE,
    )(tokens, cotangent, expert_ids.T, gate_probs.T)


def own_columns(values, group_count, parity):
    unit = values.shape[1] // group_count * 2
    blocks = [values[:, k * unit : (k + 1) * unit] for k in range(group_count // 2)]
    even, odd = jnp.concatenate(blocks[0::2], axis=1), jnp.concatenate(blocks[1::2], axis=1)
    return jnp.where(parity == 1, odd, even)


def expert_kernel(group_count, place, *refs):
    blocks, (gate_up, down), made = refs[:-7], refs[-7:-5], refs[-5:]
    tok_own, hid_own, scaled, back_first, back_second = made
    width, units = gate_up.shape[0], down.shape[0]
    tile, split = units // 2, back_first.shape[0]
    me, parity = place[0], place[1]
    lane = lax.broadcasted_iota(jnp.int32, (1, LANES), 1)
    at = 0
    for block in blocks:
        coded = wide(block[:, 2 * width :])
        part = [
            jnp.sum(jnp.where(lane == 3 * me + k, coded, 0.0), axis=1, keepdims=True)
            for k in range(3)
        ]
        weight = (part[0] + part[1]) + part[2]
        here = slice(at, at + block.shape[0])
        scaled[here, :] = narrow(wide(block[:, width : 2 * width]) * weight)
        at += block.shape[0]
    rows = jnp.concatenate([block[:, :width] for block in blocks], axis=0)
    tok_own[...] = own_columns(rows, group_count, parity)
    grads = scaled[...]
    contract = (((1,), (1,)), ((), ()))
    hidden = []
    for at in range(0, units, tile):
        gate = jnp.dot(rows, gate_up[:, at : at + tile], preferred_element_type=jnp.float32)
        up = jnp.dot(
            rows, gate_up[:, units + at : units + at + tile], preferred_element_type=jnp.float32
        )
        sig = jax.nn.sigmoid(gate)
        activated = gate * sig
        hidden.append(narrow(activated * up))
        back_hidden = lax.dot_general(
            grads, down[at : at + tile, :], contract, preferred_element_type=jnp.float32
        )
        slope = up * sig * (1.0 + gate * (1.0 - sig))
        back_gate, back_up = narrow(back_hidden * slope), narrow(back_hidden * activated)
        for back, here in ((back_first, slice(0, split)), (back_second, slice(split, None))):
            back[:, at : at + tile] = back_gate[here]
            back[:, units + at : units + at + tile] = back_up[here]
    hid_own[...] = own_columns(jnp.concatenate(hidden, axis=1), group_count, parity)


def expert_rows(group_count, place, blocks, gate_up, down):
    rows, width = sum(block.shape[0] for block in blocks), gate_up.shape[0]
    units = down.shape[0]
    vmem = pl.BlockSpec(memory_space=pltpu.VMEM)
    shapes = [(rows, width // 2), (rows, units // 2), (rows, width)]
    shapes += [(rows // 2, 2 * units)] * 2
    return pl.pallas_call(
        functools.partial(expert_kernel, group_count),
        out_shape=tuple(jax.ShapeDtypeStruct(shape, jnp.bfloat16) for shape in shapes),
        in_specs=[pl.BlockSpec(memory_space=pltpu.SMEM)] + [vmem] * (len(blocks) + 2),
        out_specs=(vmem,) * 5,
        compiler_params=pltpu.CompilerParams(vmem_limit_bytes=24 << 20),
        cost_estimate=FREE,
    )(place, *blocks, gate_up, down)


ROWS = (((0,), (0,)), ((), ()))


def hold(values, awaited):
    here = pl.BlockSpec(memory_space=pl.ANY)
    return pl.pallas_call(
        lambda *refs: None,
        out_shape=tuple(jax.ShapeDtypeStruct(v.shape, v.dtype) for v in values),
        in_specs=[here] * (len(values) + len(awaited)),
        out_specs=(here,) * len(values),
        input_output_aliases={k: k for k in range(len(values))},
        compiler_params=pltpu.CompilerParams(vmem_limit_bytes=1 << 20),
        cost_estimate=FREE,
    )(*values, *awaited)


def terms_kernel(*refs):
    blocks, (gate_sum, down_sum, sent, mark) = refs[:-4], refs[-4:]
    for k in range(len(blocks) // 5):
        tok_cols, hid_cols, scaled, *halves = [block[...] for block in blocks[5 * k : 5 * k + 5]]
        back = jnp.concatenate(halves, axis=0)
        gate = lax.dot_general(tok_cols, back, ROWS, preferred_element_type=jnp.float32)
        down = lax.dot_general(hid_cols, scaled, ROWS, preferred_element_type=jnp.float32)
        gate_sum[...] = gate if k == 0 else gate_sum[...] + gate
        down_sum[...] = down if k == 0 else down_sum[...] + down
        if k < 2:
            count = halves[1].shape[0]
            sent[k * count : (k + 1) * count, :] = halves[1]
    mark[...] = jnp.zeros_like(mark)


def early_terms(made):
    tok_cols, hid_cols, scaled, back, _ = made[0]
    vmem = pl.BlockSpec(memory_space=pltpu.VMEM)
    return pl.pallas_call(
        terms_kernel,
        out_shape=(
            jax.ShapeDtypeStruct((tok_cols.shape[1], back.shape[1]), jnp.float32),
            jax.ShapeDtypeStruct((hid_cols.shape[1], scaled.shape[1]), jnp.float32),
            jax.ShapeDtypeStruct((2 * back.shape[0], back.shape[1]), jnp.bfloat16),
            jax.ShapeDtypeStruct((8, LANES), jnp.float32),
        ),
        in_specs=[vmem] * (5 * len(made)),
        out_specs=(vmem,) * 4,
        compiler_params=pltpu.CompilerParams(vmem_limit_bytes=24 << 20),
        cost_estimate=FREE,
    )(*[v for block in made for v in block])


def on_device(
    tokens, cotangent, expert_ids, gate_probs, gate_up_weight, down_weight, down_residual
):
    tok_rows, model_width = tokens.shape
    expert_count = lax.axis_size("expert")
    group_count = lax.axis_size("dp")
    gate_up, down_matrix = gate_up_weight[0], down_weight[0]
    hidden_units = down_matrix.shape[0]
    me, group = lax.axis_index("expert"), lax.axis_index("dp")
    bits = [lax.convert_element_type((group >> k) & 1, jnp.uint32) for k in range(3)]
    bits += [1 - bit for bit in bits]
    place = jnp.stack([me, (group >> 1) & 1]).astype(jnp.int32)
    high_count, half = group_count // 8, tok_rows // 2

    rows_own = packed(tokens, cotangent, expert_ids, gate_probs, expert_count)
    rows_own, place, bits = lax.optimization_barrier((rows_own, place, bits))
    bit0, bit1, bit2, not0, not1, not2 = bits
    rows_c = flip(rows_own, "expert", 1)
    rows_x, rows_n = flip(rows_own, "expert", 2), flip(rows_own, "dp", 2)
    residual = down_residual[0, 0].reshape(high_count, 2, 2, 2, -1, model_width)


    def pair_sum(kept, got):
        return wide(kept) + wide(got)

    def residual_side(parity, first):
        return take(take(residual, 2, parity), 2, first)

    res_other = flip(residual_side(not1, not0), "dp", 1)
    res_mine = residual_side(bit1, not0)

    def expert_on(*blocks):
        return expert_rows(group_count, place, blocks, gate_up, down_matrix)

    made = [expert_on(rows_own, rows_c)]
    res_send = narrow(pair_sum(residual_side(not1, bit0), res_other))
    rows_x, rows_n, res_send, res_mine = hold(
        (rows_x, rows_n, res_send, res_mine), (made[0][1],)
    )
    diagonal = [flip(rows_x[:half], "dp", 2), flip(rows_n[half:], "expert", 2)]
    made += [expert_on(rows, flip(rows, "expert", 1)) for rows in (rows_x, rows_n)]
    res_mine = flip(res_mine, "dp", 1)
    gate_early, down_early, back_sent, mark = early_terms(made)
    *diagonal, res_send, res_mine = hold((*diagonal, res_send, res_mine), (mark,))
    diagonal += [flip(rows, "expert", 1) for rows in diagonal]

    def terms(tok_cols, hid_cols, scaled, back):
        gate = lax.dot_general(tok_cols, back, ROWS, preferred_element_type=jnp.float32)
        down = lax.dot_general(hid_cols, scaled, ROWS, preferred_element_type=jnp.float32)
        return gate, down

    tok_late, hid_late, scaled_late, *back_late = expert_on(*diagonal)
    gate_late, down_late = terms(
        tok_late, hid_late, scaled_late, jnp.concatenate(back_late, axis=0)
    )
    gate_term = narrow(gate_early + gate_late).reshape(high_count, 2, 2, -1, 2 * hidden_units)
    down_term = narrow(down_early + down_late).reshape(high_count, 2, 2, -1, model_width)

    def side(term, third, first):
        return take(take(term, 1, third), 1, first)

    count = gate_term.shape[3]
    first = max(count * 3 // 8, 16)
    edges = [0, first, count]
    far_sent, far_kept = [
        [side(gate_term[:, :, :, i:j], not2, bit) for i, j in zip(edges, edges[1:])]
        for bit in (not0, bit0)
    ]
    far_got = [flip(piece, "dp", 1) for piece in far_sent]
    crossed = [
        flip(narrow(pair_sum(kept, got)), "dp", 4) for kept, got in zip(far_kept, far_got)
    ]
    res_near = flip(res_send, "dp", 2)
    res_near, down_sent = hold(
        (res_near, side(down_term, not2, not0)), (far_got[0],)
    )
    (near_sent,) = hold((side(gate_term, bit2, not0),), (far_got[1],))
    res_sum = pair_sum(residual_side(bit1, bit0), res_mine) + wide(res_near)
    far_down = pair_sum(side(down_term, not2, bit0), flip(down_sent, "dp", 1))
    crossed_down = flip(narrow(far_down + take(res_sum, 1, not2)), "dp", 4)

    def input_part(back):
        return narrow(jnp.dot(back, gate_up.T, preferred_element_type=jnp.float32))

    (back_sent,) = hold((back_sent,), (far_sent[0],))
    core = flip(input_part(back_sent), "expert", 1)
    back_kept = jnp.concatenate([made[0][3], made[1][3]], axis=0)
    total = wide(input_part(back_kept)) + wide(core)
    across = flip(narrow(total[tok_rows:]), "expert", 2)
    token_grad = narrow(total[:tok_rows] + wide(across))

    near_gate = pair_sum(side(gate_term, bit2, bit0), flip(near_sent, "dp", 1))
    (near_sent,) = hold((side(down_term, bit2, not0),), (across,))
    near_down = pair_sum(side(down_term, bit2, bit0), flip(near_sent, "dp", 1))
    crossed[-1] = hold((crossed[-1],), (near_sent,))[0]
    gate_sum = near_gate + wide(jnp.concatenate(crossed, axis=1))
    down_sum = near_down + take(res_sum, 1, bit2) + wide(crossed_down)
    bit = 8
    while bit < group_count:
        mine = lax.convert_element_type((group // bit) & 1, jnp.uint32)
        halves = [v.reshape(-1, 2, *v.shape[1:]) for v in (gate_sum, down_sum)]
        gate_sum, down_sum = [
            take(v, 1, mine) + wide(flip(narrow(take(v, 1, 1 - mine)), "dp", bit)) for v in halves
        ]
        bit *= 2
    factor = 1.0 / group_count
    grad_gate_up, grad_down = gate_sum * factor, down_sum * factor
    return (token_grad, grad_gate_up, grad_down)


def solution(mesh):
    placed = (
        P(("dp", "expert"), None),
        P(("dp", "expert"), None),
        P(("dp", "expert"), None),
        P(("dp", "expert"), None),
        P("expert", None, None),
        P("expert", None, None),
        P("dp", "expert", None, None),
    )
    return jax.shard_map(
        on_device,
        mesh=mesh,
        in_specs=placed,
        out_specs=(P(("dp", "expert"), None), P("expert", "dp", None), P("expert", "dp", None)),
        check_vma=False,
    )
```

```python
import functools

import jax
import jax.numpy as jnp
import numpy as np
from jax import lax
from jax.experimental import pallas as pl
from jax.experimental.pallas import tpu as pltpu
from jax.sharding import PartitionSpec as P

LANES = 128
FREE = pl.CostEstimate(flops=0, bytes_accessed=0, transcendentals=0)


def wide(values):
    return values.astype(jnp.float32)


def narrow(values):
    return values.astype(jnp.bfloat16)


def flip(values, axis, bit):
    return lax.ppermute(values, axis, [(i, i ^ bit) for i in range(lax.axis_size(axis))])


def take(values, axis, index):
    starts = [np.uint32(0)] * values.ndim
    starts[axis] = index
    sizes = [1 if k == axis else size for k, size in enumerate(values.shape)]
    return lax.squeeze(lax.dynamic_slice(values, starts, sizes), (axis,))


def pack_kernel(expert_count, tokens, cotangent, ids, probs, packed, coded, sems):
    width = tokens.shape[1]
    moves = [(tokens, packed.at[:, :width]), (cotangent, packed.at[:, width : 2 * width])]
    copies = [pltpu.make_async_copy(src, dst, sems.at[k]) for k, (src, dst) in enumerate(moves)]
    for copy in copies:
        copy.start()
    line = lax.broadcasted_iota(jnp.int32, (LANES, tokens.shape[0]), 0)
    route = jnp.zeros(line.shape, jnp.float32)
    for k in range(ids.shape[0]):
        first = 3 * ids[k : k + 1, :]
        hit = (line >= first) & (line < first + 3)
        route = route + jnp.where(hit, probs[k : k + 1, :], 0.0)
    high = wide(narrow(route))
    middle = wide(narrow(route - high))
    low = (route - high) - middle
    part = lax.rem(line, 3)
    lines = jnp.where(part == 0, high, jnp.where(part == 1, middle, low))
    coded[...] = narrow(lines.T)
    last = pltpu.make_async_copy(coded, packed.at[:, 2 * width :], sems.at[2])
    last.start()
    for copy in (*copies, last):
        copy.wait()


def packed(tokens, cotangent, expert_ids, gate_probs, expert_count):
    rows, width = tokens.shape
    here, vmem = pl.BlockSpec(memory_space=pl.ANY), pl.BlockSpec(memory_space=pltpu.VMEM)
    return pl.pallas_call(
        functools.partial(pack_kernel, expert_count),
        out_shape=jax.ShapeDtypeStruct((rows, 2 * width + LANES), jnp.bfloat16),
        in_specs=[here, here, vmem, vmem],
        out_specs=here,
        scratch_shapes=[pltpu.VMEM((rows, LANES), jnp.bfloat16), pltpu.SemaphoreType.DMA((3,))],
        compiler_params=pltpu.CompilerParams(vmem_limit_bytes=4 << 20),
        cost_estimate=FREE,
    )(tokens, cotangent, expert_ids.T, gate_probs.T)


def own_columns(values, group_count, parity):
    unit = values.shape[1] // group_count * 2
    blocks = [values[:, k * unit : (k + 1) * unit] for k in range(group_count // 2)]
    even, odd = jnp.concatenate(blocks[0::2], axis=1), jnp.concatenate(blocks[1::2], axis=1)
    return jnp.where(parity == 1, odd, even)


def expert_kernel(group_count, place, *refs):
    blocks, (gate_up, down), made = refs[:-7], refs[-7:-5], refs[-5:]
    tok_own, hid_own, scaled, back_first, back_second = made
    width, units = gate_up.shape[0], down.shape[0]
    tile, split = units // 2, back_first.shape[0]
    me, parity = place[0], place[1]
    lane = lax.broadcasted_iota(jnp.int32, (1, LANES), 1)
    at = 0
    for block in blocks:
        coded = wide(block[:, 2 * width :])
        part = [
            jnp.sum(jnp.where(lane == 3 * me + k, coded, 0.0), axis=1, keepdims=True)
            for k in range(3)
        ]
        weight = (part[0] + part[1]) + part[2]
        here = slice(at, at + block.shape[0])
        scaled[here, :] = narrow(wide(block[:, width : 2 * width]) * weight)
        at += block.shape[0]
    rows = jnp.concatenate([block[:, :width] for block in blocks], axis=0)
    tok_own[...] = own_columns(rows, group_count, parity)
    grads = scaled[...]
    contract = (((1,), (1,)), ((), ()))
    hidden = []
    for at in range(0, units, tile):
        gate = jnp.dot(rows, gate_up[:, at : at + tile], preferred_element_type=jnp.float32)
        up = jnp.dot(
            rows, gate_up[:, units + at : units + at + tile], preferred_element_type=jnp.float32
        )
        sig = jax.nn.sigmoid(gate)
        activated = gate * sig
        hidden.append(narrow(activated * up))
        back_hidden = lax.dot_general(
            grads, down[at : at + tile, :], contract, preferred_element_type=jnp.float32
        )
        slope = up * sig * (1.0 + gate * (1.0 - sig))
        back_gate, back_up = narrow(back_hidden * slope), narrow(back_hidden * activated)
        for back, here in ((back_first, slice(0, split)), (back_second, slice(split, None))):
            back[:, at : at + tile] = back_gate[here]
            back[:, units + at : units + at + tile] = back_up[here]
    hid_own[...] = own_columns(jnp.concatenate(hidden, axis=1), group_count, parity)


def expert_rows(group_count, place, blocks, gate_up, down):
    rows, width = sum(block.shape[0] for block in blocks), gate_up.shape[0]
    units = down.shape[0]
    vmem = pl.BlockSpec(memory_space=pltpu.VMEM)
    shapes = [(rows, width // 2), (rows, units // 2), (rows, width)]
    shapes += [(rows // 2, 2 * units)] * 2
    return pl.pallas_call(
        functools.partial(expert_kernel, group_count),
        out_shape=tuple(jax.ShapeDtypeStruct(shape, jnp.bfloat16) for shape in shapes),
        in_specs=[pl.BlockSpec(memory_space=pltpu.SMEM)] + [vmem] * (len(blocks) + 2),
        out_specs=(vmem,) * 5,
        compiler_params=pltpu.CompilerParams(vmem_limit_bytes=24 << 20),
        cost_estimate=FREE,
    )(place, *blocks, gate_up, down)


ROWS = (((0,), (0,)), ((), ()))


def hold(values, awaited):
    here = pl.BlockSpec(memory_space=pl.ANY)
    return pl.pallas_call(
        lambda *refs: None,
        out_shape=tuple(jax.ShapeDtypeStruct(v.shape, v.dtype) for v in values),
        in_specs=[here] * (len(values) + len(awaited)),
        out_specs=(here,) * len(values),
        input_output_aliases={k: k for k in range(len(values))},
        compiler_params=pltpu.CompilerParams(vmem_limit_bytes=1 << 20),
        cost_estimate=FREE,
    )(*values, *awaited)


def terms_kernel(*refs):
    blocks, (gate_sum, down_sum, sent, mark) = refs[:-4], refs[-4:]
    for k in range(len(blocks) // 5):
        tok_cols, hid_cols, scaled, *halves = [block[...] for block in blocks[5 * k : 5 * k + 5]]
        back = jnp.concatenate(halves, axis=0)
        gate = lax.dot_general(tok_cols, back, ROWS, preferred_element_type=jnp.float32)
        down = lax.dot_general(hid_cols, scaled, ROWS, preferred_element_type=jnp.float32)
        gate_sum[...] = gate if k == 0 else gate_sum[...] + gate
        down_sum[...] = down if k == 0 else down_sum[...] + down
        if k < 2:
            count = halves[1].shape[0]
            sent[k * count : (k + 1) * count, :] = halves[1]
    mark[...] = jnp.zeros_like(mark)


def early_terms(made):
    tok_cols, hid_cols, scaled, back, _ = made[0]
    vmem = pl.BlockSpec(memory_space=pltpu.VMEM)
    return pl.pallas_call(
        terms_kernel,
        out_shape=(
            jax.ShapeDtypeStruct((tok_cols.shape[1], back.shape[1]), jnp.float32),
            jax.ShapeDtypeStruct((hid_cols.shape[1], scaled.shape[1]), jnp.float32),
            jax.ShapeDtypeStruct((2 * back.shape[0], back.shape[1]), jnp.bfloat16),
            jax.ShapeDtypeStruct((8, LANES), jnp.float32),
        ),
        in_specs=[vmem] * (5 * len(made)),
        out_specs=(vmem,) * 4,
        compiler_params=pltpu.CompilerParams(vmem_limit_bytes=24 << 20),
        cost_estimate=FREE,
    )(*[v for block in made for v in block])


def on_device(
    tokens, cotangent, expert_ids, gate_probs, gate_up_weight, down_weight, down_residual
):
    tok_rows, model_width = tokens.shape
    expert_count = lax.axis_size("expert")
    group_count = lax.axis_size("dp")
    gate_up, down_matrix = gate_up_weight[0], down_weight[0]
    hidden_units = down_matrix.shape[0]
    me, group = lax.axis_index("expert"), lax.axis_index("dp")
    bits = [lax.convert_element_type((group >> k) & 1, jnp.uint32) for k in range(3)]
    bits += [1 - bit for bit in bits]
    place = jnp.stack([me, (group >> 1) & 1]).astype(jnp.int32)
    high_count, half = group_count // 8, tok_rows // 2

    rows_own = packed(tokens, cotangent, expert_ids, gate_probs, expert_count)
    rows_own, place, bits = lax.optimization_barrier((rows_own, place, bits))
    bit0, bit1, bit2, not0, not1, not2 = bits
    rows_c = flip(rows_own, "expert", 1)
    rows_x, rows_n = flip(rows_own, "expert", 2), flip(rows_own, "dp", 2)
    residual = down_residual[0, 0].reshape(high_count, 2, 2, 2, -1, model_width)


    def pair_sum(kept, got):
        return wide(kept) + wide(got)

    def residual_side(parity, first):
        part = take(take(residual, 3, first), 2, parity)
        return jnp.stack([take(part, 1, third) for third in (not2, bit2)], axis=1)

    res_other = flip(residual_side(not1, not0), "dp", 1)
    res_mine = residual_side(bit1, not0)

    def expert_on(*blocks):
        return expert_rows(group_count, place, blocks, gate_up, down_matrix)

    made = [expert_on(rows_own, rows_c)]
    res_send = narrow(pair_sum(residual_side(not1, bit0), res_other))
    rows_x, rows_n, res_send, res_mine = hold(
        (rows_x, rows_n, res_send, res_mine), (made[0][1],)
    )
    diagonal = [flip(rows_x[:half], "dp", 2), flip(rows_n[half:], "expert", 2)]
    made += [expert_on(rows, flip(rows, "expert", 1)) for rows in (rows_x, rows_n)]
    res_mine = flip(res_mine, "dp", 1)
    gate_early, down_early, back_sent, mark = early_terms(made)
    *diagonal, res_send, res_mine = hold((*diagonal, res_send, res_mine), (mark,))
    diagonal += [flip(rows, "expert", 1) for rows in diagonal]

    def terms(tok_cols, hid_cols, scaled, back):
        gate = lax.dot_general(tok_cols, back, ROWS, preferred_element_type=jnp.float32)
        down = lax.dot_general(hid_cols, scaled, ROWS, preferred_element_type=jnp.float32)
        return gate, down

    tok_late, hid_late, scaled_late, *back_late = expert_on(*diagonal)
    gate_late, down_late = terms(
        tok_late, hid_late, scaled_late, jnp.concatenate(back_late, axis=0)
    )
    gate_term = narrow(gate_early + gate_late).reshape(high_count, 2, 2, -1, 2 * hidden_units)
    down_term = narrow(down_early + down_late).reshape(high_count, 2, 2, -1, model_width)

    def side(term, third, first):
        return take(take(term, 1, third), 1, first)

    count = gate_term.shape[3]
    first = max(count * 3 // 8, 16)
    edges = [0, first, count]
    far_sent, far_kept = [
        [side(gate_term[:, :, :, i:j], not2, bit) for i, j in zip(edges, edges[1:])]
        for bit in (not0, bit0)
    ]
    far_got = [flip(piece, "dp", 1) for piece in far_sent]
    crossed = [
        flip(narrow(pair_sum(kept, got)), "dp", 4) for kept, got in zip(far_kept, far_got)
    ]
    res_near = flip(res_send, "dp", 2)
    res_near, down_sent = hold(
        (res_near, side(down_term, not2, not0)), (far_got[0],)
    )
    (near_sent,) = hold((side(gate_term, bit2, not0),), (far_got[1],))
    res_sum = pair_sum(residual_side(bit1, bit0), res_mine) + wide(res_near)
    far_down = pair_sum(side(down_term, not2, bit0), flip(down_sent, "dp", 1))
    crossed_down = flip(narrow(far_down + res_sum[:, 0]), "dp", 4)

    def input_part(back):
        return narrow(jnp.dot(back, gate_up.T, preferred_element_type=jnp.float32))

    (back_sent,) = hold((back_sent,), (far_sent[0],))
    core = flip(input_part(back_sent), "expert", 1)
    back_kept = jnp.concatenate([made[0][3], made[1][3]], axis=0)
    total = wide(input_part(back_kept)) + wide(core)
    across = flip(narrow(total[tok_rows:]), "expert", 2)
    token_grad = narrow(total[:tok_rows] + wide(across))

    near_gate = pair_sum(side(gate_term, bit2, bit0), flip(near_sent, "dp", 1))
    (near_sent,) = hold((side(down_term, bit2, not0),), (across,))
    near_down = pair_sum(side(down_term, bit2, bit0), flip(near_sent, "dp", 1))
    crossed[-1] = hold((crossed[-1],), (near_sent,))[0]
    gate_sum = near_gate + wide(jnp.concatenate(crossed, axis=1))
    down_sum = near_down + res_sum[:, 1] + wide(crossed_down)
    bit = 8
    while bit < group_count:
        mine = lax.convert_element_type((group // bit) & 1, jnp.uint32)
        halves = [v.reshape(-1, 2, *v.shape[1:]) for v in (gate_sum, down_sum)]
        gate_sum, down_sum = [
            take(v, 1, mine) + wide(flip(narrow(take(v, 1, 1 - mine)), "dp", bit)) for v in halves
        ]
        bit *= 2
    factor = 1.0 / group_count
    grad_gate_up, grad_down = gate_sum * factor, down_sum * factor
    return (token_grad, grad_gate_up, grad_down)


def solution(mesh):
    placed = (
        P(("dp", "expert"), None),
        P(("dp", "expert"), None),
        P(("dp", "expert"), None),
        P(("dp", "expert"), None),
        P("expert", None, None),
        P("expert", None, None),
        P("dp", "expert", None, None),
    )
    return jax.shard_map(
        on_device,
        mesh=mesh,
        in_specs=placed,
        out_specs=(P(("dp", "expert"), None), P("expert", "dp", None), P("expert", "dp", None)),
        check_vma=False,
    )
```

```python
import functools

import jax
import jax.numpy as jnp
import numpy as np
from jax import lax
from jax.experimental import pallas as pl
from jax.experimental.pallas import tpu as pltpu
from jax.sharding import PartitionSpec as P

LANES = 128
HERE = pl.BlockSpec(memory_space=pl.ANY)
FREE = pl.CostEstimate(flops=0, bytes_accessed=0, transcendentals=0)


def wide(values):
    return values.astype(jnp.float32)


def narrow(values):
    return values.astype(jnp.bfloat16)


def flip(values, axis, bit):
    return lax.ppermute(values, axis, [(i, i ^ bit) for i in range(lax.axis_size(axis))])


def take(values, axis, index):
    starts = [np.uint32(0)] * values.ndim
    starts[axis] = index
    sizes = [1 if k == axis else size for k, size in enumerate(values.shape)]
    return lax.squeeze(lax.dynamic_slice(values, starts, sizes), (axis,))


def begin(moves, sems):
    copies = [pltpu.make_async_copy(src, dst, sems.at[k]) for k, (src, dst) in enumerate(moves)]
    for copy in copies:
        copy.start()
    return copies


def pack_kernel(tokens, cotangent, ids_in, probs_in, packed, coded, ids, probs, sems):
    width = tokens.shape[1]
    small = begin([(ids_in, ids), (probs_in, probs)], sems)
    moves = [(tokens, packed.at[:, :width]), (cotangent, packed.at[:, width : 2 * width])]
    large = begin(moves, sems.at[2:4])
    for copy in small:
        copy.wait()
    line = lax.broadcasted_iota(jnp.int32, (LANES, tokens.shape[0]), 0)
    route = jnp.zeros(line.shape, jnp.float32)
    for k in range(ids.shape[0]):
        first = 3 * ids[k : k + 1, :]
        hit = (line >= first) & (line < first + 3)
        route = route + jnp.where(hit, probs[k : k + 1, :], 0.0)
    high = wide(narrow(route))
    middle = wide(narrow(route - high))
    low = (route - high) - middle
    part = lax.rem(line, 3)
    lines = jnp.where(part == 0, high, jnp.where(part == 1, middle, low))
    coded[...] = narrow(lines.T)
    last = begin([(coded, packed.at[:, 2 * width :])], sems.at[4:5])
    for copy in (*large, *last):
        copy.wait()


def packed(tokens, cotangent, expert_ids, gate_probs):
    rows, width = tokens.shape
    top = expert_ids.shape[1]
    return pl.pallas_call(
        pack_kernel,
        out_shape=jax.ShapeDtypeStruct((rows, 2 * width + LANES), jnp.bfloat16),
        in_specs=[HERE] * 4,
        out_specs=HERE,
        scratch_shapes=[
            pltpu.VMEM((rows, LANES), jnp.bfloat16),
            pltpu.VMEM((top, rows), jnp.int32),
            pltpu.VMEM((top, rows), jnp.float32),
            pltpu.SemaphoreType.DMA((5,)),
        ],
        cost_estimate=FREE,
    )(tokens, cotangent, expert_ids.T, gate_probs.T)


def own_columns(values, group_count, parity):
    unit = values.shape[1] // group_count * 2
    blocks = [values[:, k * unit : (k + 1) * unit] for k in range(group_count // 2)]
    even, odd = jnp.concatenate(blocks[0::2], axis=1), jnp.concatenate(blocks[1::2], axis=1)
    return jnp.where(parity == 1, odd, even)


def expert_kernel(group_count, place, *refs):
    blocks, (gate_up, down), made = refs[:-7], refs[-7:-5], refs[-5:]
    tok_own, hid_own, scaled, back_first, back_second = made
    width, units = gate_up.shape[0], down.shape[0]
    tile, split = units // 2, back_first.shape[0]
    me, parity = place[0], place[1]
    lane = lax.broadcasted_iota(jnp.int32, (1, LANES), 1)
    at = 0
    for block in blocks:
        coded = wide(block[:, 2 * width :])
        part = [
            jnp.sum(jnp.where(lane == 3 * me + k, coded, 0.0), axis=1, keepdims=True)
            for k in range(3)
        ]
        weight = (part[0] + part[1]) + part[2]
        here = slice(at, at + block.shape[0])
        scaled[here, :] = narrow(wide(block[:, width : 2 * width]) * weight)
        at += block.shape[0]
    rows = jnp.concatenate([block[:, :width] for block in blocks], axis=0)
    tok_own[...] = own_columns(rows, group_count, parity)
    grads = scaled[...]
    contract = (((1,), (1,)), ((), ()))
    hidden = []
    for at in range(0, units, tile):
        gate = jnp.dot(rows, gate_up[:, at : at + tile], preferred_element_type=jnp.float32)
        up = jnp.dot(
            rows, gate_up[:, units + at : units + at + tile], preferred_element_type=jnp.float32
        )
        sig = jax.nn.sigmoid(gate)
        activated = gate * sig
        hidden.append(narrow(activated * up))
        back_hidden = lax.dot_general(
            grads, down[at : at + tile, :], contract, preferred_element_type=jnp.float32
        )
        slope = up * sig * (1.0 + gate * (1.0 - sig))
        back_gate, back_up = narrow(back_hidden * slope), narrow(back_hidden * activated)
        for back, here in ((back_first, slice(0, split)), (back_second, slice(split, None))):
            back[:, at : at + tile] = back_gate[here]
            back[:, units + at : units + at + tile] = back_up[here]
    hid_own[...] = own_columns(jnp.concatenate(hidden, axis=1), group_count, parity)


def expert_rows(group_count, place, blocks, gate_up, down):
    rows, width = sum(block.shape[0] for block in blocks), gate_up.shape[0]
    units = down.shape[0]
    vmem = pl.BlockSpec(memory_space=pltpu.VMEM)
    shapes = [(rows, width // 2), (rows, units // 2), (rows, width)]
    shapes += [(rows // 2, 2 * units)] * 2
    return pl.pallas_call(
        functools.partial(expert_kernel, group_count),
        out_shape=tuple(jax.ShapeDtypeStruct(shape, jnp.bfloat16) for shape in shapes),
        in_specs=[pl.BlockSpec(memory_space=pltpu.SMEM)] + [vmem] * (len(blocks) + 2),
        out_specs=(vmem,) * 5,
        compiler_params=pltpu.CompilerParams(vmem_limit_bytes=24 << 20),
        cost_estimate=FREE,
    )(place, *blocks, gate_up, down)


ROWS = (((0,), (0,)), ((), ()))


def hold(values, awaited):
    here = pl.BlockSpec(memory_space=pl.ANY)
    return pl.pallas_call(
        lambda *refs: None,
        out_shape=tuple(jax.ShapeDtypeStruct(v.shape, v.dtype) for v in values),
        in_specs=[here] * (len(values) + len(awaited)),
        out_specs=(here,) * len(values),
        input_output_aliases={k: k for k in range(len(values))},
        compiler_params=pltpu.CompilerParams(vmem_limit_bytes=1 << 20),
        cost_estimate=FREE,
    )(*values, *awaited)


def terms_kernel(*refs):
    blocks, (gate_sum, down_sum, sent, mark) = refs[:-4], refs[-4:]
    for k in range(len(blocks) // 5):
        tok_cols, hid_cols, scaled, *halves = [block[...] for block in blocks[5 * k : 5 * k + 5]]
        back = jnp.concatenate(halves, axis=0)
        gate = lax.dot_general(tok_cols, back, ROWS, preferred_element_type=jnp.float32)
        down = lax.dot_general(hid_cols, scaled, ROWS, preferred_element_type=jnp.float32)
        gate_sum[...] = gate if k == 0 else gate_sum[...] + gate
        down_sum[...] = down if k == 0 else down_sum[...] + down
        if k < 2:
            count = halves[1].shape[0]
            sent[k * count : (k + 1) * count, :] = halves[1]
    mark[...] = jnp.zeros_like(mark)


def early_terms(made):
    tok_cols, hid_cols, scaled, back, _ = made[0]
    vmem = pl.BlockSpec(memory_space=pltpu.VMEM)
    return pl.pallas_call(
        terms_kernel,
        out_shape=(
            jax.ShapeDtypeStruct((tok_cols.shape[1], back.shape[1]), jnp.float32),
            jax.ShapeDtypeStruct((hid_cols.shape[1], scaled.shape[1]), jnp.float32),
            jax.ShapeDtypeStruct((2 * back.shape[0], back.shape[1]), jnp.bfloat16),
            jax.ShapeDtypeStruct((8, LANES), jnp.float32),
        ),
        in_specs=[vmem] * (5 * len(made)),
        out_specs=(vmem,) * 4,
        compiler_params=pltpu.CompilerParams(vmem_limit_bytes=24 << 20),
        cost_estimate=FREE,
    )(*[v for block in made for v in block])


def on_device(
    tokens, cotangent, expert_ids, gate_probs, gate_up_weight, down_weight, down_residual
):
    tok_rows, model_width = tokens.shape
    expert_count = lax.axis_size("expert")
    group_count = lax.axis_size("dp")
    gate_up, down_matrix = gate_up_weight[0], down_weight[0]
    hidden_units = down_matrix.shape[0]
    me, group = lax.axis_index("expert"), lax.axis_index("dp")
    bits = [lax.convert_element_type((group >> k) & 1, jnp.uint32) for k in range(3)]
    bits += [1 - bit for bit in bits]
    place = jnp.stack([me, (group >> 1) & 1]).astype(jnp.int32)
    high_count, half = group_count // 8, tok_rows // 2

    rows_own = packed(tokens, cotangent, expert_ids, gate_probs)
    rows_own, place, bits = lax.optimization_barrier((rows_own, place, bits))
    bit0, bit1, bit2, not0, not1, not2 = bits
    rows_c = flip(rows_own, "expert", 1)
    rows_x, rows_n = flip(rows_own, "expert", 2), flip(rows_own, "dp", 2)
    residual = down_residual[0, 0].reshape(high_count, 2, 2, 2, -1, model_width)


    def pair_sum(kept, got):
        return wide(kept) + wide(got)

    def residual_side(parity, first):
        part = take(take(residual, 3, first), 2, parity)
        return jnp.stack([take(part, 1, third) for third in (not2, bit2)], axis=1)

    res_other = flip(residual_side(not1, not0), "dp", 1)
    res_mine = residual_side(bit1, not0)

    def expert_on(*blocks):
        return expert_rows(group_count, place, blocks, gate_up, down_matrix)

    made = [expert_on(rows_own, rows_c)]
    res_send = narrow(pair_sum(residual_side(not1, bit0), res_other))
    rows_x, rows_n, res_send, res_mine = hold(
        (rows_x, rows_n, res_send, res_mine), (made[0][1],)
    )
    diagonal = [flip(rows_x[:half], "dp", 2), flip(rows_n[half:], "expert", 2)]
    made += [expert_on(rows, flip(rows, "expert", 1)) for rows in (rows_x, rows_n)]
    res_mine = flip(res_mine, "dp", 1)
    gate_early, down_early, back_sent, mark = early_terms(made)
    *diagonal, res_send, res_mine = hold((*diagonal, res_send, res_mine), (mark,))
    diagonal += [flip(rows, "expert", 1) for rows in diagonal]

    def terms(tok_cols, hid_cols, scaled, back):
        gate = lax.dot_general(tok_cols, back, ROWS, preferred_element_type=jnp.float32)
        down = lax.dot_general(hid_cols, scaled, ROWS, preferred_element_type=jnp.float32)
        return gate, down

    tok_late, hid_late, scaled_late, *back_late = expert_on(*diagonal)
    gate_late, down_late = terms(
        tok_late, hid_late, scaled_late, jnp.concatenate(back_late, axis=0)
    )
    gate_term = narrow(gate_early + gate_late).reshape(high_count, 2, 2, -1, 2 * hidden_units)
    down_term = narrow(down_early + down_late).reshape(high_count, 2, 2, -1, model_width)

    def side(term, third, first):
        return take(take(term, 1, third), 1, first)

    count = gate_term.shape[3]
    first = max(count * 3 // 8, 16)
    edges = [0, first, count]
    far_sent, far_kept = [
        [side(gate_term[:, :, :, i:j], not2, bit) for i, j in zip(edges, edges[1:])]
        for bit in (not0, bit0)
    ]
    far_got = [flip(piece, "dp", 1) for piece in far_sent]
    crossed = [
        flip(narrow(pair_sum(kept, got)), "dp", 4) for kept, got in zip(far_kept, far_got)
    ]
    res_near = flip(res_send, "dp", 2)
    res_near, down_sent = hold(
        (res_near, side(down_term, not2, not0)), (far_got[0],)
    )
    (near_sent,) = hold((side(gate_term, bit2, not0),), (far_got[1],))
    res_sum = pair_sum(residual_side(bit1, bit0), res_mine) + wide(res_near)
    far_down = pair_sum(side(down_term, not2, bit0), flip(down_sent, "dp", 1))
    crossed_down = flip(narrow(far_down + res_sum[:, 0]), "dp", 4)

    def input_part(back):
        return narrow(jnp.dot(back, gate_up.T, preferred_element_type=jnp.float32))

    (back_sent,) = hold((back_sent,), (far_sent[0],))
    core = flip(input_part(back_sent), "expert", 1)
    back_kept = jnp.concatenate([made[0][3], made[1][3]], axis=0)
    total = wide(input_part(back_kept)) + wide(core)
    across = flip(narrow(total[tok_rows:]), "expert", 2)
    token_grad = narrow(total[:tok_rows] + wide(across))

    near_gate = pair_sum(side(gate_term, bit2, bit0), flip(near_sent, "dp", 1))
    (near_sent,) = hold((side(down_term, bit2, not0),), (across,))
    near_down = pair_sum(side(down_term, bit2, bit0), flip(near_sent, "dp", 1))
    crossed[-1] = hold((crossed[-1],), (near_sent,))[0]
    gate_sum = near_gate + wide(jnp.concatenate(crossed, axis=1))
    down_sum = near_down + res_sum[:, 1] + wide(crossed_down)
    bit = 8
    while bit < group_count:
        mine = lax.convert_element_type((group // bit) & 1, jnp.uint32)
        halves = [v.reshape(-1, 2, *v.shape[1:]) for v in (gate_sum, down_sum)]
        gate_sum, down_sum = [
            take(v, 1, mine) + wide(flip(narrow(take(v, 1, 1 - mine)), "dp", bit)) for v in halves
        ]
        bit *= 2
    factor = 1.0 / group_count
    grad_gate_up, grad_down = gate_sum * factor, down_sum * factor
    return (token_grad, grad_gate_up, grad_down)


def solution(mesh):
    placed = (
        P(("dp", "expert"), None),
        P(("dp", "expert"), None),
        P(("dp", "expert"), None),
        P(("dp", "expert"), None),
        P("expert", None, None),
        P("expert", None, None),
        P("dp", "expert", None, None),
    )
    return jax.shard_map(
        on_device,
        mesh=mesh,
        in_specs=placed,
        out_specs=(P(("dp", "expert"), None), P("expert", "dp", None), P("expert", "dp", None)),
        check_vma=False,
    )
```

```python
import functools

import jax
import jax.numpy as jnp
import numpy as np
from jax import lax
from jax.experimental import pallas as pl
from jax.experimental.pallas import tpu as pltpu
from jax.sharding import PartitionSpec as P

LANES = 128
HERE = pl.BlockSpec(memory_space=pl.ANY)
FREE = pl.CostEstimate(flops=0, bytes_accessed=0, transcendentals=0)


def wide(values):
    return values.astype(jnp.float32)


def narrow(values):
    return values.astype(jnp.bfloat16)


def flip(values, axis, bit):
    return lax.ppermute(values, axis, [(i, i ^ bit) for i in range(lax.axis_size(axis))])


def take(values, axis, index):
    starts = [np.uint32(0)] * values.ndim
    starts[axis] = index
    sizes = [1 if k == axis else size for k, size in enumerate(values.shape)]
    return lax.squeeze(lax.dynamic_slice(values, starts, sizes), (axis,))


def begin(moves, sems):
    copies = [pltpu.make_async_copy(src, dst, sems.at[k]) for k, (src, dst) in enumerate(moves)]
    for copy in copies:
        copy.start()
    return copies


def pack_kernel(tokens, cotangent, ids_in, probs_in, packed, ids, probs, sems):
    width = tokens.shape[1]
    small = begin([(ids_in, ids), (probs_in, probs)], sems)
    moves = [(tokens, packed.at[:, :width]), (cotangent, packed.at[:, width : 2 * width])]
    large = begin(moves, sems.at[2:4])
    for copy in small:
        copy.wait()
    line = lax.broadcasted_iota(jnp.int32, (LANES, tokens.shape[0]), 0)
    route = jnp.zeros(line.shape, jnp.float32)
    for k in range(ids.shape[0]):
        first = 3 * ids[k : k + 1, :]
        hit = (line >= first) & (line < first + 3)
        route = route + jnp.where(hit, probs[k : k + 1, :], 0.0)
    high = wide(narrow(route))
    middle = wide(narrow(route - high))
    low = (route - high) - middle
    part = lax.rem(line, 3)
    lines = jnp.where(part == 0, high, jnp.where(part == 1, middle, low))
    packed[:, 2 * width :] = narrow(lines.T)
    for copy in large:
        copy.wait()


def packed(tokens, cotangent, expert_ids, gate_probs):
    rows, width = tokens.shape
    top = expert_ids.shape[1]
    return pl.pallas_call(
        pack_kernel,
        out_shape=jax.ShapeDtypeStruct((rows, 2 * width + LANES), jnp.bfloat16),
        in_specs=[HERE] * 4,
        out_specs=pl.BlockSpec(memory_space=pltpu.VMEM),
        scratch_shapes=[
            pltpu.VMEM((top, rows), jnp.int32),
            pltpu.VMEM((top, rows), jnp.float32),
            pltpu.SemaphoreType.DMA((4,)),
        ],
        cost_estimate=FREE,
    )(tokens, cotangent, expert_ids.T, gate_probs.T)


def own_columns(values, group_count, parity):
    unit = values.shape[1] // group_count * 2
    blocks = [values[:, k * unit : (k + 1) * unit] for k in range(group_count // 2)]
    even, odd = jnp.concatenate(blocks[0::2], axis=1), jnp.concatenate(blocks[1::2], axis=1)
    return jnp.where(parity == 1, odd, even)


def expert_kernel(group_count, place, *refs):
    blocks, (gate_up, down), made = refs[:-7], refs[-7:-5], refs[-5:]
    tok_own, hid_own, scaled, back_first, back_second = made
    width, units = gate_up.shape[0], down.shape[0]
    tile, split = units // 2, back_first.shape[0]
    me, parity = place[0], place[1]
    lane = lax.broadcasted_iota(jnp.int32, (1, LANES), 1)
    at = 0
    for block in blocks:
        coded = wide(block[:, 2 * width :])
        part = [
            jnp.sum(jnp.where(lane == 3 * me + k, coded, 0.0), axis=1, keepdims=True)
            for k in range(3)
        ]
        weight = (part[0] + part[1]) + part[2]
        here = slice(at, at + block.shape[0])
        scaled[here, :] = narrow(wide(block[:, width : 2 * width]) * weight)
        at += block.shape[0]
    rows = jnp.concatenate([block[:, :width] for block in blocks], axis=0)
    tok_own[...] = own_columns(rows, group_count, parity)
    grads = scaled[...]
    contract = (((1,), (1,)), ((), ()))
    hidden = []
    for at in range(0, units, tile):
        gate = jnp.dot(rows, gate_up[:, at : at + tile], preferred_element_type=jnp.float32)
        up = jnp.dot(
            rows, gate_up[:, units + at : units + at + tile], preferred_element_type=jnp.float32
        )
        sig = jax.nn.sigmoid(gate)
        activated = gate * sig
        hidden.append(narrow(activated * up))
        back_hidden = lax.dot_general(
            grads, down[at : at + tile, :], contract, preferred_element_type=jnp.float32
        )
        slope = up * sig * (1.0 + gate * (1.0 - sig))
        back_gate, back_up = narrow(back_hidden * slope), narrow(back_hidden * activated)
        for back, here in ((back_first, slice(0, split)), (back_second, slice(split, None))):
            back[:, at : at + tile] = back_gate[here]
            back[:, units + at : units + at + tile] = back_up[here]
    hid_own[...] = own_columns(jnp.concatenate(hidden, axis=1), group_count, parity)


def expert_rows(group_count, place, blocks, gate_up, down):
    rows, width = sum(block.shape[0] for block in blocks), gate_up.shape[0]
    units = down.shape[0]
    vmem = pl.BlockSpec(memory_space=pltpu.VMEM)
    shapes = [(rows, width // 2), (rows, units // 2), (rows, width)]
    shapes += [(rows // 2, 2 * units)] * 2
    return pl.pallas_call(
        functools.partial(expert_kernel, group_count),
        out_shape=tuple(jax.ShapeDtypeStruct(shape, jnp.bfloat16) for shape in shapes),
        in_specs=[pl.BlockSpec(memory_space=pltpu.SMEM)] + [vmem] * (len(blocks) + 2),
        out_specs=(vmem,) * 5,
        compiler_params=pltpu.CompilerParams(vmem_limit_bytes=24 << 20),
        cost_estimate=FREE,
    )(place, *blocks, gate_up, down)


ROWS = (((0,), (0,)), ((), ()))


def hold(values, awaited):
    here = pl.BlockSpec(memory_space=pl.ANY)
    return pl.pallas_call(
        lambda *refs: None,
        out_shape=tuple(jax.ShapeDtypeStruct(v.shape, v.dtype) for v in values),
        in_specs=[here] * (len(values) + len(awaited)),
        out_specs=(here,) * len(values),
        input_output_aliases={k: k for k in range(len(values))},
        compiler_params=pltpu.CompilerParams(vmem_limit_bytes=1 << 20),
        cost_estimate=FREE,
    )(*values, *awaited)


def terms_kernel(*refs):
    blocks, (gate_sum, down_sum, sent, mark) = refs[:-4], refs[-4:]
    for k in range(len(blocks) // 5):
        tok_cols, hid_cols, scaled, *halves = [block[...] for block in blocks[5 * k : 5 * k + 5]]
        back = jnp.concatenate(halves, axis=0)
        gate = lax.dot_general(tok_cols, back, ROWS, preferred_element_type=jnp.float32)
        down = lax.dot_general(hid_cols, scaled, ROWS, preferred_element_type=jnp.float32)
        gate_sum[...] = gate if k == 0 else gate_sum[...] + gate
        down_sum[...] = down if k == 0 else down_sum[...] + down
        if k < 2:
            count = halves[1].shape[0]
            sent[k * count : (k + 1) * count, :] = halves[1]
    mark[...] = jnp.zeros_like(mark)


def early_terms(made):
    tok_cols, hid_cols, scaled, back, _ = made[0]
    vmem = pl.BlockSpec(memory_space=pltpu.VMEM)
    return pl.pallas_call(
        terms_kernel,
        out_shape=(
            jax.ShapeDtypeStruct((tok_cols.shape[1], back.shape[1]), jnp.float32),
            jax.ShapeDtypeStruct((hid_cols.shape[1], scaled.shape[1]), jnp.float32),
            jax.ShapeDtypeStruct((2 * back.shape[0], back.shape[1]), jnp.bfloat16),
            jax.ShapeDtypeStruct((8, LANES), jnp.float32),
        ),
        in_specs=[vmem] * (5 * len(made)),
        out_specs=(vmem,) * 4,
        compiler_params=pltpu.CompilerParams(vmem_limit_bytes=24 << 20),
        cost_estimate=FREE,
    )(*[v for block in made for v in block])


def on_device(
    tokens, cotangent, expert_ids, gate_probs, gate_up_weight, down_weight, down_residual
):
    tok_rows, model_width = tokens.shape
    expert_count = lax.axis_size("expert")
    group_count = lax.axis_size("dp")
    gate_up, down_matrix = gate_up_weight[0], down_weight[0]
    hidden_units = down_matrix.shape[0]
    me, group = lax.axis_index("expert"), lax.axis_index("dp")
    bits = [lax.convert_element_type((group >> k) & 1, jnp.uint32) for k in range(3)]
    bits += [1 - bit for bit in bits]
    place = jnp.stack([me, (group >> 1) & 1]).astype(jnp.int32)
    high_count, half = group_count // 8, tok_rows // 2

    rows_own = packed(tokens, cotangent, expert_ids, gate_probs)
    rows_own, place, bits = lax.optimization_barrier((rows_own, place, bits))
    bit0, bit1, bit2, not0, not1, not2 = bits
    rows_c = flip(rows_own, "expert", 1)
    rows_x, rows_n = flip(rows_own, "expert", 2), flip(rows_own, "dp", 2)
    residual = down_residual[0, 0].reshape(high_count, 2, 2, 2, -1, model_width)


    def pair_sum(kept, got):
        return wide(kept) + wide(got)

    def residual_side(parity, first):
        part = take(take(residual, 3, first), 2, parity)
        return jnp.stack([take(part, 1, third) for third in (not2, bit2)], axis=1)

    res_other = flip(residual_side(not1, not0), "dp", 1)
    res_mine = residual_side(bit1, not0)

    def expert_on(*blocks):
        return expert_rows(group_count, place, blocks, gate_up, down_matrix)

    made = [expert_on(rows_own, rows_c)]
    res_send = narrow(pair_sum(residual_side(not1, bit0), res_other))
    rows_x, rows_n, res_send, res_mine = hold(
        (rows_x, rows_n, res_send, res_mine), (made[0][1],)
    )
    diagonal = [flip(rows_x[:half], "dp", 2), flip(rows_n[half:], "expert", 2)]
    made += [expert_on(rows, flip(rows, "expert", 1)) for rows in (rows_x, rows_n)]
    res_mine = flip(res_mine, "dp", 1)
    gate_early, down_early, back_sent, mark = early_terms(made)
    *diagonal, res_send, res_mine = hold((*diagonal, res_send, res_mine), (mark,))
    diagonal += [flip(rows, "expert", 1) for rows in diagonal]

    def terms(tok_cols, hid_cols, scaled, back):
        gate = lax.dot_general(tok_cols, back, ROWS, preferred_element_type=jnp.float32)
        down = lax.dot_general(hid_cols, scaled, ROWS, preferred_element_type=jnp.float32)
        return gate, down

    tok_late, hid_late, scaled_late, *back_late = expert_on(*diagonal)
    gate_late, down_late = terms(
        tok_late, hid_late, scaled_late, jnp.concatenate(back_late, axis=0)
    )
    gate_term = narrow(gate_early + gate_late).reshape(high_count, 2, 2, -1, 2 * hidden_units)
    down_term = narrow(down_early + down_late).reshape(high_count, 2, 2, -1, model_width)

    def side(term, third, first):
        return take(take(term, 1, third), 1, first)

    count = gate_term.shape[3]
    first = max(count * 3 // 8, 16)
    edges = [0, first, count]
    far_sent, far_kept = [
        [side(gate_term[:, :, :, i:j], not2, bit) for i, j in zip(edges, edges[1:])]
        for bit in (not0, bit0)
    ]
    far_got = [flip(piece, "dp", 1) for piece in far_sent]
    crossed = [
        flip(narrow(pair_sum(kept, got)), "dp", 4) for kept, got in zip(far_kept, far_got)
    ]
    res_near = flip(res_send, "dp", 2)
    res_near, down_sent = hold(
        (res_near, side(down_term, not2, not0)), (far_got[0],)
    )
    (near_sent,) = hold((side(gate_term, bit2, not0),), (far_got[1],))
    res_sum = pair_sum(residual_side(bit1, bit0), res_mine) + wide(res_near)
    far_down = pair_sum(side(down_term, not2, bit0), flip(down_sent, "dp", 1))
    crossed_down = flip(narrow(far_down + res_sum[:, 0]), "dp", 4)

    def input_part(back):
        return narrow(jnp.dot(back, gate_up.T, preferred_element_type=jnp.float32))

    (back_sent,) = hold((back_sent,), (far_sent[0],))
    core = flip(input_part(back_sent), "expert", 1)
    back_kept = jnp.concatenate([made[0][3], made[1][3]], axis=0)
    total = wide(input_part(back_kept)) + wide(core)
    across = flip(narrow(total[tok_rows:]), "expert", 2)
    token_grad = narrow(total[:tok_rows] + wide(across))

    near_gate = pair_sum(side(gate_term, bit2, bit0), flip(near_sent, "dp", 1))
    (near_sent,) = hold((side(down_term, bit2, not0),), (across,))
    near_down = pair_sum(side(down_term, bit2, bit0), flip(near_sent, "dp", 1))
    crossed[-1] = hold((crossed[-1],), (near_sent,))[0]
    gate_sum = near_gate + wide(jnp.concatenate(crossed, axis=1))
    down_sum = near_down + res_sum[:, 1] + wide(crossed_down)
    bit = 8
    while bit < group_count:
        mine = lax.convert_element_type((group // bit) & 1, jnp.uint32)
        halves = [v.reshape(-1, 2, *v.shape[1:]) for v in (gate_sum, down_sum)]
        gate_sum, down_sum = [
            take(v, 1, mine) + wide(flip(narrow(take(v, 1, 1 - mine)), "dp", bit)) for v in halves
        ]
        bit *= 2
    factor = 1.0 / group_count
    grad_gate_up, grad_down = gate_sum * factor, down_sum * factor
    return (token_grad, grad_gate_up, grad_down)


def solution(mesh):
    placed = (
        P(("dp", "expert"), None),
        P(("dp", "expert"), None),
        P(("dp", "expert"), None),
        P(("dp", "expert"), None),
        P("expert", None, None),
        P("expert", None, None),
        P("dp", "expert", None, None),
    )
    return jax.shard_map(
        on_device,
        mesh=mesh,
        in_specs=placed,
        out_specs=(P(("dp", "expert"), None), P("expert", "dp", None), P("expert", "dp", None)),
        check_vma=False,
    )
```

```python
import functools

import jax
import jax.numpy as jnp
import numpy as np
from jax import lax
from jax.experimental import pallas as pl
from jax.experimental.pallas import tpu as pltpu
from jax.sharding import PartitionSpec as P

LANES = 128
HERE = pl.BlockSpec(memory_space=pl.ANY)
FREE = pl.CostEstimate(flops=0, bytes_accessed=0, transcendentals=0)


def wide(values):
    return values.astype(jnp.float32)


def narrow(values):
    return values.astype(jnp.bfloat16)


def flip(values, axis, bit):
    return lax.ppermute(values, axis, [(i, i ^ bit) for i in range(lax.axis_size(axis))])


def take(values, axis, index):
    starts = [np.uint32(0)] * values.ndim
    starts[axis] = index
    sizes = [1 if k == axis else size for k, size in enumerate(values.shape)]
    return lax.squeeze(lax.dynamic_slice(values, starts, sizes), (axis,))


def begin(moves, sems):
    copies = [pltpu.make_async_copy(src, dst, sems.at[k]) for k, (src, dst) in enumerate(moves)]
    for copy in copies:
        copy.start()
    return copies


def pack_kernel(tokens, cotangent, ids_in, probs_in, packed, ids, probs, sems):
    width = tokens.shape[1]
    small = begin([(ids_in, ids), (probs_in, probs)], sems)
    moves = [(tokens, packed.at[:, :width]), (cotangent, packed.at[:, width : 2 * width])]
    large = begin(moves, sems.at[2:4])
    for copy in small:
        copy.wait()
    line = lax.broadcasted_iota(jnp.int32, (LANES, tokens.shape[0]), 0)
    route = jnp.zeros(line.shape, jnp.float32)
    for k in range(ids.shape[0]):
        first = 3 * ids[k : k + 1, :]
        hit = (line >= first) & (line < first + 3)
        route = route + jnp.where(hit, probs[k : k + 1, :], 0.0)
    high = wide(narrow(route))
    middle = wide(narrow(route - high))
    low = (route - high) - middle
    part = lax.rem(line, 3)
    lines = jnp.where(part == 0, high, jnp.where(part == 1, middle, low))
    packed[:, 2 * width :] = narrow(lines.T)
    for copy in large:
        copy.wait()


def packed(tokens, cotangent, expert_ids, gate_probs):
    rows, width = tokens.shape
    top = expert_ids.shape[1]
    return pl.pallas_call(
        pack_kernel,
        out_shape=jax.ShapeDtypeStruct((rows, 2 * width + LANES), jnp.bfloat16),
        in_specs=[HERE] * 4,
        out_specs=pl.BlockSpec(memory_space=pltpu.VMEM),
        scratch_shapes=[
            pltpu.VMEM((top, rows), jnp.int32),
            pltpu.VMEM((top, rows), jnp.float32),
            pltpu.SemaphoreType.DMA((4,)),
        ],
        cost_estimate=FREE,
    )(tokens, cotangent, expert_ids.T, gate_probs.T)


def own_columns(values, group_count, parity):
    unit = values.shape[1] // group_count * 2
    blocks = [values[:, k * unit : (k + 1) * unit] for k in range(group_count // 2)]
    even, odd = jnp.concatenate(blocks[0::2], axis=1), jnp.concatenate(blocks[1::2], axis=1)
    return jnp.where(parity == 1, odd, even)


def expert_kernel(group_count, place, *refs):
    blocks, (gate_up, down), made = refs[:-7], refs[-7:-5], refs[-5:]
    tok_own, hid_own, scaled, back_first, back_second = made
    width, units = gate_up.shape[0], down.shape[0]
    tile, split = units // 2, back_first.shape[0]
    me, parity = place[0], place[1]
    lane = lax.broadcasted_iota(jnp.int32, (1, LANES), 1)
    at = 0
    for block in blocks:
        coded = wide(block[:, 2 * width :])
        part = [
            jnp.sum(jnp.where(lane == 3 * me + k, coded, 0.0), axis=1, keepdims=True)
            for k in range(3)
        ]
        weight = (part[0] + part[1]) + part[2]
        here = slice(at, at + block.shape[0])
        scaled[here, :] = narrow(wide(block[:, width : 2 * width]) * weight)
        at += block.shape[0]
    rows = jnp.concatenate([block[:, :width] for block in blocks], axis=0)
    tok_own[...] = own_columns(rows, group_count, parity)
    grads = scaled[...]
    contract = (((1,), (1,)), ((), ()))
    hidden = []
    for at in range(0, units, tile):
        gate = jnp.dot(rows, gate_up[:, at : at + tile], preferred_element_type=jnp.float32)
        up = jnp.dot(
            rows, gate_up[:, units + at : units + at + tile], preferred_element_type=jnp.float32
        )
        sig = jax.nn.sigmoid(gate)
        activated = gate * sig
        hidden.append(narrow(activated * up))
        back_hidden = lax.dot_general(
            grads, down[at : at + tile, :], contract, preferred_element_type=jnp.float32
        )
        slope = up * sig * (1.0 + gate * (1.0 - sig))
        back_gate, back_up = narrow(back_hidden * slope), narrow(back_hidden * activated)
        for back, here in ((back_first, slice(0, split)), (back_second, slice(split, None))):
            back[:, at : at + tile] = back_gate[here]
            back[:, units + at : units + at + tile] = back_up[here]
    hid_own[...] = own_columns(jnp.concatenate(hidden, axis=1), group_count, parity)


def last_kernel(group_count, place, *refs):
    *blocks, gate_up, down, early, tok_own, hid_own, scaled, first, second, piece = refs
    made = (tok_own, hid_own, scaled, first, second)
    expert_kernel(group_count, place, *blocks, gate_up, down, *made)
    start, count = pl.multiple_of(place[2], LANES), piece.shape[1]
    back = jnp.concatenate([first[...], second[...]], axis=0)
    late = lax.dot_general(
        tok_own[:, pl.ds(start, LANES)], back, ROWS, preferred_element_type=jnp.float32
    )
    piece[0] = narrow(early[pl.ds(start, count), :] + late[:count])


def last_rows(group_count, place, blocks, gate_up, down, early, count):
    rows, width = sum(block.shape[0] for block in blocks), gate_up.shape[0]
    units = down.shape[0]
    vmem = pl.BlockSpec(memory_space=pltpu.VMEM)
    shapes = [(rows, width // 2), (rows, units // 2), (rows, width)]
    shapes += [(rows // 2, 2 * units)] * 2 + [(1, count, 2 * units)]
    return pl.pallas_call(
        functools.partial(last_kernel, group_count),
        out_shape=tuple(jax.ShapeDtypeStruct(shape, jnp.bfloat16) for shape in shapes),
        in_specs=[pl.BlockSpec(memory_space=pltpu.SMEM)] + [vmem] * (len(blocks) + 3),
        out_specs=(vmem,) * 6,
        compiler_params=pltpu.CompilerParams(vmem_limit_bytes=24 << 20),
        cost_estimate=FREE,
    )(place, *blocks, gate_up, down, early)


def expert_rows(group_count, place, blocks, gate_up, down):
    rows, width = sum(block.shape[0] for block in blocks), gate_up.shape[0]
    units = down.shape[0]
    vmem = pl.BlockSpec(memory_space=pltpu.VMEM)
    shapes = [(rows, width // 2), (rows, units // 2), (rows, width)]
    shapes += [(rows // 2, 2 * units)] * 2
    return pl.pallas_call(
        functools.partial(expert_kernel, group_count),
        out_shape=tuple(jax.ShapeDtypeStruct(shape, jnp.bfloat16) for shape in shapes),
        in_specs=[pl.BlockSpec(memory_space=pltpu.SMEM)] + [vmem] * (len(blocks) + 2),
        out_specs=(vmem,) * 5,
        compiler_params=pltpu.CompilerParams(vmem_limit_bytes=24 << 20),
        cost_estimate=FREE,
    )(place, *blocks, gate_up, down)


ROWS = (((0,), (0,)), ((), ()))


def hold(values, awaited):
    here = pl.BlockSpec(memory_space=pl.ANY)
    return pl.pallas_call(
        lambda *refs: None,
        out_shape=tuple(jax.ShapeDtypeStruct(v.shape, v.dtype) for v in values),
        in_specs=[here] * (len(values) + len(awaited)),
        out_specs=(here,) * len(values),
        input_output_aliases={k: k for k in range(len(values))},
        compiler_params=pltpu.CompilerParams(vmem_limit_bytes=1 << 20),
        cost_estimate=FREE,
    )(*values, *awaited)


def terms_kernel(*refs):
    blocks, (gate_sum, down_sum, sent, mark) = refs[:-4], refs[-4:]
    for k in range(len(blocks) // 5):
        tok_cols, hid_cols, scaled, *halves = [block[...] for block in blocks[5 * k : 5 * k + 5]]
        back = jnp.concatenate(halves, axis=0)
        gate = lax.dot_general(tok_cols, back, ROWS, preferred_element_type=jnp.float32)
        down = lax.dot_general(hid_cols, scaled, ROWS, preferred_element_type=jnp.float32)
        gate_sum[...] = gate if k == 0 else gate_sum[...] + gate
        down_sum[...] = down if k == 0 else down_sum[...] + down
        if k < 2:
            count = halves[1].shape[0]
            sent[k * count : (k + 1) * count, :] = halves[1]
    mark[...] = jnp.zeros_like(mark)


def early_terms(made):
    tok_cols, hid_cols, scaled, back, _ = made[0]
    vmem = pl.BlockSpec(memory_space=pltpu.VMEM)
    return pl.pallas_call(
        terms_kernel,
        out_shape=(
            jax.ShapeDtypeStruct((tok_cols.shape[1], back.shape[1]), jnp.float32),
            jax.ShapeDtypeStruct((hid_cols.shape[1], scaled.shape[1]), jnp.float32),
            jax.ShapeDtypeStruct((2 * back.shape[0], back.shape[1]), jnp.bfloat16),
            jax.ShapeDtypeStruct((8, LANES), jnp.float32),
        ),
        in_specs=[vmem] * (5 * len(made)),
        out_specs=(vmem,) * 4,
        compiler_params=pltpu.CompilerParams(vmem_limit_bytes=24 << 20),
        cost_estimate=FREE,
    )(*[v for block in made for v in block])


def on_device(
    tokens, cotangent, expert_ids, gate_probs, gate_up_weight, down_weight, down_residual
):
    tok_rows, model_width = tokens.shape
    expert_count = lax.axis_size("expert")
    group_count = lax.axis_size("dp")
    gate_up, down_matrix = gate_up_weight[0], down_weight[0]
    hidden_units = down_matrix.shape[0]
    me, group = lax.axis_index("expert"), lax.axis_index("dp")
    bits = [lax.convert_element_type((group >> k) & 1, jnp.uint32) for k in range(3)]
    bits += [1 - bit for bit in bits]
    count = model_width // group_count
    first = max(count * 3 // 8, 16)
    far_at = (2 * (1 - ((group >> 2) & 1)) + (1 - (group & 1))) * count
    place = jnp.stack([me, (group >> 1) & 1, far_at]).astype(jnp.int32)
    high_count, half = group_count // 8, tok_rows // 2

    rows_own = packed(tokens, cotangent, expert_ids, gate_probs)
    rows_own, place, bits = lax.optimization_barrier((rows_own, place, bits))
    bit0, bit1, bit2, not0, not1, not2 = bits
    rows_c = flip(rows_own, "expert", 1)
    rows_x, rows_n = flip(rows_own, "expert", 2), flip(rows_own, "dp", 2)
    residual = down_residual[0, 0].reshape(high_count, 2, 2, 2, -1, model_width)


    def pair_sum(kept, got):
        return wide(kept) + wide(got)

    def residual_side(parity, first):
        part = take(take(residual, 3, first), 2, parity)
        return jnp.stack([take(part, 1, third) for third in (not2, bit2)], axis=1)

    res_other = flip(residual_side(not1, not0), "dp", 1)
    res_mine = residual_side(bit1, not0)

    def expert_on(*blocks):
        return expert_rows(group_count, place, blocks, gate_up, down_matrix)

    made = [expert_on(rows_own, rows_c)]
    res_send = narrow(pair_sum(residual_side(not1, bit0), res_other))
    rows_x, rows_n, res_send, res_mine = hold(
        (rows_x, rows_n, res_send, res_mine), (made[0][1],)
    )
    diagonal = [flip(rows_x[:half], "dp", 2), flip(rows_n[half:], "expert", 2)]
    made += [expert_on(rows, flip(rows, "expert", 1)) for rows in (rows_x, rows_n)]
    res_mine = flip(res_mine, "dp", 1)
    gate_early, down_early, back_sent, mark = early_terms(made)
    *diagonal, res_send, res_mine = hold((*diagonal, res_send, res_mine), (mark,))
    diagonal += [flip(rows, "expert", 1) for rows in diagonal]

    def terms(tok_cols, hid_cols, scaled, back):
        gate = lax.dot_general(tok_cols, back, ROWS, preferred_element_type=jnp.float32)
        down = lax.dot_general(hid_cols, scaled, ROWS, preferred_element_type=jnp.float32)
        return gate, down

    direct = high_count == 1 and count % LANES == 0 and first <= LANES
    if direct:
        tok_late, hid_late, scaled_late, *back_late, first_piece = last_rows(
            group_count, place, diagonal, gate_up, down_matrix, gate_early, first
        )
    else:
        tok_late, hid_late, scaled_late, *back_late = expert_on(*diagonal)
    gate_late, down_late = terms(
        tok_late, hid_late, scaled_late, jnp.concatenate(back_late, axis=0)
    )
    gate_term = narrow(gate_early + gate_late).reshape(high_count, 2, 2, -1, 2 * hidden_units)
    down_term = narrow(down_early + down_late).reshape(high_count, 2, 2, -1, model_width)

    def side(term, third, first):
        return take(take(term, 1, third), 1, first)

    edges = [0, first, count]
    far_sent, far_kept = [
        [side(gate_term[:, :, :, i:j], not2, bit) for i, j in zip(edges, edges[1:])]
        for bit in (not0, bit0)
    ]
    if direct:
        far_sent[0] = first_piece
    far_got = [flip(piece, "dp", 1) for piece in far_sent]
    crossed = [
        flip(narrow(pair_sum(kept, got)), "dp", 4) for kept, got in zip(far_kept, far_got)
    ]
    res_near = flip(res_send, "dp", 2)
    res_near, down_sent = hold(
        (res_near, side(down_term, not2, not0)), (far_got[0],)
    )
    (near_sent,) = hold((side(gate_term, bit2, not0),), (far_got[1],))
    res_sum = pair_sum(residual_side(bit1, bit0), res_mine) + wide(res_near)
    far_down = pair_sum(side(down_term, not2, bit0), flip(down_sent, "dp", 1))
    crossed_down = flip(narrow(far_down + res_sum[:, 0]), "dp", 4)

    def input_part(back):
        return narrow(jnp.dot(back, gate_up.T, preferred_element_type=jnp.float32))

    (back_sent,) = hold((back_sent,), (far_sent[1],))
    core = flip(input_part(back_sent), "expert", 1)
    back_kept = jnp.concatenate([made[0][3], made[1][3]], axis=0)
    total = wide(input_part(back_kept)) + wide(core)
    across = flip(narrow(total[tok_rows:]), "expert", 2)
    token_grad = narrow(total[:tok_rows] + wide(across))

    near_gate = pair_sum(side(gate_term, bit2, bit0), flip(near_sent, "dp", 1))
    (near_sent,) = hold((side(down_term, bit2, not0),), (across,))
    near_down = pair_sum(side(down_term, bit2, bit0), flip(near_sent, "dp", 1))
    crossed[-1] = hold((crossed[-1],), (near_sent,))[0]
    gate_sum = near_gate + wide(jnp.concatenate(crossed, axis=1))
    down_sum = near_down + res_sum[:, 1] + wide(crossed_down)
    bit = 8
    while bit < group_count:
        mine = lax.convert_element_type((group // bit) & 1, jnp.uint32)
        halves = [v.reshape(-1, 2, *v.shape[1:]) for v in (gate_sum, down_sum)]
        gate_sum, down_sum = [
            take(v, 1, mine) + wide(flip(narrow(take(v, 1, 1 - mine)), "dp", bit)) for v in halves
        ]
        bit *= 2
    factor = 1.0 / group_count
    grad_gate_up, grad_down = gate_sum * factor, down_sum * factor
    return (token_grad, grad_gate_up, grad_down)


def solution(mesh):
    placed = (
        P(("dp", "expert"), None),
        P(("dp", "expert"), None),
        P(("dp", "expert"), None),
        P(("dp", "expert"), None),
        P("expert", None, None),
        P("expert", None, None),
        P("dp", "expert", None, None),
    )
    return jax.shard_map(
        on_device,
        mesh=mesh,
        in_specs=placed,
        out_specs=(P(("dp", "expert"), None), P("expert", "dp", None), P("expert", "dp", None)),
        check_vma=False,
    )
```

```python
import functools

import jax
import jax.numpy as jnp
import numpy as np
from jax import lax
from jax.experimental import pallas as pl
from jax.experimental.pallas import tpu as pltpu
from jax.sharding import PartitionSpec as P

LANES = 128
HERE = pl.BlockSpec(memory_space=pl.ANY)
FREE = pl.CostEstimate(flops=0, bytes_accessed=0, transcendentals=0)


def wide(values):
    return values.astype(jnp.float32)


def narrow(values):
    return values.astype(jnp.bfloat16)


def flip(values, axis, bit):
    return lax.ppermute(values, axis, [(i, i ^ bit) for i in range(lax.axis_size(axis))])


def take(values, axis, index):
    starts = [np.uint32(0)] * values.ndim
    starts[axis] = index
    sizes = [1 if k == axis else size for k, size in enumerate(values.shape)]
    return lax.squeeze(lax.dynamic_slice(values, starts, sizes), (axis,))


def begin(moves, sems):
    copies = [pltpu.make_async_copy(src, dst, sems.at[k]) for k, (src, dst) in enumerate(moves)]
    for copy in copies:
        copy.start()
    return copies


PARTS = 4


def pack_kernel(tokens, cotangent, ids_in, probs_in, packed, here, ids, probs, sems):
    rows, width = tokens.shape
    small = begin([(ids_in, ids), (probs_in, probs)], sems)
    spans = [slice(k * rows // PARTS, (k + 1) * rows // PARTS) for k in range(PARTS)]
    moves = []
    for span in spans:
        moves.append((tokens.at[span, :], here.at[span, :width]))
        moves.append((cotangent.at[span, :], here.at[span, width : 2 * width]))
    large = begin(moves, sems.at[2 : 2 + 2 * PARTS])
    for copy in small:
        copy.wait()
    line = lax.broadcasted_iota(jnp.int32, (LANES, tokens.shape[0]), 0)
    route = jnp.zeros(line.shape, jnp.float32)
    for k in range(ids.shape[0]):
        first = 3 * ids[k : k + 1, :]
        hit = (line >= first) & (line < first + 3)
        route = route + jnp.where(hit, probs[k : k + 1, :], 0.0)
    high = wide(narrow(route))
    middle = wide(narrow(route - high))
    low = (route - high) - middle
    part = lax.rem(line, 3)
    lines = jnp.where(part == 0, high, jnp.where(part == 1, middle, low))
    here[:, 2 * width :] = narrow(lines.T)
    out = []
    for k, span in enumerate(spans):
        large[2 * k].wait()
        large[2 * k + 1].wait()
        move = (here.at[span, :], packed.at[span, :])
        out += begin([move], sems.at[2 + 2 * PARTS + k : 3 + 2 * PARTS + k])
    for copy in out:
        copy.wait()


def packed(tokens, cotangent, expert_ids, gate_probs):
    rows, width = tokens.shape
    top = expert_ids.shape[1]
    return pl.pallas_call(
        pack_kernel,
        out_shape=jax.ShapeDtypeStruct((rows, 2 * width + LANES), jnp.bfloat16),
        in_specs=[HERE] * 4,
        out_specs=HERE,
        scratch_shapes=[
            pltpu.VMEM((rows, 2 * width + LANES), jnp.bfloat16),
            pltpu.VMEM((top, rows), jnp.int32),
            pltpu.VMEM((top, rows), jnp.float32),
            pltpu.SemaphoreType.DMA((2 + 3 * PARTS,)),
        ],
        cost_estimate=FREE,
    )(tokens, cotangent, expert_ids.T, gate_probs.T)


def own_columns(values, group_count, parity):
    unit = values.shape[1] // group_count * 2
    blocks = [values[:, k * unit : (k + 1) * unit] for k in range(group_count // 2)]
    even, odd = jnp.concatenate(blocks[0::2], axis=1), jnp.concatenate(blocks[1::2], axis=1)
    return jnp.where(parity == 1, odd, even)


def expert_kernel(group_count, place, *refs):
    blocks, (gate_up, down), made = refs[:-7], refs[-7:-5], refs[-5:]
    tok_own, hid_own, scaled, back_first, back_second = made
    width, units = gate_up.shape[0], down.shape[0]
    tile, split = units // 2, back_first.shape[0]
    me, parity = place[0], place[1]
    lane = lax.broadcasted_iota(jnp.int32, (1, LANES), 1)
    at = 0
    for block in blocks:
        coded = wide(block[:, 2 * width :])
        part = [
            jnp.sum(jnp.where(lane == 3 * me + k, coded, 0.0), axis=1, keepdims=True)
            for k in range(3)
        ]
        weight = (part[0] + part[1]) + part[2]
        here = slice(at, at + block.shape[0])
        scaled[here, :] = narrow(wide(block[:, width : 2 * width]) * weight)
        at += block.shape[0]
    rows = jnp.concatenate([block[:, :width] for block in blocks], axis=0)
    tok_own[...] = own_columns(rows, group_count, parity)
    grads = scaled[...]
    contract = (((1,), (1,)), ((), ()))
    hidden = []
    for at in range(0, units, tile):
        gate = jnp.dot(rows, gate_up[:, at : at + tile], preferred_element_type=jnp.float32)
        up = jnp.dot(
            rows, gate_up[:, units + at : units + at + tile], preferred_element_type=jnp.float32
        )
        sig = jax.nn.sigmoid(gate)
        activated = gate * sig
        hidden.append(narrow(activated * up))
        back_hidden = lax.dot_general(
            grads, down[at : at + tile, :], contract, preferred_element_type=jnp.float32
        )
        slope = up * sig * (1.0 + gate * (1.0 - sig))
        back_gate, back_up = narrow(back_hidden * slope), narrow(back_hidden * activated)
        for back, here in ((back_first, slice(0, split)), (back_second, slice(split, None))):
            back[:, at : at + tile] = back_gate[here]
            back[:, units + at : units + at + tile] = back_up[here]
    hid_own[...] = own_columns(jnp.concatenate(hidden, axis=1), group_count, parity)


def last_kernel(group_count, place, *refs):
    *blocks, gate_up, down, early, tok_own, hid_own, scaled, first, second, piece = refs
    made = (tok_own, hid_own, scaled, first, second)
    expert_kernel(group_count, place, *blocks, gate_up, down, *made)
    start, count = pl.multiple_of(place[2], LANES), piece.shape[1]
    back = jnp.concatenate([first[...], second[...]], axis=0)
    late = lax.dot_general(
        tok_own[:, pl.ds(start, LANES)], back, ROWS, preferred_element_type=jnp.float32
    )
    piece[0] = narrow(early[pl.ds(start, count), :] + late[:count])


def last_rows(group_count, place, blocks, gate_up, down, early, count):
    rows, width = sum(block.shape[0] for block in blocks), gate_up.shape[0]
    units = down.shape[0]
    vmem = pl.BlockSpec(memory_space=pltpu.VMEM)
    shapes = [(rows, width // 2), (rows, units // 2), (rows, width)]
    shapes += [(rows // 2, 2 * units)] * 2 + [(1, count, 2 * units)]
    return pl.pallas_call(
        functools.partial(last_kernel, group_count),
        out_shape=tuple(jax.ShapeDtypeStruct(shape, jnp.bfloat16) for shape in shapes),
        in_specs=[pl.BlockSpec(memory_space=pltpu.SMEM)] + [vmem] * (len(blocks) + 3),
        out_specs=(vmem,) * 6,
        compiler_params=pltpu.CompilerParams(vmem_limit_bytes=24 << 20),
        cost_estimate=FREE,
    )(place, *blocks, gate_up, down, early)


def expert_rows(group_count, place, blocks, gate_up, down):
    rows, width = sum(block.shape[0] for block in blocks), gate_up.shape[0]
    units = down.shape[0]
    vmem = pl.BlockSpec(memory_space=pltpu.VMEM)
    shapes = [(rows, width // 2), (rows, units // 2), (rows, width)]
    shapes += [(rows // 2, 2 * units)] * 2
    return pl.pallas_call(
        functools.partial(expert_kernel, group_count),
        out_shape=tuple(jax.ShapeDtypeStruct(shape, jnp.bfloat16) for shape in shapes),
        in_specs=[pl.BlockSpec(memory_space=pltpu.SMEM)] + [vmem] * (len(blocks) + 2),
        out_specs=(vmem,) * 5,
        compiler_params=pltpu.CompilerParams(vmem_limit_bytes=24 << 20),
        cost_estimate=FREE,
    )(place, *blocks, gate_up, down)


ROWS = (((0,), (0,)), ((), ()))


def hold(values, awaited):
    here = pl.BlockSpec(memory_space=pl.ANY)
    return pl.pallas_call(
        lambda *refs: None,
        out_shape=tuple(jax.ShapeDtypeStruct(v.shape, v.dtype) for v in values),
        in_specs=[here] * (len(values) + len(awaited)),
        out_specs=(here,) * len(values),
        input_output_aliases={k: k for k in range(len(values))},
        compiler_params=pltpu.CompilerParams(vmem_limit_bytes=1 << 20),
        cost_estimate=FREE,
    )(*values, *awaited)


def terms_kernel(*refs):
    blocks, (gate_sum, down_sum, sent, mark) = refs[:-4], refs[-4:]
    for k in range(len(blocks) // 5):
        tok_cols, hid_cols, scaled, *halves = [block[...] for block in blocks[5 * k : 5 * k + 5]]
        back = jnp.concatenate(halves, axis=0)
        gate = lax.dot_general(tok_cols, back, ROWS, preferred_element_type=jnp.float32)
        down = lax.dot_general(hid_cols, scaled, ROWS, preferred_element_type=jnp.float32)
        gate_sum[...] = gate if k == 0 else gate_sum[...] + gate
        down_sum[...] = down if k == 0 else down_sum[...] + down
        if k < 2:
            count = halves[1].shape[0]
            sent[k * count : (k + 1) * count, :] = halves[1]
    mark[...] = jnp.zeros_like(mark)


def early_terms(made):
    tok_cols, hid_cols, scaled, back, _ = made[0]
    vmem = pl.BlockSpec(memory_space=pltpu.VMEM)
    return pl.pallas_call(
        terms_kernel,
        out_shape=(
            jax.ShapeDtypeStruct((tok_cols.shape[1], back.shape[1]), jnp.float32),
            jax.ShapeDtypeStruct((hid_cols.shape[1], scaled.shape[1]), jnp.float32),
            jax.ShapeDtypeStruct((2 * back.shape[0], back.shape[1]), jnp.bfloat16),
            jax.ShapeDtypeStruct((8, LANES), jnp.float32),
        ),
        in_specs=[vmem] * (5 * len(made)),
        out_specs=(vmem,) * 4,
        compiler_params=pltpu.CompilerParams(vmem_limit_bytes=24 << 20),
        cost_estimate=FREE,
    )(*[v for block in made for v in block])


def on_device(
    tokens, cotangent, expert_ids, gate_probs, gate_up_weight, down_weight, down_residual
):
    tok_rows, model_width = tokens.shape
    expert_count = lax.axis_size("expert")
    group_count = lax.axis_size("dp")
    gate_up, down_matrix = gate_up_weight[0], down_weight[0]
    hidden_units = down_matrix.shape[0]
    me, group = lax.axis_index("expert"), lax.axis_index("dp")
    bits = [lax.convert_element_type((group >> k) & 1, jnp.uint32) for k in range(3)]
    bits += [1 - bit for bit in bits]
    count = model_width // group_count
    first = max(count * 3 // 8, 16)
    far_at = (2 * (1 - ((group >> 2) & 1)) + (1 - (group & 1))) * count
    place = jnp.stack([me, (group >> 1) & 1, far_at]).astype(jnp.int32)
    high_count, half = group_count // 8, tok_rows // 2

    rows_own = packed(tokens, cotangent, expert_ids, gate_probs)
    rows_own, place, bits = lax.optimization_barrier((rows_own, place, bits))
    bit0, bit1, bit2, not0, not1, not2 = bits
    rows_c = flip(rows_own, "expert", 1)
    rows_x, rows_n = flip(rows_own, "expert", 2), flip(rows_own, "dp", 2)
    residual = down_residual[0, 0].reshape(high_count, 2, 2, 2, -1, model_width)


    def pair_sum(kept, got):
        return wide(kept) + wide(got)

    def residual_side(parity, first):
        part = take(take(residual, 3, first), 2, parity)
        return jnp.stack([take(part, 1, third) for third in (not2, bit2)], axis=1)

    res_other = flip(residual_side(not1, not0), "dp", 1)
    res_mine = residual_side(bit1, not0)

    def expert_on(*blocks):
        return expert_rows(group_count, place, blocks, gate_up, down_matrix)

    made = [expert_on(rows_own, rows_c)]
    res_send = narrow(pair_sum(residual_side(not1, bit0), res_other))
    rows_x, rows_n, res_send, res_mine = hold(
        (rows_x, rows_n, res_send, res_mine), (made[0][1],)
    )
    diagonal = [flip(rows_x[:half], "dp", 2), flip(rows_n[half:], "expert", 2)]
    made += [expert_on(rows, flip(rows, "expert", 1)) for rows in (rows_x, rows_n)]
    res_mine = flip(res_mine, "dp", 1)
    gate_early, down_early, back_sent, mark = early_terms(made)
    *diagonal, res_send, res_mine = hold((*diagonal, res_send, res_mine), (mark,))
    diagonal += [flip(rows, "expert", 1) for rows in diagonal]

    def terms(tok_cols, hid_cols, scaled, back):
        gate = lax.dot_general(tok_cols, back, ROWS, preferred_element_type=jnp.float32)
        down = lax.dot_general(hid_cols, scaled, ROWS, preferred_element_type=jnp.float32)
        return gate, down

    direct = high_count == 1 and count % LANES == 0 and first <= LANES
    if direct:
        tok_late, hid_late, scaled_late, *back_late, first_piece = last_rows(
            group_count, place, diagonal, gate_up, down_matrix, gate_early, first
        )
    else:
        tok_late, hid_late, scaled_late, *back_late = expert_on(*diagonal)
    gate_late, down_late = terms(
        tok_late, hid_late, scaled_late, jnp.concatenate(back_late, axis=0)
    )
    gate_term = narrow(gate_early + gate_late).reshape(high_count, 2, 2, -1, 2 * hidden_units)
    down_term = narrow(down_early + down_late).reshape(high_count, 2, 2, -1, model_width)

    def side(term, third, first):
        return take(take(term, 1, third), 1, first)

    edges = [0, first, count]
    far_sent, far_kept = [
        [side(gate_term[:, :, :, i:j], not2, bit) for i, j in zip(edges, edges[1:])]
        for bit in (not0, bit0)
    ]
    if direct:
        far_sent[0] = first_piece
    far_got = [flip(piece, "dp", 1) for piece in far_sent]
    crossed = [
        flip(narrow(pair_sum(kept, got)), "dp", 4) for kept, got in zip(far_kept, far_got)
    ]
    res_near = flip(res_send, "dp", 2)
    res_near, down_sent = hold(
        (res_near, side(down_term, not2, not0)), (far_got[0],)
    )
    (near_sent,) = hold((side(gate_term, bit2, not0),), (far_got[1],))
    res_sum = pair_sum(residual_side(bit1, bit0), res_mine) + wide(res_near)
    far_down = pair_sum(side(down_term, not2, bit0), flip(down_sent, "dp", 1))
    crossed_down = flip(narrow(far_down + res_sum[:, 0]), "dp", 4)

    def input_part(back):
        return narrow(jnp.dot(back, gate_up.T, preferred_element_type=jnp.float32))

    (back_sent,) = hold((back_sent,), (far_sent[1],))
    core = flip(input_part(back_sent), "expert", 1)
    back_kept = jnp.concatenate([made[0][3], made[1][3]], axis=0)
    total = wide(input_part(back_kept)) + wide(core)
    across = flip(narrow(total[tok_rows:]), "expert", 2)
    token_grad = narrow(total[:tok_rows] + wide(across))

    near_gate = pair_sum(side(gate_term, bit2, bit0), flip(near_sent, "dp", 1))
    (near_sent,) = hold((side(down_term, bit2, not0),), (across,))
    near_down = pair_sum(side(down_term, bit2, bit0), flip(near_sent, "dp", 1))
    crossed[-1] = hold((crossed[-1],), (near_sent,))[0]
    gate_sum = near_gate + wide(jnp.concatenate(crossed, axis=1))
    near_down = lax.optimization_barrier(near_down + res_sum[:, 1])
    down_sum = near_down + wide(crossed_down)
    bit = 8
    while bit < group_count:
        mine = lax.convert_element_type((group // bit) & 1, jnp.uint32)
        halves = [v.reshape(-1, 2, *v.shape[1:]) for v in (gate_sum, down_sum)]
        gate_sum, down_sum = [
            take(v, 1, mine) + wide(flip(narrow(take(v, 1, 1 - mine)), "dp", bit)) for v in halves
        ]
        bit *= 2
    factor = 1.0 / group_count
    grad_gate_up, grad_down = gate_sum * factor, down_sum * factor
    return (token_grad, grad_gate_up, grad_down)


def solution(mesh):
    placed = (
        P(("dp", "expert"), None),
        P(("dp", "expert"), None),
        P(("dp", "expert"), None),
        P(("dp", "expert"), None),
        P("expert", None, None),
        P("expert", None, None),
        P("dp", "expert", None, None),
    )
    return jax.shard_map(
        on_device,
        mesh=mesh,
        in_specs=placed,
        out_specs=(P(("dp", "expert"), None), P("expert", "dp", None), P("expert", "dp", None)),
        check_vma=False,
    )
```

```python
import functools

import jax
import jax.numpy as jnp
import numpy as np
from jax import lax
from jax.experimental import pallas as pl
from jax.experimental.pallas import tpu as pltpu
from jax.sharding import PartitionSpec as P

LANES = 128
HERE = pl.BlockSpec(memory_space=pl.ANY)
FREE = pl.CostEstimate(flops=0, bytes_accessed=0, transcendentals=0)


def wide(values):
    return values.astype(jnp.float32)


def narrow(values):
    return values.astype(jnp.bfloat16)


def flip(values, axis, bit):
    return lax.ppermute(values, axis, [(i, i ^ bit) for i in range(lax.axis_size(axis))])


def take(values, axis, index):
    starts = [np.uint32(0)] * values.ndim
    starts[axis] = index
    sizes = [1 if k == axis else size for k, size in enumerate(values.shape)]
    return lax.squeeze(lax.dynamic_slice(values, starts, sizes), (axis,))


def begin(moves, sems):
    copies = [pltpu.make_async_copy(src, dst, sems.at[k]) for k, (src, dst) in enumerate(moves)]
    for copy in copies:
        copy.start()
    return copies


PARTS = 4


def pack_kernel(tokens, cotangent, ids_in, probs_in, packed, here, ids, probs, sems):
    rows, width = tokens.shape
    small = begin([(ids_in, ids), (probs_in, probs)], sems)
    spans = [slice(k * rows // PARTS, (k + 1) * rows // PARTS) for k in range(PARTS)]
    moves = []
    for span in spans:
        moves.append((tokens.at[span, :], here.at[span, :width]))
        moves.append((cotangent.at[span, :], here.at[span, width : 2 * width]))
    large = begin(moves, sems.at[2 : 2 + 2 * PARTS])
    for copy in small:
        copy.wait()
    line = lax.broadcasted_iota(jnp.int32, (LANES, tokens.shape[0]), 0)
    route = jnp.zeros(line.shape, jnp.float32)
    for k in range(ids.shape[0]):
        first = 3 * ids[k : k + 1, :]
        hit = (line >= first) & (line < first + 3)
        route = route + jnp.where(hit, probs[k : k + 1, :], 0.0)
    high = wide(narrow(route))
    middle = wide(narrow(route - high))
    low = (route - high) - middle
    part = lax.rem(line, 3)
    lines = jnp.where(part == 0, high, jnp.where(part == 1, middle, low))
    here[:, 2 * width :] = narrow(lines.T)
    out = []
    for k, span in enumerate(spans):
        large[2 * k].wait()
        large[2 * k + 1].wait()
        move = (here.at[span, :], packed.at[span, :])
        out += begin([move], sems.at[2 + 2 * PARTS + k : 3 + 2 * PARTS + k])
    for copy in out:
        copy.wait()


def packed(tokens, cotangent, expert_ids, gate_probs):
    rows, width = tokens.shape
    top = expert_ids.shape[1]
    return pl.pallas_call(
        pack_kernel,
        out_shape=jax.ShapeDtypeStruct((rows, 2 * width + LANES), jnp.bfloat16),
        in_specs=[HERE] * 4,
        out_specs=HERE,
        scratch_shapes=[
            pltpu.VMEM((rows, 2 * width + LANES), jnp.bfloat16),
            pltpu.VMEM((top, rows), jnp.int32),
            pltpu.VMEM((top, rows), jnp.float32),
            pltpu.SemaphoreType.DMA((2 + 3 * PARTS,)),
        ],
        cost_estimate=FREE,
    )(tokens, cotangent, expert_ids.T, gate_probs.T)


def own_columns(values, group_count, parity):
    unit = values.shape[1] // group_count * 2
    blocks = [values[:, k * unit : (k + 1) * unit] for k in range(group_count // 2)]
    even, odd = jnp.concatenate(blocks[0::2], axis=1), jnp.concatenate(blocks[1::2], axis=1)
    return jnp.where(parity == 1, odd, even)


def expert_kernel(group_count, place, *refs):
    blocks, (gate_up, down), made = refs[:-7], refs[-7:-5], refs[-5:]
    tok_own, hid_own, scaled, back_first, back_second = made
    width, units = gate_up.shape[0], down.shape[0]
    tile, split = units // 2, back_first.shape[0]
    me, parity = place[0], place[1]
    lane = lax.broadcasted_iota(jnp.int32, (1, LANES), 1)
    at = 0
    for block in blocks:
        coded = wide(block[:, 2 * width :])
        part = [
            jnp.sum(jnp.where(lane == 3 * me + k, coded, 0.0), axis=1, keepdims=True)
            for k in range(3)
        ]
        weight = (part[0] + part[1]) + part[2]
        here = slice(at, at + block.shape[0])
        scaled[here, :] = narrow(wide(block[:, width : 2 * width]) * weight)
        at += block.shape[0]
    rows = jnp.concatenate([block[:, :width] for block in blocks], axis=0)
    tok_own[...] = own_columns(rows, group_count, parity)
    grads = scaled[...]
    contract = (((1,), (1,)), ((), ()))
    hidden = []
    for at in range(0, units, tile):
        gate = jnp.dot(rows, gate_up[:, at : at + tile], preferred_element_type=jnp.float32)
        up = jnp.dot(
            rows, gate_up[:, units + at : units + at + tile], preferred_element_type=jnp.float32
        )
        sig = jax.nn.sigmoid(gate)
        activated = gate * sig
        hidden.append(narrow(activated * up))
        back_hidden = lax.dot_general(
            grads, down[at : at + tile, :], contract, preferred_element_type=jnp.float32
        )
        slope = up * sig * (1.0 + gate * (1.0 - sig))
        back_gate, back_up = narrow(back_hidden * slope), narrow(back_hidden * activated)
        for back, here in ((back_first, slice(0, split)), (back_second, slice(split, None))):
            back[:, at : at + tile] = back_gate[here]
            back[:, units + at : units + at + tile] = back_up[here]
    hid_own[...] = own_columns(jnp.concatenate(hidden, axis=1), group_count, parity)


def last_kernel(group_count, place, *refs):
    *blocks, gate_up, down, early, tok_own, hid_own, scaled, first, second, piece = refs
    made = (tok_own, hid_own, scaled, first, second)
    expert_kernel(group_count, place, *blocks, gate_up, down, *made)
    start, count = pl.multiple_of(place[2], LANES), piece.shape[1]
    back = jnp.concatenate([first[...], second[...]], axis=0)
    late = lax.dot_general(
        tok_own[:, pl.ds(start, LANES)], back, ROWS, preferred_element_type=jnp.float32
    )
    piece[0] = narrow(early[pl.ds(start, count), :] + late[:count])


def last_rows(group_count, place, blocks, gate_up, down, early, count):
    rows, width = sum(block.shape[0] for block in blocks), gate_up.shape[0]
    units = down.shape[0]
    vmem = pl.BlockSpec(memory_space=pltpu.VMEM)
    shapes = [(rows, width // 2), (rows, units // 2), (rows, width)]
    shapes += [(rows // 2, 2 * units)] * 2 + [(1, count, 2 * units)]
    return pl.pallas_call(
        functools.partial(last_kernel, group_count),
        out_shape=tuple(jax.ShapeDtypeStruct(shape, jnp.bfloat16) for shape in shapes),
        in_specs=[pl.BlockSpec(memory_space=pltpu.SMEM)] + [vmem] * (len(blocks) + 3),
        out_specs=(vmem,) * 6,
        compiler_params=pltpu.CompilerParams(vmem_limit_bytes=24 << 20),
        cost_estimate=FREE,
    )(place, *blocks, gate_up, down, early)


def expert_rows(group_count, place, blocks, gate_up, down):
    rows, width = sum(block.shape[0] for block in blocks), gate_up.shape[0]
    units = down.shape[0]
    vmem = pl.BlockSpec(memory_space=pltpu.VMEM)
    shapes = [(rows, width // 2), (rows, units // 2), (rows, width)]
    shapes += [(rows // 2, 2 * units)] * 2
    return pl.pallas_call(
        functools.partial(expert_kernel, group_count),
        out_shape=tuple(jax.ShapeDtypeStruct(shape, jnp.bfloat16) for shape in shapes),
        in_specs=[pl.BlockSpec(memory_space=pltpu.SMEM)] + [vmem] * (len(blocks) + 2),
        out_specs=(vmem,) * 5,
        compiler_params=pltpu.CompilerParams(vmem_limit_bytes=24 << 20),
        cost_estimate=FREE,
    )(place, *blocks, gate_up, down)


ROWS = (((0,), (0,)), ((), ()))


def hold(values, awaited):
    here = pl.BlockSpec(memory_space=pl.ANY)
    return pl.pallas_call(
        lambda *refs: None,
        out_shape=tuple(jax.ShapeDtypeStruct(v.shape, v.dtype) for v in values),
        in_specs=[here] * (len(values) + len(awaited)),
        out_specs=(here,) * len(values),
        input_output_aliases={k: k for k in range(len(values))},
        compiler_params=pltpu.CompilerParams(vmem_limit_bytes=1 << 20),
        cost_estimate=FREE,
    )(*values, *awaited)


def terms_kernel(*refs):
    blocks, (gate_sum, down_sum, sent, mark) = refs[:-4], refs[-4:]
    for k in range(len(blocks) // 5):
        tok_cols, hid_cols, scaled, *halves = [block[...] for block in blocks[5 * k : 5 * k + 5]]
        back = jnp.concatenate(halves, axis=0)
        gate = lax.dot_general(tok_cols, back, ROWS, preferred_element_type=jnp.float32)
        down = lax.dot_general(hid_cols, scaled, ROWS, preferred_element_type=jnp.float32)
        gate_sum[...] = gate if k == 0 else gate_sum[...] + gate
        down_sum[...] = down if k == 0 else down_sum[...] + down
        if k < 2:
            count = halves[1].shape[0]
            sent[k * count : (k + 1) * count, :] = halves[1]
    mark[...] = jnp.zeros_like(mark)


def early_terms(made):
    tok_cols, hid_cols, scaled, back, _ = made[0]
    vmem = pl.BlockSpec(memory_space=pltpu.VMEM)
    return pl.pallas_call(
        terms_kernel,
        out_shape=(
            jax.ShapeDtypeStruct((tok_cols.shape[1], back.shape[1]), jnp.float32),
            jax.ShapeDtypeStruct((hid_cols.shape[1], scaled.shape[1]), jnp.float32),
            jax.ShapeDtypeStruct((2 * back.shape[0], back.shape[1]), jnp.bfloat16),
            jax.ShapeDtypeStruct((8, LANES), jnp.float32),
        ),
        in_specs=[vmem] * (5 * len(made)),
        out_specs=(vmem,) * 4,
        compiler_params=pltpu.CompilerParams(vmem_limit_bytes=24 << 20),
        cost_estimate=FREE,
    )(*[v for block in made for v in block])


def on_device(
    tokens, cotangent, expert_ids, gate_probs, gate_up_weight, down_weight, down_residual
):
    tok_rows, model_width = tokens.shape
    expert_count = lax.axis_size("expert")
    group_count = lax.axis_size("dp")
    gate_up, down_matrix = gate_up_weight[0], down_weight[0]
    hidden_units = down_matrix.shape[0]
    me, group = lax.axis_index("expert"), lax.axis_index("dp")
    bits = [lax.convert_element_type((group >> k) & 1, jnp.uint32) for k in range(3)]
    bits += [1 - bit for bit in bits]
    count = model_width // group_count
    first = max(count * 5 // 16, 16)
    far_at = (2 * (1 - ((group >> 2) & 1)) + (1 - (group & 1))) * count
    place = jnp.stack([me, (group >> 1) & 1, far_at]).astype(jnp.int32)
    high_count, half = group_count // 8, tok_rows // 2

    rows_own = packed(tokens, cotangent, expert_ids, gate_probs)
    rows_own, place, bits = lax.optimization_barrier((rows_own, place, bits))
    bit0, bit1, bit2, not0, not1, not2 = bits
    rows_c = flip(rows_own, "expert", 1)
    rows_x, rows_n = flip(rows_own, "expert", 2), flip(rows_own, "dp", 2)
    residual = down_residual[0, 0].reshape(high_count, 2, 2, 2, -1, model_width)


    def pair_sum(kept, got):
        return wide(kept) + wide(got)

    def residual_side(parity, first):
        part = take(take(residual, 3, first), 2, parity)
        return jnp.stack([take(part, 1, third) for third in (not2, bit2)], axis=1)

    res_other = flip(residual_side(not1, not0), "dp", 1)
    res_mine = residual_side(bit1, not0)

    def expert_on(*blocks):
        return expert_rows(group_count, place, blocks, gate_up, down_matrix)

    made = [expert_on(rows_own, rows_c)]
    res_send = narrow(pair_sum(residual_side(not1, bit0), res_other))
    rows_x, rows_n, res_send, res_mine = hold(
        (rows_x, rows_n, res_send, res_mine), (made[0][1],)
    )
    diagonal = [flip(rows_x[:half], "dp", 2), flip(rows_n[half:], "expert", 2)]
    made += [expert_on(rows, flip(rows, "expert", 1)) for rows in (rows_x, rows_n)]
    res_mine = flip(res_mine, "dp", 1)
    gate_early, down_early, back_sent, mark = early_terms(made)
    *diagonal, res_send, res_mine = hold((*diagonal, res_send, res_mine), (mark,))
    diagonal += [flip(rows, "expert", 1) for rows in diagonal]

    def terms(tok_cols, hid_cols, scaled, back):
        gate = lax.dot_general(tok_cols, back, ROWS, preferred_element_type=jnp.float32)
        down = lax.dot_general(hid_cols, scaled, ROWS, preferred_element_type=jnp.float32)
        return gate, down

    direct = high_count == 1 and count % LANES == 0 and first <= LANES
    if direct:
        tok_late, hid_late, scaled_late, *back_late, first_piece = last_rows(
            group_count, place, diagonal, gate_up, down_matrix, gate_early, first
        )
    else:
        tok_late, hid_late, scaled_late, *back_late = expert_on(*diagonal)
    gate_late, down_late = terms(
        tok_late, hid_late, scaled_late, jnp.concatenate(back_late, axis=0)
    )
    gate_term = narrow(gate_early + gate_late).reshape(high_count, 2, 2, -1, 2 * hidden_units)
    down_term = narrow(down_early + down_late).reshape(high_count, 2, 2, -1, model_width)

    def side(term, third, first):
        return take(take(term, 1, third), 1, first)

    edges = [0, first, count]
    far_sent, far_kept = [
        [side(gate_term[:, :, :, i:j], not2, bit) for i, j in zip(edges, edges[1:])]
        for bit in (not0, bit0)
    ]
    if direct:
        far_sent[0] = first_piece
    far_got = [flip(piece, "dp", 1) for piece in far_sent]
    crossed = [
        flip(narrow(pair_sum(kept, got)), "dp", 4) for kept, got in zip(far_kept, far_got)
    ]
    res_near = flip(res_send, "dp", 2)
    res_near, down_sent = hold(
        (res_near, side(down_term, not2, not0)), (far_got[0],)
    )
    (near_sent,) = hold((side(gate_term, bit2, not0),), (far_got[1],))
    res_sum = pair_sum(residual_side(bit1, bit0), res_mine) + wide(res_near)
    far_down = pair_sum(side(down_term, not2, bit0), flip(down_sent, "dp", 1))
    crossed_down = flip(narrow(far_down + res_sum[:, 0]), "dp", 4)

    def input_part(back):
        return narrow(jnp.dot(back, gate_up.T, preferred_element_type=jnp.float32))

    (back_sent,) = hold((back_sent,), (far_sent[1],))
    core = flip(input_part(back_sent), "expert", 1)
    back_kept = jnp.concatenate([made[0][3], made[1][3]], axis=0)
    total = wide(input_part(back_kept)) + wide(core)
    across = flip(narrow(total[tok_rows:]), "expert", 2)
    token_grad = narrow(total[:tok_rows] + wide(across))

    near_gate = pair_sum(side(gate_term, bit2, bit0), flip(near_sent, "dp", 1))
    (near_sent,) = hold((side(down_term, bit2, not0),), (across,))
    near_down = pair_sum(side(down_term, bit2, bit0), flip(near_sent, "dp", 1))
    crossed[-1] = hold((crossed[-1],), (near_sent,))[0]
    gate_sum = near_gate + wide(jnp.concatenate(crossed, axis=1))
    down_sum = near_down + res_sum[:, 1] + wide(crossed_down)
    bit = 8
    while bit < group_count:
        mine = lax.convert_element_type((group // bit) & 1, jnp.uint32)
        halves = [v.reshape(-1, 2, *v.shape[1:]) for v in (gate_sum, down_sum)]
        gate_sum, down_sum = [
            take(v, 1, mine) + wide(flip(narrow(take(v, 1, 1 - mine)), "dp", bit)) for v in halves
        ]
        bit *= 2
    factor = 1.0 / group_count
    grad_gate_up, grad_down = gate_sum * factor, down_sum * factor
    return (token_grad, grad_gate_up, grad_down)


def solution(mesh):
    placed = (
        P(("dp", "expert"), None),
        P(("dp", "expert"), None),
        P(("dp", "expert"), None),
        P(("dp", "expert"), None),
        P("expert", None, None),
        P("expert", None, None),
        P("dp", "expert", None, None),
    )
    return jax.shard_map(
        on_device,
        mesh=mesh,
        in_specs=placed,
        out_specs=(P(("dp", "expert"), None), P("expert", "dp", None), P("expert", "dp", None)),
        check_vma=False,
    )
```
